32 devices in a mesh: dir: 8 (over y, x, core), region: 4 (over z).
Axes of the slice: x: 2, y: 2, z: 4, core: 2. Of those that a mesh axis runs over, the one named last changes fastest.
Arguments:
- currents: bfloat16 [4, 48, 128, 256], P('region', 'dir'), may hold values from -6 to 6
- radiate: bfloat16 [1536, 128], replicated, may hold values from -0.5 to 0.5
- receive: bfloat16 [128, 1536], replicated, may hold values from -0.15625 to 0.15625
- transfer_table: bfloat16 [316, 1536], replicated, may hold values from -0.875 to 0.875
- near_blocks: bfloat16 [4, 48, 27, 128, 128], P('region', 'dir'), may hold values from -0.109375 to 0.109375
- dir_offsets: int32 [9], replicated, may hold values from 0 to 1536, as said below
- trans_src: int32 [4, 48, 48], P('region'), may hold values from -1 to 95, as said below
- trans_tid: int32 [4, 48, 48], P('region'), may hold values from 0 to 315
- near_src: int32 [4, 48, 27], P('region', 'dir'), may hold values from -1 to 71, as said below
Outputs:
- scattered: bfloat16 [4, 48, 128, 256], P('region', 'dir')
The draws below stay inside these ranges and needn't reach their ends.
Inputs may be any that keep to these rules, and one draw needn't show every extreme that they name: dir_offsets starts at 0, ends at 1536 and rises; every band holds 96 to 288 direction samples, and some band holds exactly 288. `trans_src`: in each box's list the non-empty slots come first and name distinct boxes; a list holds 24 to 48 of them, and some list is full. `near_src`: each box's list starts with the box itself, then names distinct other boxes, then empty slots; a list holds 13 to 27 non-empty slots, and some list is full.
All inputs are finite; a program needn't handle non-finite values.
Results may differ from the reference program's by a relative error of at most 0.005.
Values may be sent and summed in bfloat16 or wider, within the bound.
No kernel may reach another device: no remote copies, remote signals or barrier semaphores. Data moves between devices by JAX's collectives and lax.ppermute only.
A program may use at most 192 MiB of HBM per device.

```python
import jax
import jax.numpy as jnp
from jax import lax

Q = 128
K = 1536
R = 256
NT = 316
L = 48
NN = 27
REGIONS = 4
RB = 48
HB = 24
HN = 12
N_DIR = 8


def draw_dir_offsets(key, part):
    mean_share = K // N_DIR
    half_share = mean_share // 2
    chosen = jax.random.permutation(jax.random.fold_in(key, 11), N_DIR)
    jitter = jax.random.randint(jax.random.fold_in(key, 12), (), 0, half_share)
    change = jnp.zeros((N_DIR,), jnp.int32)
    change = change.at[chosen[0]].add(half_share).at[chosen[1]].add(-half_share)
    change = change.at[chosen[2]].add(jitter).at[chosen[3]].add(-jitter)
    share_sizes = (mean_share + change).astype(jnp.int32)
    return jnp.concatenate([jnp.zeros((1,), jnp.int32), jnp.cumsum(share_sizes).astype(jnp.int32)])


def live_mask(key, rows_all, slots, least):
    live_counts = jax.random.randint(jax.random.fold_in(key, 5), (rows_all,), least, slots + 1)
    live_counts = live_counts.at[0].set(slots).at[1].set(least)
    slot_index = jnp.arange(slots, dtype=jnp.int32)
    return slot_index[None, :] < live_counts[:, None]


def draw_trans_src(key, part):
    rows_all = REGIONS * RB
    extent = RB + 2 * HB
    row_keys = jax.random.split(jax.random.fold_in(key, 21), rows_all)
    shuffled = jax.vmap(lambda row_key: jax.random.permutation(row_key, extent))(row_keys).astype(jnp.int32)
    first_top = jnp.argmax(shuffled[0] == extent - 1).astype(jnp.int32)
    shuffled = shuffled.at[0].set(jnp.roll(shuffled[0], -first_top))
    chosen = shuffled[:, :L]
    keep = live_mask(jax.random.fold_in(key, 22), rows_all, L, L // 2)
    return jnp.where(keep, chosen, -1).astype(jnp.int32).reshape(REGIONS, RB, L)


def draw_near_src(key, part):
    rows_all = REGIONS * RB
    extent = RB + 2 * HN
    row_keys = jax.random.split(jax.random.fold_in(key, 31), rows_all)
    shuffled = jax.vmap(lambda row_key: jax.random.permutation(row_key, extent - 1))(row_keys).astype(jnp.int32)
    first_top = jnp.argmax(shuffled[0] == extent - 2).astype(jnp.int32)
    shuffled = shuffled.at[0].set(jnp.roll(shuffled[0], -first_top))
    own_index = (jnp.arange(rows_all, dtype=jnp.int32) % RB + HN).astype(jnp.int32)
    others = shuffled[:, :NN - 1]
    others = others + (others >= own_index[:, None]).astype(jnp.int32)
    chosen = jnp.concatenate([own_index[:, None], others], 1)
    keep = live_mask(jax.random.fold_in(key, 32), rows_all, NN, NN // 2)
    return jnp.where(keep, chosen, -1).astype(jnp.int32).reshape(REGIONS, RB, NN)


def set_ends(drawn, rng, low, largest):
    place = [jax.random.randint(jax.random.fold_in(rng, axis), (), 0, length) for axis, length in enumerate(drawn.shape)]
    widest = drawn.shape.index(max(drawn.shape))
    beside = place[:widest] + [(place[widest] + 1) % drawn.shape[widest]] + place[widest + 1:]
    return drawn.at[tuple(place)].set(low).at[tuple(beside)].set(largest)


def block_levels(stream_key, shape, pieces, low, top_value):
    factor_of = 1.0
    for axis_at, parts in pieces:
        draws = jax.random.uniform(jax.random.fold_in(jax.random.fold_in(stream_key, 6), axis_at), (parts,), jnp.float32, low / len(pieces), top_value / len(pieces))
        factor_of = factor_of * jnp.repeat(jnp.exp(draws), shape[axis_at] // parts).reshape((-1,) + (1,) * (len(shape) - 1 - axis_at))
    return factor_of


def bell_draw(own_key, shape, width, reach, cuts=(), held_as=jnp.bfloat16):
    gain = block_levels(own_key, shape, cuts, -0.22, 0.18) if cuts else 1.0
    array = jax.random.normal(own_key, shape, jnp.float32) * width * gain
    return jnp.minimum(jnp.maximum(array, -reach), reach).astype(held_as)


def setup_inputs(seed: int = 0) -> dict:
    splits = jax.random.split(jax.random.key(seed), 10)
    currents = bell_draw(splits[0], (REGIONS, RB, Q, R), 1.0, 6.0, ((0, 4), (1, 8)))
    radiate = bell_draw(splits[1], (K, Q), Q ** -0.5, 0.5)
    receive = bell_draw(splits[2], (Q, K), K ** -0.5, 0.15625)
    transfer_table = bell_draw(splits[3], (NT, K), L ** -0.5, 0.875)
    near_blocks = bell_draw(splits[4], (REGIONS, RB, NN, Q, Q), (NN * Q) ** -0.5, 0.109375, ((0, 4), (1, 8)))
    dir_offsets = draw_dir_offsets(jax.random.fold_in(splits[9], 71), 0)
    trans_src = draw_trans_src(jax.random.fold_in(splits[9], 71), 0)
    trans_tid = set_ends(jax.random.randint(splits[7], (REGIONS, RB, L), 0, NT), jax.random.fold_in(splits[7], 1), 0, NT - 1).astype(jnp.int32)
    near_src = draw_near_src(jax.random.fold_in(splits[9], 71), 0)
    return dict(currents=currents, radiate=radiate, receive=receive, transfer_table=transfer_table, near_blocks=near_blocks, dir_offsets=dir_offsets, trans_src=trans_src, trans_tid=trans_tid, near_src=near_src)


def band_weights(offsets, directions):
    dir_count = offsets.shape[0] - 1
    position = jnp.arange(directions, dtype=jnp.int32)
    starts = offsets[:-1]
    band_ends = offsets[1:]
    inside = (position[None, :] >= starts[:, None]) & (position[None, :] < band_ends[:, None])
    per_band = directions / (dir_count * (band_ends - starts).astype(jnp.float32))
    return jnp.sum(jnp.where(inside, per_band[:, None], jnp.zeros((), jnp.float32)), axis=0)


def region_rim(blocks_all, region_index, rim_width):
    count_all = blocks_all.shape[0]
    lower_rim = lax.dynamic_index_in_dim(blocks_all, jnp.maximum(region_index - 1, 0), 0, False)[-rim_width:]
    upper_rim = lax.dynamic_index_in_dim(blocks_all, jnp.minimum(region_index + 1, count_all - 1), 0, False)[:rim_width]
    lower_rim = jnp.where(region_index > 0, lower_rim, jnp.zeros_like(lower_rim))
    upper_rim = jnp.where(region_index < count_all - 1, upper_rim, jnp.zeros_like(upper_rim))
    own_block = lax.dynamic_index_in_dim(blocks_all, region_index, 0, False)
    return jnp.concatenate([lower_rim, own_block, upper_rim], 0)


def reference(currents, radiate, receive, transfer_table, near_blocks, dir_offsets, trans_src, trans_tid, near_src):
    weights = band_weights(dir_offsets, K)
    recv_w = (receive.astype(jnp.float32) * weights[None, :]).astype(jnp.bfloat16)
    radiate_full = radiate.astype(jnp.float32)

    def aggregate(region_field):
        return jnp.einsum('kq,jqr->jkr', radiate_full, region_field.astype(jnp.float32)).astype(jnp.bfloat16)

    patterns = lax.map(aggregate, currents)

    def one_region(region_index):
        extended = region_rim(patterns, region_index, HB)
        sources = trans_src[region_index]
        classes_here = trans_tid[region_index]

        def add_entry(entry, running):
            source_col = sources[:, entry]
            class_col = classes_here[:, entry]
            gathered = jnp.take(extended, jnp.maximum(source_col, 0), axis=0).astype(jnp.float32)
            factor = jnp.take(transfer_table, class_col, axis=0).astype(jnp.float32)
            factor = jnp.where((source_col >= 0)[:, None], factor, jnp.zeros((), jnp.float32))
            return running + factor[:, :, None] * gathered

        translated = lax.fori_loop(0, L, add_entry, jnp.zeros((RB, K, R), jnp.float32)).astype(jnp.bfloat16)
        far_field = jnp.einsum('qk,jkr->jqr', recv_w.astype(jnp.float32), translated.astype(jnp.float32))
        near_ext = region_rim(currents, region_index, HN)
        near_here = near_src[region_index]
        picked = jnp.take(near_ext, jnp.maximum(near_here, 0), axis=0).astype(jnp.float32)
        picked = jnp.where((near_here >= 0)[:, :, None, None], picked, jnp.zeros((), jnp.float32))
        block_here = lax.dynamic_index_in_dim(near_blocks, region_index, 0, False).astype(jnp.float32)
        near_field = jnp.einsum('jmpq,jmqr->jpr', block_here, picked)
        return (far_field + near_field).astype(jnp.bfloat16)

    return lax.map(one_region, jnp.arange(REGIONS, dtype=jnp.int32))
```

```python
import functools

import jax
import jax.numpy as jnp
from jax import lax
from jax.experimental import pallas as pl
from jax.experimental.pallas import tpu as pltpu
from jax.sharding import PartitionSpec as P

BF16, F32, I32 = jnp.bfloat16, jnp.float32, jnp.int32
NT_DIMS = (((1,), (1,)), ((), ()))
LANES = 128
ROWS = 8
UNROLL = 4
MIB = 2**20


def pad_to(size, tile):
    return -(-size // tile) * tile


def whole(memory_space):
    return pl.BlockSpec(memory_space=memory_space)


def index_kernel(classes, near_shift, boxes, src_ref, tid_ref, near_ref, cls_ref, near_map_ref, used_ref):
    first = lax.axis_index("dir") * boxes
    slots = src_ref.shape[2]
    near_slots = near_ref.shape[2]
    width = cls_ref.shape[1]
    used_width = used_ref.shape[1]
    ext_at = lax.broadcasted_iota(I32, (width, slots), 0)
    near_at = lax.broadcasted_iota(I32, (width, near_slots), 0)
    class_at = lax.broadcasted_iota(I32, (used_width, slots), 0)
    row_at = lax.broadcasted_iota(I32, (ROWS, slots), 0)
    near_row_at = lax.broadcasted_iota(I32, (ROWS, near_slots), 0)
    near_lane_at = lax.broadcasted_iota(I32, (ROWS, near_slots), 1)
    out_row = lax.broadcasted_iota(I32, (ROWS, width), 0)
    seen = jnp.zeros((used_width, slots), F32)
    cls = jnp.full((ROWS, width), classes, I32)
    near_map = jnp.full((ROWS, width), near_slots, I32)
    for j in range(boxes):
        src = src_ref[0, pl.ds(first + j, 1), :]
        tid = tid_ref[0, pl.ds(first + j, 1), :]
        seen = jnp.maximum(seen, jnp.where((class_at == tid) & (src >= 0), 1.0, 0.0))
        hot = jnp.where(ext_at == src, 1.0, 0.0).astype(BF16)
        parts = jnp.where(row_at == 0, tid // 16, jnp.where(row_at == 1, tid % 16, 1)).astype(F32).astype(BF16)
        found = lax.dot_general(parts, hot, NT_DIMS, preferred_element_type=F32).astype(I32)
        value = jnp.where(found[2:3] > 0, found[0:1] * 16 + found[1:2], classes)
        cls = jnp.where(out_row == j, value, cls)
        near = near_ref[0, j : j + 1, :]
        near_hot = jnp.where((near_at == near + near_shift) & (near >= 0), 1.0, 0.0).astype(BF16)
        near_parts = jnp.where(near_row_at == 0, near_lane_at, 1).astype(F32).astype(BF16)
        near_found = lax.dot_general(near_parts, near_hot, NT_DIMS, preferred_element_type=F32).astype(I32)
        near_value = jnp.where(near_found[1:2] > 0, near_found[0:1], near_slots)
        near_map = jnp.where(out_row == j, near_value, near_map)
    ones = jnp.ones((ROWS, slots), BF16)
    used_ref[...] = lax.dot_general(ones, seen.astype(BF16), NT_DIMS, preferred_element_type=F32).astype(I32)
    cls_ref[...] = cls
    near_map_ref[...] = near_map


def operator_kernel(low, high, dir_count, aliased, off_ref, used_ref, table_ref, recv_ref, rad_ref, *rest):
    if aliased:
        _, out_ref, rows_ref, weighted_ref, list_ref = rest
    else:
        out_ref, rows_ref, weighted_ref, list_ref = rest
    directions = recv_ref.shape[1]
    position = lax.broadcasted_iota(I32, (1, directions), 1)
    band_size = jnp.ones((1, directions), I32)
    for d in range(off_ref.shape[0] - 1):
        start, end = off_ref[d], off_ref[d + 1]
        band_size = jnp.where((position >= start) & (position < end), end - start, band_size)
    weight = directions / ((off_ref.shape[0] - 1) * band_size.astype(F32))
    weighted_ref[...] = (recv_ref[...].astype(F32) * weight).astype(BF16)
    rows_ref[...] = table_ref[low:high, :].astype(F32)
    if not aliased:
        out_ref[out_ref.shape[0] - 1] = jnp.zeros(out_ref.shape[1:], BF16)

    def note(n, count):
        list_ref[count] = n
        return count + (used_ref[0, n] > 0).astype(I32)

    count = lax.fori_loop(low, high, note, 0, unroll=8)
    for u in range(UNROLL):
        list_ref[count + u] = list_ref[jnp.maximum(count - 1, 0)]

    def step(i, carry):
        for u in range(UNROLL):
            n = list_ref[i * UNROLL + u]
            row = rows_ref[pl.ds(n - low, 1), :].astype(BF16)
            product = weighted_ref[...] * row
            out_ref[n] = jnp.dot(product, rad_ref[...], preferred_element_type=F32).astype(BF16)
        return carry

    lax.fori_loop(0, (count + UNROLL - 1) // UNROLL, step, 0)


def apply_kernel(places, boxes, halo, first_call, last_call, cls_ref, near_map_ref, t_ref, near_ref, *rest):
    source_refs = rest[: sum(len(parts) for _, _, parts in places)]
    rest = rest[len(source_refs) :]
    if not first_call:
        sum_ref, out_ref, *lhs_refs = rest
    else:
        out_ref, *lhs_refs = rest
    me = lax.axis_index("dir")
    region_boxes = boxes * lax.axis_size("dir")
    near_slots = near_ref.shape[2]
    size = near_ref.shape[3]
    total = None if first_call else sum_ref[...]
    at = 0
    for step, (rim, mask, parts) in enumerate(places):
        lhs_ref = lhs_refs[step % len(lhs_refs)]
        owner = me ^ mask
        if rim:
            upper = owner * boxes >= halo
            base = owner * boxes + jnp.where(upper, halo - region_boxes, halo + region_boxes)
        else:
            base = owner * boxes + halo
        for j in range(boxes):
            for b in range(boxes):
                n = cls_ref[j, base + b]
                m = near_map_ref[j, base + b]
                near = near_ref[0, j, jnp.minimum(m, near_slots - 1)]
                block = t_ref[n] + jnp.where(m < near_slots, near, jnp.zeros_like(near))
                lhs_ref[j * size : (j + 1) * size, b * size : (b + 1) * size] = block
        values = [ref[...] for ref in source_refs[at : at + len(parts)]]
        at += len(parts)
        rhs = values[0] if len(values) == 1 else jnp.concatenate(values, 0)
        rhs = rhs.reshape(boxes * size, rhs.shape[-1])
        added = jnp.dot(lhs_ref[...], rhs, preferred_element_type=F32)
        if step == 0 and first_call:
            out_ref[...] = added.reshape(out_ref.shape)
        elif step == 0:
            out_ref[...] = sum_ref[...] + added.reshape(out_ref.shape)
        else:
            out_ref[...] += added.reshape(out_ref.shape)


def shards(
    currents,
    radiate,
    receive,
    transfer_table,
    near_blocks,
    dir_offsets,
    trans_src,
    trans_tid,
    near_src,
):
    dir_count = lax.axis_size("dir")
    region_count = lax.axis_size("region")
    own = currents[0]
    boxes, unknowns, incidences = own.shape
    region_boxes = boxes * dir_count
    halo = region_boxes // 2
    near_halo = region_boxes // 4
    classes, directions = transfer_table.shape
    half = pad_to(classes // 2, 16)
    top = dir_count // 2
    inner = range(2, top, 2)
    split = boxes // 2

    def partner(array, mask):
        return lax.ppermute(array, "dir", [(i, i ^ mask) for i in range(dir_count)])

    along = []
    for i in range(dir_count):
        for z in range(region_count):
            target = z + 1 if i >= top else z - 1
            if 0 <= target < region_count:
                along.append((i * region_count + z, i * region_count + target))

    def beyond(array):
        return lax.ppermute(array, ("dir", "region"), along)

    width = pad_to(region_boxes + 2 * halo, LANES)
    used_width = pad_to(classes, LANES)
    cls, near_map, used = pl.pallas_call(
        functools.partial(index_kernel, classes, halo - near_halo, boxes),
        out_shape=(
            jax.ShapeDtypeStruct((ROWS, width), I32),
            jax.ShapeDtypeStruct((ROWS, width), I32),
            jax.ShapeDtypeStruct((ROWS, used_width), I32),
        ),
    )(trans_src, trans_tid, near_src)

    def operators(low, high, before):
        aliased = before is not None
        args = [dir_offsets, used, transfer_table, receive, radiate] + ([before] if aliased else [])
        specs = [whole(pltpu.SMEM), whole(pltpu.SMEM)] + [whole(pltpu.VMEM)] * (len(args) - 2)
        return pl.pallas_call(
            functools.partial(operator_kernel, low, high, dir_count, aliased),
            in_specs=specs,
            out_specs=whole(pltpu.VMEM),
            out_shape=pltpu.VMEM((classes + 1, unknowns, unknowns), BF16),
            input_output_aliases={5: 0} if aliased else {},
            scratch_shapes=[
                pltpu.VMEM((high - low, directions), F32),
                pltpu.VMEM((unknowns, directions), BF16),
                pltpu.SMEM((pad_to(high - low, 8) + 2 * UNROLL,), I32),
            ],
            compiler_params=pltpu.CompilerParams(vmem_limit_bytes=40 * MIB),
            cost_estimate=pl.CostEstimate(
                flops=classes * unknowns * unknowns * directions, bytes_accessed=MIB, transcendentals=0
            ),
        )(*args)

    def apply(places, total, last):
        parts = [part for _, _, group in places for part in group]
        args = [cls, near_map, table, near_blocks] + parts + ([] if total is None else [total])
        specs = [whole(pltpu.SMEM)] * 2 + [whole(pltpu.VMEM)] * (len(args) - 2)
        layout = [(rim, mask, [None] * len(group)) for rim, mask, group in places]
        shape = (boxes, unknowns, incidences)
        return pl.pallas_call(
            functools.partial(apply_kernel, layout, boxes, halo, total is None, last),
            in_specs=specs,
            out_specs=whole(pltpu.VMEM),
            out_shape=pltpu.VMEM(shape, F32),
            input_output_aliases={} if total is None else {len(args) - 1: 0},
            scratch_shapes=[pltpu.VMEM((boxes * unknowns, boxes * unknowns), BF16)] * 2,
            compiler_params=pltpu.CompilerParams(vmem_limit_bytes=48 * MIB),
            cost_estimate=pl.CostEstimate(
                flops=2 * len(places) * (boxes * unknowns) ** 2 * incidences, bytes_accessed=MIB, transcendentals=0
            ),
        )(*args)

    field = {0: own}
    rim = {}
    for m in inner:
        field[m] = partner(own, m)
    field[top] = partner(own, top)
    rim[0] = beyond(own)
    field[1] = partner(own, 1)
    table = operators(0, half, None)

    tied = lax.optimization_barrier((table, [field[m] for m in inner], field[top], rim[0]))
    table, inner_fields, field[top], rim[0] = tied
    for m, value in zip(inner, inner_fields):
        field[m] = value
    for m in inner:
        field[top + m] = partner(field[top], m)
    rim[top] = partner(rim[0], top)
    for m in inner:
        rim[m] = beyond(field[m])
    for m in inner:
        field[m + 1] = partner(field[m], 1)
    field[top + 1] = partner(field[top], 1)
    rim[1] = partner(rim[0], 1)
    table = operators(half, classes, table)
    early = [(False, m, [field[m]]) for m in (0, 1, *inner, *[m + 1 for m in inner], top, top + 1)]
    early += [(True, m, [rim[m]]) for m in (0, 1)]
    total = apply(early, None, False)

    tied = lax.optimization_barrier(
        (total, [field[top + m] for m in inner], [rim[m] for m in inner], rim[top])
    )
    total, far_fields, inner_rims, rim[top] = tied
    for m, value, other in zip(inner, far_fields, inner_rims):
        field[top + m], rim[m] = value, other
    last = {}
    for m in inner:
        last[m] = [partner(rim[top][:split], m), partner(rim[m][split:], top)]
    for m in inner:
        field[top + m + 1] = partner(field[top + m], 1)
        rim[m + 1] = partner(rim[m], 1)
    rim[top + 1] = partner(rim[top], 1)
    middle = [(False, top + m, [field[top + m]]) for m in inner]
    middle += [(True, m, [rim[m]]) for m in (*inner, top)]
    total = apply(middle, total, False)
    late = [(False, top + m + 1, [field[top + m + 1]]) for m in inner]
    late += [(True, m + 1, [rim[m + 1]]) for m in (*inner, top)]
    late += [(True, top + m, last[m]) for m in inner]
    late += [(True, top + m + 1, [partner(part, 1) for part in last[m]]) for m in inner]
    total = apply(late, total, True)
    return total.astype(BF16)[None]


def solution(mesh):
    placed = (
        P("region", "dir", None, None),
        P(),
        P(),
        P(),
        P("region", "dir", None, None, None),
        P(),
        P("region", None, None),
        P("region", None, None),
        P("region", "dir", None),
    )
    return jax.shard_map(
        shards,
        mesh=mesh,
        in_specs=placed,
        out_specs=P("region", "dir", None, None),
        check_vma=False,
    )
```

```python
import functools

import jax
import jax.numpy as jnp
from jax import lax
from jax.experimental import pallas as pl
from jax.experimental.pallas import tpu as pltpu
from jax.sharding import PartitionSpec as P

BF16, F32, I32 = jnp.bfloat16, jnp.float32, jnp.int32
NT_DIMS = (((1,), (1,)), ((), ()))
LANES = 128
ROWS = 8
UNROLL = 16
TAIL = 4
MIB = 2**20


def pad_to(size, tile):
    return -(-size // tile) * tile


def whole(memory_space):
    return pl.BlockSpec(memory_space=memory_space)


def lookup(parts, hot):
    return lax.dot_general(parts.astype(F32).astype(BF16), hot.astype(BF16), NT_DIMS, preferred_element_type=F32).astype(I32)


def fill_operators(low, high, used_ref, rows_ref, weighted_ref, rad_ref, out_ref, list_ref):
    def note(n, count):
        list_ref[count] = n
        return count + (used_ref[0, n] > 0).astype(I32)

    count = lax.fori_loop(low, high, note, 0, unroll=8)
    for u in range(TAIL):
        list_ref[count + u] = list_ref[jnp.maximum(count - 1, 0)]

    def step(at, wide):
        for u in range(wide):
            n = list_ref[at + u]
            row = rows_ref[pl.ds(n - low, 1), :].astype(BF16)
            product = weighted_ref[...] * row
            out_ref[n] = jnp.dot(product, rad_ref[...], preferred_element_type=F32).astype(BF16)

    def main_step(i, carry):
        step(i * UNROLL, UNROLL)
        return carry

    def tail_step(i, carry):
        step(main * UNROLL + i * TAIL, TAIL)
        return carry

    main = count // UNROLL
    lax.fori_loop(0, main, main_step, 0)
    lax.fori_loop(0, (count - main * UNROLL + TAIL - 1) // TAIL, tail_step, 0)


def first_kernel(
    half,
    boxes,
    halo,
    region_boxes,
    off_ref,
    src_hbm,
    tid_hbm,
    table_hbm,
    recv_hbm,
    rad_hbm,
    t_ref,
    weighted_ref,
    rad_ref,
    rows_ref,
    used_ref,
    cls_ref,
    src_ref,
    tid_ref,
    table_ref,
    recv_ref,
    low_ref,
    used_smem,
    list_ref,
    sems,
):
    pairs = [(src_hbm, src_ref), (tid_hbm, tid_ref), (recv_hbm, recv_ref), (table_hbm, table_ref), (rad_hbm, rad_ref)]
    copies = [pltpu.make_async_copy(a, b, sems.at[i]) for i, (a, b) in enumerate(pairs)]
    for copy in copies:
        copy.start()
    classes = table_ref.shape[0]
    directions = recv_ref.shape[1]
    t_ref[classes] = jnp.zeros(t_ref.shape[1:], BF16)
    position = lax.broadcasted_iota(I32, (1, directions), 1)
    band_size = jnp.ones((1, directions), I32)
    bands = off_ref.shape[0] - 1
    for d in range(bands):
        start, end = off_ref[d], off_ref[d + 1]
        band_size = jnp.where((position >= start) & (position < end), end - start, band_size)
    weight = directions / (bands * band_size.astype(F32))

    me = lax.axis_index("dir")
    slots = src_ref.shape[2]
    width = cls_ref.shape[1]
    used_width = used_ref.shape[1]
    ext_at = lax.broadcasted_iota(I32, (width, slots), 0)
    class_at = lax.broadcasted_iota(I32, (used_width, slots), 0)
    row_at = lax.broadcasted_iota(I32, (ROWS, slots), 0)
    out_row = lax.broadcasted_iota(I32, cls_ref.shape, 0)
    seen = jnp.zeros((used_width, slots), F32)
    cls = jnp.full(cls_ref.shape, classes, I32)
    copies[0].wait()
    copies[1].wait()
    for j in range(2 * boxes):
        target = (me if j < boxes else me ^ 1) * boxes + j % boxes
        src = src_ref[0, pl.ds(target, 1), :]
        tid = tid_ref[0, pl.ds(target, 1), :]
        owner = (src - halo + region_boxes) // boxes
        here = (src >= 0) & (((owner ^ me) & 1) == 0)
        seen = jnp.where((class_at == tid) & here, 1.0, seen)
        parts = jnp.where(row_at == 0, tid // 16, jnp.where(row_at == 1, tid % 16, 1))
        found = lookup(parts, jnp.where(ext_at == src, 1.0, 0.0))
        value = jnp.where(found[2:3] > 0, found[0:1] * 16 + found[1:2], classes)
        cls = jnp.where(out_row == j, value, cls)
    used_ref[...] = lookup(jnp.ones((ROWS, slots), I32), seen)
    cls_ref[...] = cls
    to_smem = pltpu.make_async_copy(used_ref, used_smem, sems.at[len(pairs)])
    to_smem.start()
    copies[2].wait()
    weighted_ref[...] = (recv_ref[...].astype(F32) * weight).astype(BF16)
    copies[3].wait()
    low_ref[...] = table_ref[:half, :].astype(F32)
    rows_ref[...] = table_ref[half:, :].astype(F32)
    copies[4].wait()
    to_smem.wait()
    fill_operators(0, half, used_smem, low_ref, weighted_ref, rad_ref, t_ref, list_ref)


def second_kernel(
    half,
    near_shift,
    used_ref,
    rows_ref,
    weighted_ref,
    rad_ref,
    near_src_ref,
    near_src_other_ref,
    near_hbm,
    near_other_hbm,
    _,
    t_ref,
    near_ref,
    near_map_ref,
    list_ref,
    sems,
):
    boxes, near_slots = near_hbm.shape[1:3]
    copies = []
    for i, array in enumerate((near_hbm, near_other_hbm)):
        for j in range(boxes):
            row = i * boxes + j
            copies.append(
                pltpu.make_async_copy(array.at[0, j], near_ref.at[row, pl.ds(0, near_slots)], sems.at[row])
            )
            copies[-1].start()
    for row in range(2 * boxes):
        near_ref[row, near_slots] = jnp.zeros(near_ref.shape[2:], BF16)
    width = near_map_ref.shape[1]
    near_at = lax.broadcasted_iota(I32, (width, near_slots), 0)
    row_at = lax.broadcasted_iota(I32, (ROWS, near_slots), 0)
    lane_at = lax.broadcasted_iota(I32, (ROWS, near_slots), 1)
    out_row = lax.broadcasted_iota(I32, near_map_ref.shape, 0)
    near_map = jnp.full(near_map_ref.shape, near_slots, I32)
    for j in range(2 * boxes):
        near = (near_src_ref if j < boxes else near_src_other_ref)[0, j % boxes : j % boxes + 1, :]
        found = lookup(jnp.where(row_at == 0, lane_at, 1), jnp.where((near_at == near + near_shift) & (near >= 0), 1.0, 0.0))
        value = jnp.where(found[1:2] > 0, found[0:1], near_slots)
        near_map = jnp.where(out_row == j, value, near_map)
    near_map_ref[...] = near_map
    fill_operators(half, half + rows_ref.shape[0], used_ref, rows_ref, weighted_ref, rad_ref, t_ref, list_ref)
    for copy in copies:
        copy.wait()


def apply_kernel(places, boxes, halo, first_call, last_call, cls_ref, near_map_ref, t_ref, near_ref, *rest):
    source_refs = rest[: sum(parts for _, _, parts in places)]
    rest = rest[len(source_refs) :]
    if not first_call:
        sum_ref, *rest = rest
    if last_call:
        own_ref, other_ref, *lhs_refs = rest
    else:
        out_ref, *lhs_refs = rest
    me = lax.axis_index("dir")
    region_boxes = boxes * lax.axis_size("dir")
    size = near_ref.shape[2]
    targets = near_ref.shape[0]
    at = 0
    total = None
    for step, (rim, mask, parts) in enumerate(places):
        lhs_ref = lhs_refs[step % len(lhs_refs)]
        owner = me ^ mask
        base = owner * boxes + halo
        if rim:
            base = base + jnp.where(owner * boxes >= halo, -region_boxes, region_boxes)
        for j in range(targets):
            for b in range(boxes):
                block = t_ref[cls_ref[j, base + b]] + near_ref[j, near_map_ref[j, base + b]]
                lhs_ref[j * size : (j + 1) * size, b * size : (b + 1) * size] = block
        values = [ref[...] for ref in source_refs[at : at + parts]]
        at += parts
        rhs = values[0] if parts == 1 else jnp.concatenate(values, 0)
        rhs = rhs.reshape(boxes * size, rhs.shape[-1])
        added = jnp.dot(lhs_ref[...], rhs, preferred_element_type=F32).reshape(targets, size, rhs.shape[-1])
        if step == 0:
            total = added if first_call else sum_ref[...] + added
        else:
            total = (total if last_call else out_ref[...]) + added
        if not last_call:
            out_ref[...] = total
    if last_call:
        own_ref[...] = total[:boxes]
        other_ref[...] = total[boxes:].astype(BF16)


def shards(
    currents,
    radiate,
    receive,
    transfer_table,
    near_blocks,
    dir_offsets,
    trans_src,
    trans_tid,
    near_src,
):
    dir_count = lax.axis_size("dir")
    region_count = lax.axis_size("region")
    own = currents[0]
    boxes, unknowns, incidences = own.shape
    near_slots = near_src.shape[2]
    region_boxes = boxes * dir_count
    halo = region_boxes // 2
    near_halo = region_boxes // 4
    classes, directions = transfer_table.shape
    half = pad_to(classes // 2, 16)
    top = dir_count // 2
    inner = range(2, top, 2)
    split = boxes // 2
    targets = 2 * boxes

    def partner(array, mask):
        return lax.ppermute(array, "dir", [(i, i ^ mask) for i in range(dir_count)])

    along = []
    for i in range(dir_count):
        for z in range(region_count):
            target = z + 1 if i >= top else z - 1
            if 0 <= target < region_count:
                along.append((i * region_count + z, i * region_count + target))

    def beyond(array):
        return lax.ppermute(array, ("dir", "region"), along)

    def pinned(array):
        return pltpu.with_memory_space_constraint(array, pltpu.VMEM)

    width = pad_to(region_boxes + 2 * halo, LANES)
    used_width = pad_to(classes, LANES)
    map_shape = (pad_to(targets, ROWS), width)
    table_shape = (classes + 1, unknowns, unknowns)
    vmem, smem, hbm = whole(pltpu.VMEM), whole(pltpu.SMEM), whole(pl.ANY)
    operator_cost = pl.CostEstimate(
        flops=classes * unknowns * unknowns * directions, bytes_accessed=MIB, transcendentals=0
    )

    field = {0: own}
    rim = {}
    for m in inner:
        field[m] = partner(own, m)
    field[top] = partner(own, top)
    rim[0] = beyond(own)
    near_src_other = partner(near_src, 1)
    near_other = partner(near_blocks, 1)
    table, weighted, rad_here, rows, used, cls = pl.pallas_call(
        functools.partial(first_kernel, half, boxes, halo, region_boxes),
        in_specs=[smem] + [hbm] * 5,
        out_specs=[vmem] * 6,
        out_shape=(
            pltpu.VMEM(table_shape, BF16),
            pltpu.VMEM((unknowns, directions), BF16),
            pltpu.VMEM((directions, unknowns), BF16),
            pltpu.VMEM((classes - half, directions), F32),
            pltpu.VMEM((ROWS, used_width), I32),
            pltpu.VMEM(map_shape, I32),
        ),
        scratch_shapes=[
            pltpu.VMEM(trans_src.shape, I32),
            pltpu.VMEM(trans_tid.shape, I32),
            pltpu.VMEM(transfer_table.shape, BF16),
            pltpu.VMEM(receive.shape, BF16),
            pltpu.VMEM((half, directions), F32),
            pltpu.SMEM((ROWS, used_width), I32),
            pltpu.SMEM((pad_to(classes, 8) + UNROLL,), I32),
            pltpu.SemaphoreType.DMA((6,)),
        ],
        compiler_params=pltpu.CompilerParams(vmem_limit_bytes=24 * MIB),
        cost_estimate=operator_cost,
    )(dir_offsets, trans_src, trans_tid, transfer_table, receive, radiate)

    tied = lax.optimization_barrier((table, [field[m] for m in inner], field[top], rim[0]))
    table, inner_fields, field[top], rim[0] = tied
    for m, value in zip(inner, inner_fields):
        field[m] = value
    for m in inner:
        field[top + m] = partner(field[top], m)
    rim[top] = partner(rim[0], top)
    for m in inner:
        rim[m] = beyond(field[m])

    table, near_here, near_map = pl.pallas_call(
        functools.partial(second_kernel, half, halo - near_halo),
        in_specs=[smem] + [vmem] * 5 + [hbm] * 2 + [vmem],
        out_specs=[vmem] * 3,
        out_shape=(
            pltpu.VMEM(table_shape, BF16),
            pltpu.VMEM((targets, near_slots + 1, unknowns, unknowns), BF16),
            pltpu.VMEM(map_shape, I32),
        ),
        input_output_aliases={8: 0},
        scratch_shapes=[
            pltpu.SMEM((pad_to(classes, 8) + UNROLL,), I32),
            pltpu.SemaphoreType.DMA((targets,)),
        ],
        compiler_params=pltpu.CompilerParams(vmem_limit_bytes=16 * MIB),
        cost_estimate=operator_cost,
    )(used, pinned(rows), pinned(weighted), pinned(rad_here), near_src, near_src_other, near_blocks, near_other, pinned(table))

    def apply(places, total, last):
        parts = [part for _, _, group in places for part in group]
        args = [cls, near_map, pinned(table), pinned(near_here)] + [pinned(part) for part in parts]
        args += [] if total is None else [pinned(total)]
        specs = [smem] * 2 + [vmem] * (len(args) - 2)
        layout = [(beyond_it, mask, len(group)) for beyond_it, mask, group in places]
        shape = (boxes, unknowns, incidences)
        whole_shape = (targets, unknowns, incidences)
        return pl.pallas_call(
            functools.partial(apply_kernel, layout, boxes, halo, total is None, last),
            in_specs=specs,
            out_specs=[vmem, vmem] if last else vmem,
            out_shape=(pltpu.VMEM(shape, F32), pltpu.VMEM(shape, BF16)) if last else pltpu.VMEM(whole_shape, F32),
            input_output_aliases={} if last or total is None else {len(args) - 1: 0},
            scratch_shapes=[pltpu.VMEM((targets * unknowns, boxes * unknowns), BF16)] * 2,
            compiler_params=pltpu.CompilerParams(vmem_limit_bytes=16 * MIB),
            cost_estimate=pl.CostEstimate(
                flops=4 * len(places) * (boxes * unknowns) ** 2 * incidences, bytes_accessed=MIB, transcendentals=0
            ),
        )(*args)

    early = [(False, m, [field[m]]) for m in (0, *inner, top)] + [(True, 0, [rim[0]])]
    total = apply(early, None, False)

    tied = lax.optimization_barrier(
        (total, [field[top + m] for m in inner], [rim[m] for m in inner], rim[top])
    )
    total, far_fields, inner_rims, rim[top] = tied
    for m, value, other in zip(inner, far_fields, inner_rims):
        field[top + m], rim[m] = value, other
    last = {m: [partner(rim[top][:split], m), partner(rim[m][split:], top)] for m in inner}
    middle = [(False, top + m, [field[top + m]]) for m in inner]
    middle += [(True, m, [rim[m]]) for m in (*inner, top)]
    total = apply(middle, total, False)
    here, there = apply([(True, top + m, last[m]) for m in inner], total, True)
    return (here + partner(there, 1).astype(F32)).astype(BF16)[None]


def solution(mesh):
    placed = (
        P("region", "dir", None, None),
        P(),
        P(),
        P(),
        P("region", "dir", None, None, None),
        P(),
        P("region", None, None),
        P("region", None, None),
        P("region", "dir", None),
    )
    return jax.shard_map(
        shards,
        mesh=mesh,
        in_specs=placed,
        out_specs=P("region", "dir", None, None),
        check_vma=False,
    )
```

```python
import functools

import jax
import jax.numpy as jnp
from jax import lax
from jax.experimental import pallas as pl
from jax.experimental.pallas import tpu as pltpu
from jax.sharding import PartitionSpec as P

BF16, F32, I32 = jnp.bfloat16, jnp.float32, jnp.int32
NT_DIMS = (((1,), (1,)), ((), ()))
LANES = 128
ROWS = 8
UNROLL = 16
TAIL = 4
GROUP = 4
MIB = 2**20


def pad_to(size, tile):
    return -(-size // tile) * tile


def whole(memory_space):
    return pl.BlockSpec(memory_space=memory_space)


def lookup(parts, hot):
    return lax.dot_general(parts.astype(F32).astype(BF16), hot.astype(BF16), NT_DIMS, preferred_element_type=F32).astype(I32)


def fill_operators(low, high, used_ref, rows_ref, weighted_ref, rad_ref, out_ref, list_ref):
    def note(n, count):
        list_ref[count] = n
        return count + (used_ref[0, n] > 0).astype(I32)

    count = lax.fori_loop(low, high, note, 0, unroll=8)
    for u in range(TAIL):
        list_ref[count + u] = list_ref[jnp.maximum(count - 1, 0)]

    def step(at, wide):
        for u in range(wide):
            n = list_ref[at + u]
            row = rows_ref[pl.ds(n - low, 1), :].astype(BF16)
            product = weighted_ref[...] * row
            out_ref[n] = jnp.dot(product, rad_ref[...], preferred_element_type=F32).astype(BF16)

    def main_step(i, carry):
        step(i * UNROLL, UNROLL)
        return carry

    def tail_step(i, carry):
        step(main * UNROLL + i * TAIL, TAIL)
        return carry

    main = count // UNROLL
    lax.fori_loop(0, main, main_step, 0)
    lax.fori_loop(0, (count - main * UNROLL + TAIL - 1) // TAIL, tail_step, 0)


def first_kernel(
    half,
    boxes,
    halo,
    region_boxes,
    off_ref,
    src_hbm,
    tid_hbm,
    table_hbm,
    recv_hbm,
    rad_hbm,
    t_ref,
    weighted_ref,
    rad_ref,
    rows_ref,
    used_ref,
    cls_ref,
    src_ref,
    tid_ref,
    table_ref,
    recv_ref,
    low_ref,
    used_smem,
    list_ref,
    sems,
):
    pairs = [(src_hbm, src_ref), (tid_hbm, tid_ref), (recv_hbm, recv_ref), (table_hbm, table_ref), (rad_hbm, rad_ref)]
    copies = [pltpu.make_async_copy(a, b, sems.at[i]) for i, (a, b) in enumerate(pairs)]
    for copy in copies:
        copy.start()
    classes = table_ref.shape[0]
    directions = recv_ref.shape[1]
    position = lax.broadcasted_iota(I32, (1, directions), 1)
    band_size = jnp.ones((1, directions), I32)
    bands = off_ref.shape[0] - 1
    for d in range(bands):
        start, end = off_ref[d], off_ref[d + 1]
        band_size = jnp.where((position >= start) & (position < end), end - start, band_size)
    weight = directions / (bands * band_size.astype(F32))

    me = lax.axis_index("dir")
    slots = src_ref.shape[2]
    width = cls_ref.shape[1]
    used_width = used_ref.shape[1]
    ext_at = lax.broadcasted_iota(I32, (width, slots), 0)
    class_at = lax.broadcasted_iota(I32, (used_width, slots), 0)
    row_at = lax.broadcasted_iota(I32, (ROWS, slots), 0)
    out_row = lax.broadcasted_iota(I32, cls_ref.shape, 0)
    seen = jnp.zeros((used_width, slots), F32)
    cls = jnp.full(cls_ref.shape, classes, I32)
    copies[0].wait()
    copies[1].wait()
    for j in range(2 * boxes):
        target = (me if j < boxes else me ^ 1) * boxes + j % boxes
        src = src_ref[0, pl.ds(target, 1), :]
        tid = tid_ref[0, pl.ds(target, 1), :]
        owner = (src - halo + region_boxes) // boxes
        here = (src >= 0) & (((owner ^ me) & 1) == 0)
        seen = jnp.where((class_at == tid) & here, 1.0, seen)
        parts = jnp.where(row_at == 0, tid // 16, jnp.where(row_at == 1, tid % 16, 1))
        found = lookup(parts, jnp.where(ext_at == src, 1.0, 0.0))
        value = jnp.where(found[2:3] > 0, found[0:1] * 16 + found[1:2], classes)
        cls = jnp.where(out_row == j, value, cls)
    used_ref[...] = lookup(jnp.ones((ROWS, slots), I32), seen)
    cls_ref[...] = cls
    to_smem = pltpu.make_async_copy(used_ref, used_smem, sems.at[len(pairs)])
    to_smem.start()
    copies[2].wait()
    weighted_ref[...] = (recv_ref[...].astype(F32) * weight).astype(BF16)
    copies[3].wait()
    low_ref[...] = table_ref[:half, :].astype(F32)
    rows_ref[...] = table_ref[half:, :].astype(F32)
    copies[4].wait()
    to_smem.wait()
    fill_operators(0, half, used_smem, low_ref, weighted_ref, rad_ref, t_ref, list_ref)


def second_kernel(
    half,
    near_shift,
    used_ref,
    rows_ref,
    weighted_ref,
    rad_ref,
    near_src_ref,
    near_src_other_ref,
    near_hbm,
    near_other_hbm,
    low_ref,
    t_ref,
    near_ref,
    near_map_ref,
    list_ref,
    sems,
):
    boxes, near_slots = near_hbm.shape[1:3]
    copies = []
    for i, array in enumerate((near_hbm, near_other_hbm)):
        for j in range(boxes):
            row = i * boxes + j
            copies.append(
                pltpu.make_async_copy(array.at[0, j], near_ref.at[row, pl.ds(0, near_slots)], sems.at[row])
            )
            copies[-1].start()
    copies.append(pltpu.make_async_copy(low_ref, t_ref.at[pl.ds(0, half)], sems.at[2 * boxes]))
    copies[-1].start()
    t_ref[t_ref.shape[0] - 1] = jnp.zeros(t_ref.shape[1:], BF16)
    for row in range(2 * boxes):
        near_ref[row, near_slots] = jnp.zeros(near_ref.shape[2:], BF16)
    width = near_map_ref.shape[1]
    near_at = lax.broadcasted_iota(I32, (width, near_slots), 0)
    row_at = lax.broadcasted_iota(I32, (ROWS, near_slots), 0)
    lane_at = lax.broadcasted_iota(I32, (ROWS, near_slots), 1)
    out_row = lax.broadcasted_iota(I32, near_map_ref.shape, 0)
    near_map = jnp.full(near_map_ref.shape, near_slots, I32)
    for j in range(2 * boxes):
        near = (near_src_ref if j < boxes else near_src_other_ref)[0, j % boxes : j % boxes + 1, :]
        found = lookup(jnp.where(row_at == 0, lane_at, 1), jnp.where((near_at == near + near_shift) & (near >= 0), 1.0, 0.0))
        value = jnp.where(found[1:2] > 0, found[0:1], near_slots)
        near_map = jnp.where(out_row == j, value, near_map)
    near_map_ref[...] = near_map
    fill_operators(half, half + rows_ref.shape[0], used_ref, rows_ref, weighted_ref, rad_ref, t_ref, list_ref)
    for copy in copies:
        copy.wait()


def apply_kernel(places, boxes, halo, first_call, last_call, cls_ref, near_map_ref, t_ref, near_ref, *rest):
    source_refs = rest[: sum(parts for _, _, parts in places)]
    rest = rest[len(source_refs) :]
    if not first_call:
        sum_ref, *rest = rest
    if last_call:
        own_ref, other_ref, *lhs_refs = rest
    else:
        out_ref, *lhs_refs = rest
    me = lax.axis_index("dir")
    region_boxes = boxes * lax.axis_size("dir")
    size = near_ref.shape[2]
    targets = near_ref.shape[0]
    at = 0
    total = None
    for step, (rim, mask, parts) in enumerate(places):
        lhs_ref = lhs_refs[step % len(lhs_refs)]
        owner = me ^ mask
        base = owner * boxes + halo
        if rim:
            base = base + jnp.where(owner * boxes >= halo, -region_boxes, region_boxes)
        for j in range(targets):
            for b in range(boxes):
                block = t_ref[cls_ref[j, base + b]] + near_ref[j, near_map_ref[j, base + b]]
                lhs_ref[j * size : (j + 1) * size, b * size : (b + 1) * size] = block
        values = [ref[...] for ref in source_refs[at : at + parts]]
        at += parts
        rhs = values[0] if parts == 1 else jnp.concatenate(values, 0)
        rhs = rhs.reshape(boxes * size, rhs.shape[-1])
        added = jnp.dot(lhs_ref[...], rhs, preferred_element_type=F32).reshape(targets, size, rhs.shape[-1])
        if step == 0:
            total = added if first_call else sum_ref[...] + added
        else:
            total = (total if last_call else out_ref[...]) + added
        if not last_call:
            out_ref[...] = total
    if last_call:
        own_ref[...] = total[:boxes]
        other_ref[...] = total[boxes:].astype(BF16)


def shards(
    currents,
    radiate,
    receive,
    transfer_table,
    near_blocks,
    dir_offsets,
    trans_src,
    trans_tid,
    near_src,
):
    dir_count = lax.axis_size("dir")
    region_count = lax.axis_size("region")
    own = currents[0]
    boxes, unknowns, incidences = own.shape
    near_slots = near_src.shape[2]
    region_boxes = boxes * dir_count
    halo = region_boxes // 2
    near_halo = region_boxes // 4
    classes, directions = transfer_table.shape
    half = pad_to(classes // 2, 16)
    top = dir_count // 2
    inner = range(2, top, 2)
    split = boxes // 2
    targets = 2 * boxes

    def partner(array, mask):
        return lax.ppermute(array, "dir", [(i, i ^ mask) for i in range(dir_count)])

    along = []
    for i in range(dir_count):
        for z in range(region_count):
            target = z + 1 if i >= top else z - 1
            if 0 <= target < region_count:
                along.append((i * region_count + z, i * region_count + target))

    def beyond(array):
        return lax.ppermute(array, ("dir", "region"), along)

    def pinned(array):
        return pltpu.with_memory_space_constraint(array, pltpu.VMEM)

    def in_hbm(array):
        return pltpu.with_memory_space_constraint(array, pltpu.HBM)

    width = pad_to(region_boxes + 2 * halo, LANES)
    used_width = pad_to(classes, LANES)
    map_shape = (pad_to(targets, ROWS), width)
    table_shape = (classes + 1, unknowns, unknowns)
    low_shape = (half, unknowns, unknowns)
    vmem, smem, hbm = whole(pltpu.VMEM), whole(pltpu.SMEM), whole(pltpu.HBM)
    operator_cost = pl.CostEstimate(
        flops=classes * unknowns * unknowns * directions, bytes_accessed=MIB, transcendentals=0
    )

    field = {0: own}
    rim = {}
    for m in inner:
        field[m] = partner(own, m)
    field[top] = partner(own, top)
    rim[0] = beyond(own)
    near_src_other = partner(near_src, 1)
    near_other = partner(near_blocks, 1)
    table, weighted, rad_here, rows, used, cls = pl.pallas_call(
        functools.partial(first_kernel, half, boxes, halo, region_boxes),
        in_specs=[smem] + [hbm] * 5,
        out_specs=[vmem] * 6,
        out_shape=(
            pltpu.VMEM(low_shape, BF16),
            pltpu.VMEM((unknowns, directions), BF16),
            pltpu.VMEM((directions, unknowns), BF16),
            pltpu.VMEM((classes - half, directions), F32),
            pltpu.VMEM((ROWS, used_width), I32),
            pltpu.VMEM(map_shape, I32),
        ),
        scratch_shapes=[
            pltpu.VMEM(trans_src.shape, I32),
            pltpu.VMEM(trans_tid.shape, I32),
            pltpu.VMEM(transfer_table.shape, BF16),
            pltpu.VMEM(receive.shape, BF16),
            pltpu.VMEM((half, directions), F32),
            pltpu.SMEM((ROWS, used_width), I32),
            pltpu.SMEM((pad_to(classes, 8) + UNROLL,), I32),
            pltpu.SemaphoreType.DMA((6,)),
        ],
        compiler_params=pltpu.CompilerParams(vmem_limit_bytes=8 * MIB),
        cost_estimate=operator_cost,
    )(dir_offsets, *[in_hbm(a) for a in (trans_src, trans_tid, transfer_table, receive, radiate)])

    tied = lax.optimization_barrier((table, [field[m] for m in inner], field[top], rim[0]))
    table, inner_fields, field[top], rim[0] = tied
    for m, value in zip(inner, inner_fields):
        field[m] = value
    for m in inner:
        field[top + m] = partner(field[top], m)
    rim[top] = partner(rim[0], top)
    for m in inner:
        rim[m] = beyond(field[m])

    table, near_here, near_map = pl.pallas_call(
        functools.partial(second_kernel, half, halo - near_halo),
        in_specs=[smem] + [vmem] * 5 + [hbm] * 2 + [vmem],
        out_specs=[vmem] * 3,
        out_shape=(
            pltpu.VMEM(table_shape, BF16),
            pltpu.VMEM((targets, near_slots + 1, unknowns, unknowns), BF16),
            pltpu.VMEM(map_shape, I32),
        ),
        scratch_shapes=[
            pltpu.SMEM((pad_to(classes, 8) + UNROLL,), I32),
            pltpu.SemaphoreType.DMA((targets + 1,)),
        ],
        compiler_params=pltpu.CompilerParams(vmem_limit_bytes=8 * MIB),
        cost_estimate=operator_cost,
    )(used, pinned(rows), pinned(weighted), pinned(rad_here), near_src, near_src_other, in_hbm(near_blocks), near_other, pinned(table))

    def apply(places, total, last):
        if len(places) > GROUP:
            total = apply(places[:GROUP], total, False)
            return apply(places[GROUP:], total, last)
        parts = [part for _, _, group in places for part in group]
        args = [cls, near_map, pinned(table), pinned(near_here)] + [pinned(part) for part in parts]
        args += [] if total is None else [pinned(total)]
        specs = [smem] * 2 + [vmem] * (len(args) - 2)
        layout = [(beyond_it, mask, len(group)) for beyond_it, mask, group in places]
        shape = (boxes, unknowns, incidences)
        whole_shape = (targets, unknowns, incidences)
        return pl.pallas_call(
            functools.partial(apply_kernel, layout, boxes, halo, total is None, last),
            in_specs=specs,
            out_specs=[vmem, vmem] if last else vmem,
            out_shape=(pltpu.VMEM(shape, F32), pltpu.VMEM(shape, BF16)) if last else pltpu.VMEM(whole_shape, F32),
            input_output_aliases={} if last or total is None else {len(args) - 1: 0},
            scratch_shapes=[pltpu.VMEM((targets * unknowns, boxes * unknowns), BF16)] * 2,
            compiler_params=pltpu.CompilerParams(vmem_limit_bytes=14 * MIB),
            cost_estimate=pl.CostEstimate(
                flops=4 * len(places) * (boxes * unknowns) ** 2 * incidences, bytes_accessed=MIB, transcendentals=0
            ),
        )(*args)

    early = [(False, m, [field[m]]) for m in (0, *inner, top)] + [(True, 0, [rim[0]])]
    total = apply(early, None, False)

    tied = lax.optimization_barrier(
        (total, [field[top + m] for m in inner], [rim[m] for m in inner], rim[top])
    )
    total, far_fields, inner_rims, rim[top] = tied
    for m, value, other in zip(inner, far_fields, inner_rims):
        field[top + m], rim[m] = value, other
    last = {m: [partner(rim[top][:split], m), partner(rim[m][split:], top)] for m in inner}
    middle = [(False, top + m, [field[top + m]]) for m in inner]
    middle += [(True, m, [rim[m]]) for m in (*inner, top)]
    total = apply(middle, total, False)
    here, there = apply([(True, top + m, last[m]) for m in inner], total, True)
    return (here + partner(there, 1).astype(F32)).astype(BF16)[None]


def solution(mesh):
    placed = (
        P("region", "dir", None, None),
        P(),
        P(),
        P(),
        P("region", "dir", None, None, None),
        P(),
        P("region", None, None),
        P("region", None, None),
        P("region", "dir", None),
    )
    return jax.shard_map(
        shards,
        mesh=mesh,
        in_specs=placed,
        out_specs=P("region", "dir", None, None),
        check_vma=False,
    )
```

```python
import functools

import jax
import jax.numpy as jnp
from jax import lax
from jax.experimental import pallas as pl
from jax.experimental.pallas import tpu as pltpu
from jax.sharding import PartitionSpec as P

BF16, F32, I32 = jnp.bfloat16, jnp.float32, jnp.int32
NT_DIMS = (((1,), (1,)), ((), ()))
LANES = 128
ROWS = 8
UNROLL = 16
TAIL = 4
GROUP = 8
MIB = 2**20


def pad_to(size, tile):
    return -(-size // tile) * tile


def whole(memory_space):
    return pl.BlockSpec(memory_space=memory_space)


def lookup(parts, hot):
    return lax.dot_general(parts.astype(F32).astype(BF16), hot.astype(BF16), NT_DIMS, preferred_element_type=F32).astype(I32)


def fill_operators(begin, end, list_ref, rows_ref, weighted_ref, rad_ref, out_ref):
    def step(at, wide):
        for u in range(wide):
            place = jnp.minimum(at + u, end - 1)
            row = rows_ref[pl.ds(list_ref[0, place], 1), :].astype(BF16)
            product = weighted_ref[...] * row
            out_ref[place] = jnp.dot(product, rad_ref[...], preferred_element_type=F32).astype(BF16)

    def main_step(i, carry):
        step(begin + i * UNROLL, UNROLL)
        return carry

    def tail_step(i, carry):
        step(begin + main * UNROLL + i * TAIL, TAIL)
        return carry

    count = jnp.maximum(end - begin, 0)
    main = count // UNROLL
    lax.fori_loop(0, main, main_step, 0)
    lax.fori_loop(0, (count - main * UNROLL + TAIL - 1) // TAIL, tail_step, 0)


def first_kernel(
    first_count,
    boxes,
    halo,
    region_boxes,
    off_hbm,
    src_hbm,
    tid_hbm,
    near_src_hbm,
    table_hbm,
    recv_hbm,
    rad_hbm,
    t_ref,
    weighted_ref,
    rad_ref,
    rows_ref,
    cls_ref,
    near_src_ref,
    list_ref,
    off_ref,
    src_ref,
    tid_ref,
    table_ref,
    recv_ref,
    used_ref,
    used_smem,
    sems,
):
    pairs = [
        (src_hbm, src_ref),
        (tid_hbm, tid_ref),
        (off_hbm, off_ref),
        (recv_hbm, recv_ref),
        (table_hbm, table_ref),
        (rad_hbm, rad_ref),
        (near_src_hbm, near_src_ref),
    ]
    copies = [pltpu.make_async_copy(a, b, sems.at[i]) for i, (a, b) in enumerate(pairs)]
    for copy in copies:
        copy.start()
    classes = table_ref.shape[0]
    directions = recv_ref.shape[1]
    me = lax.axis_index("dir")
    dir_count = region_boxes // boxes
    top = dir_count // 2
    slots = src_ref.shape[2]
    width = cls_ref.shape[1]
    used_width = used_ref.shape[1]
    ext_at = lax.broadcasted_iota(I32, (width, slots), 0)
    class_at = lax.broadcasted_iota(I32, (used_width, slots), 0)
    row_at = lax.broadcasted_iota(I32, (ROWS, slots), 0)
    out_row = lax.broadcasted_iota(I32, cls_ref.shape, 0)
    seen = jnp.zeros((used_width, slots), F32)
    cls = jnp.full(cls_ref.shape, classes, I32)
    copies[0].wait()
    copies[1].wait()
    for j in range(2 * boxes):
        target = (me if j < boxes else me ^ 1) * boxes + j % boxes
        src = src_ref[0, pl.ds(target, 1), :]
        tid = tid_ref[0, pl.ds(target, 1), :]
        mask = (((src - halo + region_boxes) // boxes) % dir_count) ^ me
        beyond = (src < halo) | (src >= halo + region_boxes)
        late = beyond & ((mask & top) != 0) & ((mask & (top - 2)) != 0)
        even = (mask & 1) == 0
        here = (src >= 0) & ((even | late) if j < boxes else (even & ~late))
        seen = jnp.where((class_at == tid) & here, 1.0, seen)
        parts = jnp.where(row_at == 0, tid // 16, jnp.where(row_at == 1, tid % 16, 1))
        found = lookup(parts, jnp.where(ext_at == src, 1.0, 0.0))
        value = jnp.where(found[2:3] > 0, found[0:1] * 16 + found[1:2], classes)
        cls = jnp.where(out_row == j, value, cls)
    used_ref[...] = lookup(jnp.ones((ROWS, slots), I32), seen)
    cls_ref[...] = cls
    to_smem = pltpu.make_async_copy(used_ref, used_smem, sems.at[len(pairs)])
    to_smem.start()
    copies[2].wait()
    position = lax.broadcasted_iota(I32, (1, directions), 1)
    band_size = jnp.ones((1, directions), I32)
    bands = off_ref.shape[0] - 1
    for d in range(bands):
        start, end = off_ref[d], off_ref[d + 1]
        band_size = jnp.where((position >= start) & (position < end), end - start, band_size)
    weight = directions / (bands * band_size.astype(F32))
    copies[3].wait()
    weighted_ref[...] = (recv_ref[...].astype(F32) * weight).astype(BF16)
    copies[4].wait()
    rows_ref[...] = table_ref[...].astype(F32)
    to_smem.wait()

    def note(n, count):
        list_ref[0, count] = n
        list_ref[1, n] = count
        return count + (used_smem[0, n] > 0).astype(I32)

    count = lax.fori_loop(0, classes, note, 0, unroll=8)
    list_ref[1, classes] = classes
    list_ref[0, classes + 1] = count
    copies[5].wait()
    copies[6].wait()
    fill_operators(0, jnp.minimum(count, first_count), list_ref, rows_ref, weighted_ref, rad_ref, t_ref)


def second_kernel(
    near_shift,
    list_ref,
    rows_ref,
    weighted_ref,
    rad_ref,
    near_src_ref,
    near_src_other_ref,
    near_hbm,
    near_other_hbm,
    low_ref,
    t_ref,
    near_ref,
    near_map_ref,
    sems,
):
    boxes, near_slots = near_hbm.shape[1:3]
    copies = []
    for i, array in enumerate((near_hbm, near_other_hbm)):
        for j in range(boxes):
            row = i * boxes + j
            copies.append(
                pltpu.make_async_copy(array.at[0, j], near_ref.at[row, pl.ds(0, near_slots)], sems.at[row])
            )
            copies[-1].start()
    first_count = low_ref.shape[0]
    classes = rows_ref.shape[0]
    copies.append(pltpu.make_async_copy(low_ref, t_ref.at[pl.ds(0, first_count)], sems.at[2 * boxes]))
    copies[-1].start()
    t_ref[t_ref.shape[0] - 1] = jnp.zeros(t_ref.shape[1:], BF16)
    for row in range(2 * boxes):
        near_ref[row, near_slots] = jnp.zeros(near_ref.shape[2:], BF16)
    width = near_map_ref.shape[1]
    near_at = lax.broadcasted_iota(I32, (width, near_slots), 0)
    row_at = lax.broadcasted_iota(I32, (ROWS, near_slots), 0)
    lane_at = lax.broadcasted_iota(I32, (ROWS, near_slots), 1)
    out_row = lax.broadcasted_iota(I32, near_map_ref.shape, 0)
    near_map = jnp.full(near_map_ref.shape, near_slots, I32)
    for j in range(2 * boxes):
        near = (near_src_ref if j < boxes else near_src_other_ref)[0, j % boxes : j % boxes + 1, :]
        found = lookup(jnp.where(row_at == 0, lane_at, 1), jnp.where((near_at == near + near_shift) & (near >= 0), 1.0, 0.0))
        value = jnp.where(found[1:2] > 0, found[0:1], near_slots)
        near_map = jnp.where(out_row == j, value, near_map)
    near_map_ref[...] = near_map
    fill_operators(first_count, list_ref[0, classes + 1], list_ref, rows_ref, weighted_ref, rad_ref, t_ref)
    for copy in copies:
        copy.wait()


def apply_kernel(
    places, first_row, boxes, halo, with_total, with_other, dtype, cls_ref, near_map_ref, list_ref, t_ref, near_ref, *rest
):
    source_refs, rest = rest[: sum(parts for _, _, parts in places)], rest[sum(parts for _, _, parts in places) :]
    if with_total:
        sum_ref, *rest = rest
    if with_other:
        other_ref, *rest = rest
    out_ref, total_ref, *lhs_refs = rest
    me = lax.axis_index("dir")
    region_boxes = boxes * lax.axis_size("dir")
    size = near_ref.shape[2]
    at = 0
    for step, (rim, mask, parts) in enumerate(places):
        lhs_ref = lhs_refs[step % len(lhs_refs)]
        owner = me ^ mask
        base = owner * boxes + halo
        if rim:
            base = base + jnp.where(owner * boxes >= halo, -region_boxes, region_boxes)
        for j in range(boxes):
            row = first_row + j
            for b in range(boxes):
                block = t_ref[list_ref[1, cls_ref[row, base + b]]] + near_ref[row, near_map_ref[row, base + b]]
                lhs_ref[j * size : (j + 1) * size, b * size : (b + 1) * size] = block
        values = [ref[...] for ref in source_refs[at : at + parts]]
        at += parts
        rhs = values[0] if parts == 1 else jnp.concatenate(values, 0)
        rhs = rhs.reshape(boxes * size, rhs.shape[-1])
        added = jnp.dot(lhs_ref[...], rhs, preferred_element_type=F32).reshape(total_ref.shape)
        if step == 0:
            total = sum_ref[...] + added if with_total else added
            total = total + other_ref[...].astype(F32) if with_other else total
        else:
            total = total_ref[...] + added
        if step == len(places) - 1:
            out_ref[...] = total.astype(dtype).reshape(out_ref.shape)
        else:
            total_ref[...] = total


def shards(
    currents,
    radiate,
    receive,
    transfer_table,
    near_blocks,
    dir_offsets,
    trans_src,
    trans_tid,
    near_src,
):
    dir_count = lax.axis_size("dir")
    region_count = lax.axis_size("region")
    own = currents[0]
    boxes, unknowns, incidences = own.shape
    near_slots = near_src.shape[2]
    region_boxes = boxes * dir_count
    halo = region_boxes // 2
    near_halo = region_boxes // 4
    classes, directions = transfer_table.shape
    first_count = pad_to(classes // 4, UNROLL)
    top = dir_count // 2
    inner = range(2, top, 2)
    split = boxes // 2
    targets = 2 * boxes

    def partner(array, mask):
        return lax.ppermute(array, "dir", [(i, i ^ mask) for i in range(dir_count)])

    along = []
    for i in range(dir_count):
        for z in range(region_count):
            target = z + 1 if i >= top else z - 1
            if 0 <= target < region_count:
                along.append((i * region_count + z, i * region_count + target))

    def beyond(array):
        return lax.ppermute(array, ("dir", "region"), along)

    def pinned(array):
        return pltpu.with_memory_space_constraint(array, pltpu.VMEM)

    def in_hbm(array):
        return pltpu.with_memory_space_constraint(array, pltpu.HBM)

    width = pad_to(region_boxes + 2 * halo, LANES)
    used_width = pad_to(classes, LANES)
    map_shape = (pad_to(targets, ROWS), width)
    table_shape = (classes + 1, unknowns, unknowns)
    low_shape = (first_count, unknowns, unknowns)
    list_shape = (2, pad_to(classes + 2, LANES))
    vmem, smem, hbm = whole(pltpu.VMEM), whole(pltpu.SMEM), whole(pltpu.HBM)
    operator_cost = pl.CostEstimate(
        flops=classes * unknowns * unknowns * directions, bytes_accessed=MIB, transcendentals=0
    )

    field = {0: own}
    rim = {}
    for m in inner:
        field[m] = partner(own, m)
    field[top] = partner(own, top)
    rim[0] = beyond(own)
    near_other = partner(near_blocks, 1)
    low, weighted, rad_here, rows, cls, near_src_here, listed = pl.pallas_call(
        functools.partial(first_kernel, first_count, boxes, halo, region_boxes),
        in_specs=[hbm] * 7,
        out_specs=[vmem] * 6 + [smem],
        out_shape=(
            pltpu.VMEM(low_shape, BF16),
            pltpu.VMEM((unknowns, directions), BF16),
            pltpu.VMEM((directions, unknowns), BF16),
            pltpu.VMEM((classes, directions), F32),
            pltpu.VMEM(map_shape, I32),
            pltpu.VMEM(near_src.shape, I32),
            jax.ShapeDtypeStruct(list_shape, I32),
        ),
        scratch_shapes=[
            pltpu.SMEM(dir_offsets.shape, I32),
            pltpu.VMEM(trans_src.shape, I32),
            pltpu.VMEM(trans_tid.shape, I32),
            pltpu.VMEM(transfer_table.shape, BF16),
            pltpu.VMEM(receive.shape, BF16),
            pltpu.VMEM((ROWS, used_width), I32),
            pltpu.SMEM((ROWS, used_width), I32),
            pltpu.SemaphoreType.DMA((8,)),
        ],
        compiler_params=pltpu.CompilerParams(vmem_limit_bytes=8 * MIB),
        cost_estimate=operator_cost,
    )(*[in_hbm(a) for a in (dir_offsets, trans_src, trans_tid, near_src, transfer_table, receive, radiate)])

    tied = lax.optimization_barrier((low, [field[m] for m in inner], field[top], rim[0]))
    low, inner_fields, field[top], rim[0] = tied
    near_src_other = partner(near_src_here, 1)
    for m, value in zip(inner, inner_fields):
        field[m] = value
    for m in inner:
        field[top + m] = partner(field[top], m)
    rim[top] = partner(rim[0], top)
    for m in inner:
        rim[m] = beyond(field[m])

    table, near_here, near_map = pl.pallas_call(
        functools.partial(second_kernel, halo - near_halo),
        in_specs=[smem] + [vmem] * 5 + [hbm] * 2 + [vmem],
        out_specs=[vmem] * 3,
        out_shape=(
            pltpu.VMEM(table_shape, BF16),
            pltpu.VMEM((targets, near_slots + 1, unknowns, unknowns), BF16),
            pltpu.VMEM(map_shape, I32),
        ),
        scratch_shapes=[pltpu.SemaphoreType.DMA((targets + 1,))],
        compiler_params=pltpu.CompilerParams(vmem_limit_bytes=8 * MIB),
        cost_estimate=operator_cost,
    )(
        listed,
        pinned(rows),
        pinned(weighted),
        pinned(rad_here),
        pinned(near_src_here),
        near_src_other,
        in_hbm(near_blocks),
        near_other,
        pinned(low),
    )

    def apply(places, first_row, total, other, dtype, shape):
        full = (boxes, unknowns, incidences)
        if len(places) > GROUP:
            total = apply(places[:GROUP], first_row, total, None, F32, full)
            return apply(places[GROUP:], first_row, total, other, dtype, shape)
        parts = [part for _, _, group in places for part in group]
        args = [cls, near_map, listed, pinned(table), pinned(near_here)] + [pinned(part) for part in parts]
        args += [pinned(extra) for extra in (total, other) if extra is not None]
        specs = [smem] * 3 + [vmem] * (len(args) - 3)
        layout = [(outside, mask, len(group)) for outside, mask, group in places]
        kernel = functools.partial(
            apply_kernel, layout, first_row, boxes, halo, total is not None, other is not None, dtype
        )
        return pl.pallas_call(
            kernel,
            in_specs=specs,
            out_specs=vmem,
            out_shape=pltpu.VMEM(shape, dtype) if len(shape) == 3 else jax.ShapeDtypeStruct(shape, dtype),
            scratch_shapes=[pltpu.VMEM(full, F32)]
            + [pltpu.VMEM((boxes * unknowns, boxes * unknowns), BF16)] * 2,
            compiler_params=pltpu.CompilerParams(vmem_limit_bytes=14 * MIB),
            cost_estimate=pl.CostEstimate(
                flops=2 * len(places) * (boxes * unknowns) ** 2 * incidences, bytes_accessed=MIB, transcendentals=0
            ),
        )(*args)

    tied = lax.optimization_barrier(
        (table, [field[top + m] for m in inner], [rim[m] for m in inner], rim[top])
    )
    table, far_fields, inner_rims, rim[top] = tied
    for m, value, other in zip(inner, far_fields, inner_rims):
        field[top + m], rim[m] = value, other
    last = {m: [partner(rim[top][:split], m), partner(rim[m][split:], top)] for m in inner}

    full = (boxes, unknowns, incidences)
    early = [(False, m, [field[m]]) for m in (0, *inner, top)] + [(True, 0, [rim[0]])]
    middle = [(False, top + m, [field[top + m]]) for m in inner]
    middle += [(True, m, [rim[m]]) for m in (*inner, top)]
    for_other = apply(early + middle, boxes, None, None, BF16, full)

    for_other, last = lax.optimization_barrier((for_other, last))
    late = [(True, top + m, last[m]) for m in inner]
    late += [(True, top + m + 1, [partner(part, 1) for part in last[m]]) for m in inner]
    from_other = partner(for_other, 1)
    total = apply(early, 0, None, None, F32, full)
    return apply(middle + late, 0, total, from_other, BF16, currents.shape)


def solution(mesh):
    placed = (
        P("region", "dir", None, None),
        P(),
        P(),
        P(),
        P("region", "dir", None, None, None),
        P(),
        P("region", None, None),
        P("region", None, None),
        P("region", "dir", None),
    )
    return jax.shard_map(
        shards,
        mesh=mesh,
        in_specs=placed,
        out_specs=P("region", "dir", None, None),
        check_vma=False,
    )
```

```python
import functools

import jax
import jax.numpy as jnp
from jax import lax
from jax.experimental import pallas as pl
from jax.experimental.pallas import tpu as pltpu
from jax.sharding import PartitionSpec as P

BF16, F32, I32 = jnp.bfloat16, jnp.float32, jnp.int32
NT_DIMS = (((1,), (1,)), ((), ()))
LANES = 128
ROWS = 8
UNROLL = 16
TAIL = 4
GROUP = 8
MIB = 2**20


def pad_to(size, tile):
    return -(-size // tile) * tile


def whole(memory_space):
    return pl.BlockSpec(memory_space=memory_space)


def lookup(parts, hot):
    return lax.dot_general(parts.astype(F32).astype(BF16), hot.astype(BF16), NT_DIMS, preferred_element_type=F32).astype(I32)


def fill_operators(begin, end, list_ref, rows_ref, weighted_ref, rad_ref, out_ref):
    def step(at, wide):
        for u in range(wide):
            place = jnp.minimum(at + u, end - 1)
            row = rows_ref[pl.ds(list_ref[0, place], 1), :].astype(BF16)
            product = weighted_ref[...] * row
            out_ref[place] = jnp.dot(product, rad_ref[...], preferred_element_type=F32).astype(BF16)

    def main_step(i, carry):
        step(begin + i * UNROLL, UNROLL)
        return carry

    def tail_step(i, carry):
        step(begin + main * UNROLL + i * TAIL, TAIL)
        return carry

    count = jnp.maximum(end - begin, 0)
    main = count // UNROLL
    lax.fori_loop(0, main, main_step, 0)
    lax.fori_loop(0, (count - main * UNROLL + TAIL - 1) // TAIL, tail_step, 0)


def first_kernel(
    first_count,
    boxes,
    halo,
    region_boxes,
    off_hbm,
    src_hbm,
    tid_hbm,
    near_src_hbm,
    table_hbm,
    recv_hbm,
    rad_hbm,
    t_ref,
    weighted_ref,
    rad_ref,
    rows_ref,
    cls_ref,
    near_src_ref,
    listed_ref,
    off_ref,
    src_ref,
    tid_ref,
    table_ref,
    recv_ref,
    list_ref,
    sems,
):
    pairs = [
        (src_hbm, src_ref),
        (tid_hbm, tid_ref),
        (off_hbm, off_ref),
        (recv_hbm, recv_ref),
        (table_hbm, table_ref),
        (rad_hbm, rad_ref),
        (near_src_hbm, near_src_ref),
    ]
    copies = [pltpu.make_async_copy(a, b, sems.at[i]) for i, (a, b) in enumerate(pairs)]
    for copy in copies:
        copy.start()
    classes = table_ref.shape[0]
    directions = recv_ref.shape[1]
    me = lax.axis_index("dir")
    dir_count = region_boxes // boxes
    top = dir_count // 2
    slots = src_ref.shape[2]
    width = cls_ref.shape[1]
    used_width = listed_ref.shape[1]
    ext_at = lax.broadcasted_iota(I32, (width, slots), 0)
    class_at = lax.broadcasted_iota(I32, (used_width, slots), 0)
    row_at = lax.broadcasted_iota(I32, (ROWS, slots), 0)
    out_row = lax.broadcasted_iota(I32, cls_ref.shape, 0)
    seen = jnp.zeros((used_width, slots), F32)
    cls = jnp.full(cls_ref.shape, classes, I32)
    copies[0].wait()
    copies[1].wait()
    for j in range(2 * boxes):
        target = (me if j < boxes else me ^ 1) * boxes + j % boxes
        src = src_ref[0, pl.ds(target, 1), :]
        tid = tid_ref[0, pl.ds(target, 1), :]
        mask = (((src - halo + region_boxes) // boxes) % dir_count) ^ me
        beyond = (src < halo) | (src >= halo + region_boxes)
        late = beyond & ((mask & top) != 0) & ((mask & (top - 2)) != 0)
        even = (mask & 1) == 0
        here = (src >= 0) & ((even | late) if j < boxes else (even & ~late))
        seen = jnp.where((class_at == tid) & here, 1.0, seen)
        parts = jnp.where(row_at == 0, tid // 16, jnp.where(row_at == 1, tid % 16, 1))
        found = lookup(parts, jnp.where(ext_at == src, 1.0, 0.0))
        value = jnp.where(found[2:3] > 0, found[0:1] * 16 + found[1:2], classes)
        cls = jnp.where(out_row == j, value, cls)
    cls_ref[...] = cls
    is_used = jnp.minimum(lookup(jnp.ones((ROWS, slots), I32), seen), 1)
    down = lax.broadcasted_iota(I32, (used_width, used_width), 0)
    across = lax.broadcasted_iota(I32, (used_width, used_width), 1)
    rank = lookup(is_used, jnp.where(across < down, 1.0, 0.0))
    here = (down == rank[0:1]) & (is_used[0:1] > 0)
    lane = lax.broadcasted_iota(I32, (ROWS, used_width), 1)
    list_row = lax.broadcasted_iota(I32, (ROWS, used_width), 0)
    found = lookup(jnp.where(list_row == 0, lane // 16, lane % 16), jnp.where(here, 1.0, 0.0))
    ordered = found[0:1] * 16 + found[1:2]
    rank = jnp.where(lane == classes, classes, rank)
    count = jnp.sum(is_used[0:1].astype(F32), axis=1, keepdims=True).astype(I32)
    listed = jnp.where(list_row == 0, ordered, jnp.where(list_row == 1, rank, count))
    listed_ref[...] = listed
    to_smem = pltpu.make_async_copy(listed_ref, list_ref, sems.at[len(pairs)])
    to_smem.start()
    copies[2].wait()
    position = lax.broadcasted_iota(I32, (1, directions), 1)
    band_size = jnp.ones((1, directions), I32)
    bands = off_ref.shape[0] - 1
    for d in range(bands):
        start, end = off_ref[d], off_ref[d + 1]
        band_size = jnp.where((position >= start) & (position < end), end - start, band_size)
    weight = directions / (bands * band_size.astype(F32))
    copies[3].wait()
    weighted_ref[...] = (recv_ref[...].astype(F32) * weight).astype(BF16)
    copies[4].wait()
    rows_ref[...] = table_ref[...].astype(F32)
    to_smem.wait()
    count = list_ref[2, 0]
    copies[5].wait()
    copies[6].wait()
    fill_operators(0, jnp.minimum(count, first_count), list_ref, rows_ref, weighted_ref, rad_ref, t_ref)


def second_kernel(
    near_shift,
    list_ref,
    rows_ref,
    weighted_ref,
    rad_ref,
    near_src_ref,
    near_src_other_ref,
    near_hbm,
    near_other_hbm,
    low_ref,
    t_ref,
    near_ref,
    near_map_ref,
    sems,
):
    boxes, near_slots = near_hbm.shape[1:3]
    copies = []
    for i, array in enumerate((near_hbm, near_other_hbm)):
        for j in range(boxes):
            row = i * boxes + j
            copies.append(
                pltpu.make_async_copy(array.at[0, j], near_ref.at[row, pl.ds(0, near_slots)], sems.at[row])
            )
            copies[-1].start()
    first_count = low_ref.shape[0]
    copies.append(pltpu.make_async_copy(low_ref, t_ref.at[pl.ds(0, first_count)], sems.at[2 * boxes]))
    copies[-1].start()
    t_ref[t_ref.shape[0] - 1] = jnp.zeros(t_ref.shape[1:], BF16)
    for row in range(2 * boxes):
        near_ref[row, near_slots] = jnp.zeros(near_ref.shape[2:], BF16)
    width = near_map_ref.shape[1]
    near_at = lax.broadcasted_iota(I32, (width, near_slots), 0)
    row_at = lax.broadcasted_iota(I32, (ROWS, near_slots), 0)
    lane_at = lax.broadcasted_iota(I32, (ROWS, near_slots), 1)
    out_row = lax.broadcasted_iota(I32, near_map_ref.shape, 0)
    near_map = jnp.full(near_map_ref.shape, near_slots, I32)
    for j in range(2 * boxes):
        near = (near_src_ref if j < boxes else near_src_other_ref)[j % boxes]
        found = lookup(jnp.where(row_at == 0, lane_at, 1), jnp.where((near_at == near + near_shift) & (near >= 0), 1.0, 0.0))
        value = jnp.where(found[1:2] > 0, found[0:1], near_slots)
        near_map = jnp.where(out_row == j, value, near_map)
    near_map_ref[...] = near_map
    fill_operators(first_count, list_ref[2, 0], list_ref, rows_ref, weighted_ref, rad_ref, t_ref)
    for copy in copies:
        copy.wait()


def apply_kernel(
    places, first_row, boxes, halo, with_total, with_other, dtype, cls_ref, near_map_ref, list_ref, t_ref, near_ref, *rest
):
    source_refs, rest = rest[: sum(parts for _, _, parts in places)], rest[sum(parts for _, _, parts in places) :]
    if with_total:
        sum_ref, *rest = rest
    if with_other:
        other_ref, *rest = rest
    (out_ref,) = rest
    me = lax.axis_index("dir")
    region_boxes = boxes * lax.axis_size("dir")
    groups = []
    at = 0
    for rim, mask, parts in places:
        owner = me ^ mask
        base = owner * boxes + halo
        if rim:
            base = base + jnp.where(owner * boxes >= halo, -region_boxes, region_boxes)
        groups.append((base, source_refs[at : at + parts]))
        at += parts
    for j in range(boxes):
        row = first_row + j
        total = sum_ref[j] if with_total else None
        if with_other:
            other = other_ref[j].astype(F32)
            total = other if total is None else total + other
        for base, refs in groups:
            blocks = []
            for b in range(boxes):
                n = list_ref[1, cls_ref[row, base + b]]
                blocks.append(t_ref[n] + near_ref[row, near_map_ref[row, base + b]])
            values = [ref[...].reshape(-1, ref.shape[-1]) for ref in refs]
            rhs = values[0] if len(values) == 1 else jnp.concatenate(values, 0)
            added = jnp.dot(jnp.concatenate(blocks, 1), rhs, preferred_element_type=F32)
            total = added if total is None else total + added
        if len(out_ref.shape) == 4:
            out_ref[0, j] = total.astype(dtype)
        else:
            out_ref[j] = total.astype(dtype)


def shards(
    currents,
    radiate,
    receive,
    transfer_table,
    near_blocks,
    dir_offsets,
    trans_src,
    trans_tid,
    near_src,
):
    dir_count = lax.axis_size("dir")
    region_count = lax.axis_size("region")
    own = currents[0]
    boxes, unknowns, incidences = own.shape
    near_slots = near_src.shape[2]
    near_src = near_src.reshape(boxes, 1, near_slots)
    region_boxes = boxes * dir_count
    halo = region_boxes // 2
    near_halo = region_boxes // 4
    classes, directions = transfer_table.shape
    first_count = pad_to(classes // 4, UNROLL)
    top = dir_count // 2
    inner = range(2, top, 2)
    split = boxes // 2
    targets = 2 * boxes

    def partner(array, mask):
        return lax.ppermute(array, "dir", [(i, i ^ mask) for i in range(dir_count)])

    along = []
    for i in range(dir_count):
        for z in range(region_count):
            target = z + 1 if i >= top else z - 1
            if 0 <= target < region_count:
                along.append((i * region_count + z, i * region_count + target))

    def beyond(array):
        return lax.ppermute(array, ("dir", "region"), along)

    def pinned(array):
        return pltpu.with_memory_space_constraint(array, pltpu.VMEM)

    def in_hbm(array):
        return pltpu.with_memory_space_constraint(array, pltpu.HBM)

    width = pad_to(region_boxes + 2 * halo, LANES)
    map_shape = (pad_to(targets, ROWS), width)
    table_shape = (classes + 1, unknowns, unknowns)
    low_shape = (first_count, unknowns, unknowns)
    list_shape = (ROWS, pad_to(classes + 1, LANES))
    vmem, smem, hbm = whole(pltpu.VMEM), whole(pltpu.SMEM), whole(pltpu.HBM)
    operator_cost = pl.CostEstimate(
        flops=classes * unknowns * unknowns * directions, bytes_accessed=MIB, transcendentals=0
    )

    field = {0: own}
    rim = {}
    for m in inner:
        field[m] = partner(own, m)
    field[top] = partner(own, top)
    rim[0] = beyond(own)
    near_other = partner(near_blocks, 1)
    low, weighted, rad_here, rows, cls, near_src_here, listed = pl.pallas_call(
        functools.partial(first_kernel, first_count, boxes, halo, region_boxes),
        in_specs=[hbm] * 7,
        out_specs=[vmem] * 7,
        out_shape=(
            pltpu.VMEM(low_shape, BF16),
            pltpu.VMEM((unknowns, directions), BF16),
            pltpu.VMEM((directions, unknowns), BF16),
            pltpu.VMEM((classes, directions), F32),
            pltpu.VMEM(map_shape, I32),
            pltpu.VMEM(near_src.shape, I32),
            pltpu.VMEM(list_shape, I32),
        ),
        scratch_shapes=[
            pltpu.SMEM(dir_offsets.shape, I32),
            pltpu.VMEM(trans_src.shape, I32),
            pltpu.VMEM(trans_tid.shape, I32),
            pltpu.VMEM(transfer_table.shape, BF16),
            pltpu.VMEM(receive.shape, BF16),
            pltpu.SMEM(list_shape, I32),
            pltpu.SemaphoreType.DMA((8,)),
        ],
        compiler_params=pltpu.CompilerParams(vmem_limit_bytes=8 * MIB),
        cost_estimate=operator_cost,
    )(*[in_hbm(a) for a in (dir_offsets, trans_src, trans_tid, near_src, transfer_table, receive, radiate)])

    tied = lax.optimization_barrier((low, [field[m] for m in inner], field[top], rim[0]))
    low, inner_fields, field[top], rim[0] = tied
    near_src_other = partner(near_src_here, 1)
    for m, value in zip(inner, inner_fields):
        field[m] = value
    for m in inner:
        field[top + m] = partner(field[top], m)
    rim[top] = partner(rim[0], top)
    for m in inner:
        rim[m] = beyond(field[m])

    table, near_here, near_map = pl.pallas_call(
        functools.partial(second_kernel, halo - near_halo),
        in_specs=[smem] + [vmem] * 5 + [hbm] * 2 + [vmem],
        out_specs=[vmem] * 3,
        out_shape=(
            pltpu.VMEM(table_shape, BF16),
            pltpu.VMEM((targets, near_slots + 1, unknowns, unknowns), BF16),
            pltpu.VMEM(map_shape, I32),
        ),
        scratch_shapes=[pltpu.SemaphoreType.DMA((targets + 1,))],
        compiler_params=pltpu.CompilerParams(vmem_limit_bytes=8 * MIB),
        cost_estimate=operator_cost,
    )(
        listed,
        pinned(rows),
        pinned(weighted),
        pinned(rad_here),
        pinned(near_src_here),
        near_src_other,
        in_hbm(near_blocks),
        near_other,
        pinned(low),
    )

    def apply(places, first_row, total, other, dtype, shape):
        full = (boxes, unknowns, incidences)
        if len(places) > GROUP:
            total = apply(places[:GROUP], first_row, total, None, F32, full)
            return apply(places[GROUP:], first_row, total, other, dtype, shape)
        parts = [part for _, _, group in places for part in group]
        args = [cls, near_map, listed, pinned(table), pinned(near_here)] + [pinned(part) for part in parts]
        args += [pinned(extra) for extra in (total, other) if extra is not None]
        specs = [smem] * 3 + [vmem] * (len(args) - 3)
        layout = [(outside, mask, len(group)) for outside, mask, group in places]
        kernel = functools.partial(
            apply_kernel, layout, first_row, boxes, halo, total is not None, other is not None, dtype
        )
        return pl.pallas_call(
            kernel,
            in_specs=specs,
            out_specs=vmem,
            out_shape=pltpu.VMEM(shape, dtype) if len(shape) == 3 else jax.ShapeDtypeStruct(shape, dtype),
            compiler_params=pltpu.CompilerParams(vmem_limit_bytes=12 * MIB),
            cost_estimate=pl.CostEstimate(
                flops=2 * len(places) * (boxes * unknowns) ** 2 * incidences, bytes_accessed=MIB, transcendentals=0
            ),
        )(*args)

    tied = lax.optimization_barrier(
        (table, [field[top + m] for m in inner], [rim[m] for m in inner], rim[top])
    )
    table, far_fields, inner_rims, rim[top] = tied
    for m, value, other in zip(inner, far_fields, inner_rims):
        field[top + m], rim[m] = value, other
    last = {m: [partner(rim[top][:split], m), partner(rim[m][split:], top)] for m in inner}

    full = (boxes, unknowns, incidences)
    early = [(False, m, [field[m]]) for m in (0, *inner, top)] + [(True, 0, [rim[0]])]
    middle = [(False, top + m, [field[top + m]]) for m in inner]
    middle += [(True, m, [rim[m]]) for m in (*inner, top)]
    for_other = apply(early + middle, boxes, None, None, BF16, full)

    for_other, last = lax.optimization_barrier((for_other, last))
    late = [(True, top + m, last[m]) for m in inner]
    late += [(True, top + m + 1, [partner(part, 1) for part in last[m]]) for m in inner]
    from_other = partner(for_other, 1)
    total = apply(early, 0, None, None, F32, full)
    return apply(middle + late, 0, total, from_other, BF16, currents.shape)


def solution(mesh):
    placed = (
        P("region", "dir", None, None),
        P(),
        P(),
        P(),
        P("region", "dir", None, None, None),
        P(),
        P("region", None, None),
        P("region", None, None),
        P("region", "dir", None),
    )
    return jax.shard_map(
        shards,
        mesh=mesh,
        in_specs=placed,
        out_specs=P("region", "dir", None, None),
        check_vma=False,
    )
```

```python
import functools

import jax
import jax.numpy as jnp
from jax import lax
from jax.experimental import pallas as pl
from jax.experimental.pallas import tpu as pltpu
from jax.sharding import PartitionSpec as P

BF16, F32, I32 = jnp.bfloat16, jnp.float32, jnp.int32
NT_DIMS = (((1,), (1,)), ((), ()))
LANES = 128
ROWS = 8
UNROLL = 16
TAIL = 4
GROUP = 8
MIB = 2**20


def pad_to(size, tile):
    return -(-size // tile) * tile


def whole(memory_space):
    return pl.BlockSpec(memory_space=memory_space)


def lookup(parts, hot):
    return lax.dot_general(parts.astype(F32).astype(BF16), hot.astype(BF16), NT_DIMS, preferred_element_type=F32).astype(I32)


def fill_operators(begin, end, list_ref, rows_ref, weighted_ref, rad_ref, out_ref):
    def step(at, wide):
        for u in range(wide):
            place = jnp.minimum(at + u, end - 1)
            row = rows_ref[pl.ds(list_ref[0, place], 1), :].astype(BF16)
            product = weighted_ref[...] * row
            out_ref[place] = jnp.dot(product, rad_ref[...], preferred_element_type=F32).astype(BF16)

    def main_step(i, carry):
        step(begin + i * UNROLL, UNROLL)
        return carry

    def tail_step(i, carry):
        step(begin + main * UNROLL + i * TAIL, TAIL)
        return carry

    count = jnp.maximum(end - begin, 0)
    main = count // UNROLL
    lax.fori_loop(0, main, main_step, 0)
    lax.fori_loop(0, (count - main * UNROLL + TAIL - 1) // TAIL, tail_step, 0)


def first_kernel(
    first_count,
    boxes,
    halo,
    region_boxes,
    off_hbm,
    src_hbm,
    tid_hbm,
    table_hbm,
    recv_hbm,
    rad_hbm,
    t_ref,
    weighted_ref,
    rad_ref,
    rows_ref,
    cls_ref,
    listed_ref,
    off_ref,
    src_ref,
    tid_ref,
    table_ref,
    recv_ref,
    list_ref,
    sems,
):
    pairs = [
        (src_hbm, src_ref),
        (tid_hbm, tid_ref),
        (off_hbm, off_ref),
        (recv_hbm, recv_ref),
        (table_hbm, table_ref),
        (rad_hbm, rad_ref),
    ]
    copies = [pltpu.make_async_copy(a, b, sems.at[i]) for i, (a, b) in enumerate(pairs)]
    for copy in copies:
        copy.start()
    classes = table_ref.shape[0]
    directions = recv_ref.shape[1]
    me = lax.axis_index("dir")
    dir_count = region_boxes // boxes
    top = dir_count // 2
    slots = src_ref.shape[2]
    width = cls_ref.shape[1]
    used_width = listed_ref.shape[1]
    ext_at = lax.broadcasted_iota(I32, (width, slots), 0)
    class_at = lax.broadcasted_iota(I32, (used_width, slots), 0)
    row_at = lax.broadcasted_iota(I32, (ROWS, slots), 0)
    out_row = lax.broadcasted_iota(I32, cls_ref.shape, 0)
    seen = jnp.zeros((used_width, slots), F32)
    cls = jnp.full(cls_ref.shape, classes, I32)
    copies[0].wait()
    copies[1].wait()
    for j in range(2 * boxes):
        target = (me if j < boxes else me ^ 1) * boxes + j % boxes
        src = src_ref[0, pl.ds(target, 1), :]
        tid = tid_ref[0, pl.ds(target, 1), :]
        mask = (((src - halo + region_boxes) // boxes) % dir_count) ^ me
        beyond = (src < halo) | (src >= halo + region_boxes)
        late = beyond & ((mask & top) != 0) & ((mask & (top - 2)) != 0)
        even = (mask & 1) == 0
        here = (src >= 0) & ((even | late) if j < boxes else (even & ~late))
        seen = jnp.where((class_at == tid) & here, 1.0, seen)
        parts = jnp.where(row_at == 0, tid // 16, jnp.where(row_at == 1, tid % 16, 1))
        found = lookup(parts, jnp.where(ext_at == src, 1.0, 0.0))
        value = jnp.where(found[2:3] > 0, found[0:1] * 16 + found[1:2], classes)
        cls = jnp.where(out_row == j, value, cls)
    cls_ref[...] = cls
    is_used = jnp.minimum(lookup(jnp.ones((ROWS, slots), I32), seen), 1)
    down = lax.broadcasted_iota(I32, (used_width, used_width), 0)
    across = lax.broadcasted_iota(I32, (used_width, used_width), 1)
    rank = lookup(is_used, jnp.where(across < down, 1.0, 0.0))
    here = (down == rank[0:1]) & (is_used[0:1] > 0)
    lane = lax.broadcasted_iota(I32, (ROWS, used_width), 1)
    list_row = lax.broadcasted_iota(I32, (ROWS, used_width), 0)
    found = lookup(jnp.where(list_row == 0, lane // 16, lane % 16), jnp.where(here, 1.0, 0.0))
    ordered = found[0:1] * 16 + found[1:2]
    rank = jnp.where(lane == classes, classes, rank)
    count = jnp.sum(is_used[0:1].astype(F32), axis=1, keepdims=True).astype(I32)
    listed = jnp.where(list_row == 0, ordered, jnp.where(list_row == 1, rank, count))
    listed_ref[...] = listed
    to_smem = pltpu.make_async_copy(listed_ref, list_ref, sems.at[len(pairs)])
    to_smem.start()
    copies[2].wait()
    position = lax.broadcasted_iota(I32, (1, directions), 1)
    band_size = jnp.ones((1, directions), I32)
    bands = off_ref.shape[0] - 1
    for d in range(bands):
        start, end = off_ref[d], off_ref[d + 1]
        band_size = jnp.where((position >= start) & (position < end), end - start, band_size)
    weight = directions / (bands * band_size.astype(F32))
    copies[3].wait()
    weighted_ref[...] = (recv_ref[...].astype(F32) * weight).astype(BF16)
    copies[4].wait()
    rows_ref[...] = table_ref[...].astype(F32)
    to_smem.wait()
    count = list_ref[2, 0]
    copies[5].wait()
    fill_operators(0, jnp.minimum(count, first_count), list_ref, rows_ref, weighted_ref, rad_ref, t_ref)


def second_kernel(
    near_shift,
    list_ref,
    rows_ref,
    weighted_ref,
    rad_ref,
    near_src_ref,
    near_src_other_ref,
    near_hbm,
    near_other_hbm,
    low_ref,
    t_ref,
    near_ref,
    near_map_ref,
    sems,
):
    boxes, near_slots = near_hbm.shape[1:3]
    copies = []
    for i, array in enumerate((near_hbm, near_other_hbm)):
        for j in range(boxes):
            row = i * boxes + j
            copies.append(
                pltpu.make_async_copy(array.at[0, j], near_ref.at[row, pl.ds(0, near_slots)], sems.at[row])
            )
            copies[-1].start()
    first_count = low_ref.shape[0]
    copies.append(pltpu.make_async_copy(low_ref, t_ref.at[pl.ds(0, first_count)], sems.at[2 * boxes]))
    copies[-1].start()
    t_ref[t_ref.shape[0] - 1] = jnp.zeros(t_ref.shape[1:], BF16)
    for row in range(2 * boxes):
        near_ref[row, near_slots] = jnp.zeros(near_ref.shape[2:], BF16)
    width = near_map_ref.shape[1]
    near_at = lax.broadcasted_iota(I32, (width, near_slots), 0)
    row_at = lax.broadcasted_iota(I32, (ROWS, near_slots), 0)
    lane_at = lax.broadcasted_iota(I32, (ROWS, near_slots), 1)
    out_row = lax.broadcasted_iota(I32, near_map_ref.shape, 0)
    near_map = jnp.full(near_map_ref.shape, near_slots, I32)
    for j in range(2 * boxes):
        near = (near_src_ref if j < boxes else near_src_other_ref)[j % boxes]
        found = lookup(jnp.where(row_at == 0, lane_at, 1), jnp.where((near_at == near + near_shift) & (near >= 0), 1.0, 0.0))
        value = jnp.where(found[1:2] > 0, found[0:1], near_slots)
        near_map = jnp.where(out_row == j, value, near_map)
    near_map_ref[...] = near_map
    fill_operators(first_count, list_ref[2, 0], list_ref, rows_ref, weighted_ref, rad_ref, t_ref)
    for copy in copies:
        copy.wait()


def apply_kernel(
    places, first_row, boxes, halo, with_total, with_other, dtype, cls_ref, near_map_ref, list_ref, t_ref, near_ref, *rest
):
    source_refs, rest = rest[: sum(parts for _, _, parts in places)], rest[sum(parts for _, _, parts in places) :]
    if with_total:
        sum_ref, *rest = rest
    if with_other:
        other_ref, *rest = rest
    (out_ref,) = rest
    me = lax.axis_index("dir")
    region_boxes = boxes * lax.axis_size("dir")
    groups = []
    at = 0
    for rim, mask, parts in places:
        owner = me ^ mask
        base = owner * boxes + halo
        if rim:
            base = base + jnp.where(owner * boxes >= halo, -region_boxes, region_boxes)
        groups.append((base, source_refs[at : at + parts]))
        at += parts
    for j in range(boxes):
        row = first_row + j
        total = sum_ref[j] if with_total else None
        if with_other:
            other = other_ref[j].astype(F32)
            total = other if total is None else total + other
        for base, refs in groups:
            blocks = []
            for b in range(boxes):
                n = list_ref[1, cls_ref[row, base + b]]
                blocks.append(t_ref[n] + near_ref[row, near_map_ref[row, base + b]])
            values = [ref[...].reshape(-1, ref.shape[-1]) for ref in refs]
            rhs = values[0] if len(values) == 1 else jnp.concatenate(values, 0)
            added = jnp.dot(jnp.concatenate(blocks, 1), rhs, preferred_element_type=F32)
            total = added if total is None else total + added
        if len(out_ref.shape) == 4:
            out_ref[0, j] = total.astype(dtype)
        else:
            out_ref[j] = total.astype(dtype)


def shards(
    currents,
    radiate,
    receive,
    transfer_table,
    near_blocks,
    dir_offsets,
    trans_src,
    trans_tid,
    near_src,
):
    dir_count = lax.axis_size("dir")
    region_count = lax.axis_size("region")
    own = currents[0]
    boxes, unknowns, incidences = own.shape
    near_slots = near_src.shape[2]
    near_src = near_src.reshape(boxes, 1, near_slots)
    region_boxes = boxes * dir_count
    halo = region_boxes // 2
    near_halo = region_boxes // 4
    classes, directions = transfer_table.shape
    first_count = pad_to(classes // 4, UNROLL)
    top = dir_count // 2
    inner = range(2, top, 2)
    split = boxes // 2
    targets = 2 * boxes

    def partner(array, mask):
        return lax.ppermute(array, "dir", [(i, i ^ mask) for i in range(dir_count)])

    along = []
    for i in range(dir_count):
        for z in range(region_count):
            target = z + 1 if i >= top else z - 1
            if 0 <= target < region_count:
                along.append((i * region_count + z, i * region_count + target))

    def beyond(array):
        return lax.ppermute(array, ("dir", "region"), along)

    def pinned(array):
        return pltpu.with_memory_space_constraint(array, pltpu.VMEM)

    def in_hbm(array):
        return pltpu.with_memory_space_constraint(array, pltpu.HBM)

    width = pad_to(region_boxes + 2 * halo, LANES)
    map_shape = (pad_to(targets, ROWS), width)
    table_shape = (classes + 1, unknowns, unknowns)
    low_shape = (first_count, unknowns, unknowns)
    list_shape = (ROWS, pad_to(classes + 1, LANES))
    vmem, smem, hbm = whole(pltpu.VMEM), whole(pltpu.SMEM), whole(pltpu.HBM)
    operator_cost = pl.CostEstimate(
        flops=classes * unknowns * unknowns * directions, bytes_accessed=MIB, transcendentals=0
    )

    field = {0: own}
    rim = {}
    for m in inner:
        field[m] = partner(own, m)
    field[top] = partner(own, top)
    rim[0] = beyond(own)
    near_other = partner(near_blocks, 1)
    near_src_other = partner(near_src, 1)
    low, weighted, rad_here, rows, cls, listed = pl.pallas_call(
        functools.partial(first_kernel, first_count, boxes, halo, region_boxes),
        in_specs=[hbm] * 6,
        out_specs=[vmem] * 6,
        out_shape=(
            pltpu.VMEM(low_shape, BF16),
            pltpu.VMEM((unknowns, directions), BF16),
            pltpu.VMEM((directions, unknowns), BF16),
            pltpu.VMEM((classes, directions), F32),
            pltpu.VMEM(map_shape, I32),
            pltpu.VMEM(list_shape, I32),
        ),
        scratch_shapes=[
            pltpu.SMEM(dir_offsets.shape, I32),
            pltpu.VMEM(trans_src.shape, I32),
            pltpu.VMEM(trans_tid.shape, I32),
            pltpu.VMEM(transfer_table.shape, BF16),
            pltpu.VMEM(receive.shape, BF16),
            pltpu.SMEM(list_shape, I32),
            pltpu.SemaphoreType.DMA((7,)),
        ],
        compiler_params=pltpu.CompilerParams(vmem_limit_bytes=8 * MIB),
        cost_estimate=operator_cost,
    )(*[in_hbm(a) for a in (dir_offsets, trans_src, trans_tid, transfer_table, receive, radiate)])

    tied = lax.optimization_barrier((low, [field[m] for m in inner], field[top], rim[0]))
    low, inner_fields, field[top], rim[0] = tied
    for m, value in zip(inner, inner_fields):
        field[m] = value
    for m in inner:
        field[top + m] = partner(field[top], m)
    rim[top] = partner(rim[0], top)
    for m in inner:
        rim[m] = beyond(field[m])

    table, near_here, near_map = pl.pallas_call(
        functools.partial(second_kernel, halo - near_halo),
        in_specs=[smem] + [vmem] * 5 + [hbm] * 2 + [vmem],
        out_specs=[vmem] * 3,
        out_shape=(
            pltpu.VMEM(table_shape, BF16),
            pltpu.VMEM((targets, near_slots + 1, unknowns, unknowns), BF16),
            pltpu.VMEM(map_shape, I32),
        ),
        scratch_shapes=[pltpu.SemaphoreType.DMA((targets + 1,))],
        compiler_params=pltpu.CompilerParams(vmem_limit_bytes=8 * MIB),
        cost_estimate=operator_cost,
    )(
        listed,
        pinned(rows),
        pinned(weighted),
        pinned(rad_here),
        near_src,
        near_src_other,
        in_hbm(near_blocks),
        near_other,
        pinned(low),
    )

    def apply(places, first_row, total, other, dtype, shape):
        full = (boxes, unknowns, incidences)
        if len(places) > GROUP:
            total = apply(places[:GROUP], first_row, total, None, F32, full)
            return apply(places[GROUP:], first_row, total, other, dtype, shape)
        parts = [part for _, _, group in places for part in group]
        args = [cls, near_map, listed, pinned(table), pinned(near_here)] + [pinned(part) for part in parts]
        args += [pinned(extra) for extra in (total, other) if extra is not None]
        specs = [smem] * 3 + [vmem] * (len(args) - 3)
        layout = [(outside, mask, len(group)) for outside, mask, group in places]
        kernel = functools.partial(
            apply_kernel, layout, first_row, boxes, halo, total is not None, other is not None, dtype
        )
        return pl.pallas_call(
            kernel,
            in_specs=specs,
            out_specs=vmem,
            out_shape=pltpu.VMEM(shape, dtype) if len(shape) == 3 else jax.ShapeDtypeStruct(shape, dtype),
            compiler_params=pltpu.CompilerParams(vmem_limit_bytes=12 * MIB),
            cost_estimate=pl.CostEstimate(
                flops=2 * len(places) * (boxes * unknowns) ** 2 * incidences, bytes_accessed=MIB, transcendentals=0
            ),
        )(*args)

    tied = lax.optimization_barrier(
        (table, [field[top + m] for m in inner], [rim[m] for m in inner], rim[top])
    )
    table, far_fields, inner_rims, rim[top] = tied
    for m, value, other in zip(inner, far_fields, inner_rims):
        field[top + m], rim[m] = value, other
    last = {m: [partner(rim[top][:split], m), partner(rim[m][split:], top)] for m in inner}

    full = (boxes, unknowns, incidences)
    early = [(False, m, [field[m]]) for m in (0, *inner, top)] + [(True, 0, [rim[0]])]
    middle = [(False, top + m, [field[top + m]]) for m in inner]
    middle += [(True, m, [rim[m]]) for m in (*inner, top)]
    for_other = apply(early + middle, boxes, None, None, BF16, full)

    from_other = partner(for_other, 1)
    total = apply(early, 0, None, None, F32, full)

    total, last = lax.optimization_barrier((total, last))
    turned = {m: [partner(part, 1) for part in last[m]] for m in inner}
    total = apply(middle, 0, total, from_other, F32, full)
    late = [(True, top + m, last[m]) for m in inner] + [(True, top + m + 1, turned[m]) for m in inner]
    return apply(late, 0, total, None, BF16, currents.shape)


def solution(mesh):
    placed = (
        P("region", "dir", None, None),
        P(),
        P(),
        P(),
        P("region", "dir", None, None, None),
        P(),
        P("region", None, None),
        P("region", None, None),
        P("region", "dir", None),
    )
    return jax.shard_map(
        shards,
        mesh=mesh,
        in_specs=placed,
        out_specs=P("region", "dir", None, None),
        check_vma=False,
    )
```

```python
import functools

import jax
import jax.numpy as jnp
from jax import lax
from jax.experimental import pallas as pl
from jax.experimental.pallas import tpu as pltpu
from jax.sharding import PartitionSpec as P

BF16, F32, I32 = jnp.bfloat16, jnp.float32, jnp.int32
NT_DIMS = (((1,), (1,)), ((), ()))
LANES = 128
ROWS = 8
UNROLL = 16
TAIL = 4
GROUP = 8
MIB = 2**20


def pad_to(size, tile):
    return -(-size // tile) * tile


def whole(memory_space):
    return pl.BlockSpec(memory_space=memory_space)


def lookup(parts, hot):
    return lax.dot_general(parts.astype(F32).astype(BF16), hot.astype(BF16), NT_DIMS, preferred_element_type=F32).astype(I32)


def fill_operators(begin, end, list_ref, rows_ref, weighted_ref, rad_ref, out_ref):
    def step(at, wide):
        for u in range(wide):
            place = jnp.minimum(at + u, end - 1)
            row = rows_ref[pl.ds(list_ref[0, place], 1), :].astype(BF16)
            product = weighted_ref[...] * row
            out_ref[place] = jnp.dot(product, rad_ref[...], preferred_element_type=F32).astype(BF16)

    def main_step(i, carry):
        step(begin + i * UNROLL, UNROLL)
        return carry

    def tail_step(i, carry):
        step(begin + main * UNROLL + i * TAIL, TAIL)
        return carry

    count = jnp.maximum(end - begin, 0)
    main = count // UNROLL
    lax.fori_loop(0, main, main_step, 0)
    lax.fori_loop(0, (count - main * UNROLL + TAIL - 1) // TAIL, tail_step, 0)


def first_kernel(
    first_count,
    boxes,
    halo,
    region_boxes,
    off_hbm,
    src_hbm,
    tid_hbm,
    table_hbm,
    recv_hbm,
    rad_hbm,
    t_ref,
    weighted_ref,
    rad_ref,
    rows_ref,
    cls_ref,
    listed_ref,
    off_ref,
    src_ref,
    tid_ref,
    table_ref,
    recv_ref,
    list_ref,
    sems,
):
    pairs = [
        (src_hbm, src_ref),
        (tid_hbm, tid_ref),
        (off_hbm, off_ref),
        (recv_hbm, recv_ref),
        (table_hbm, table_ref),
        (rad_hbm, rad_ref),
    ]
    copies = [pltpu.make_async_copy(a, b, sems.at[i]) for i, (a, b) in enumerate(pairs)]
    for copy in copies:
        copy.start()
    classes = table_ref.shape[0]
    directions = recv_ref.shape[1]
    me = lax.axis_index("dir")
    dir_count = region_boxes // boxes
    top = dir_count // 2
    slots = src_ref.shape[2]
    width = cls_ref.shape[1]
    used_width = listed_ref.shape[1]
    ext_at = lax.broadcasted_iota(I32, (width, slots), 0)
    class_at = lax.broadcasted_iota(I32, (used_width, slots), 0)
    row_at = lax.broadcasted_iota(I32, (ROWS, slots), 0)
    out_row = lax.broadcasted_iota(I32, cls_ref.shape, 0)
    seen = jnp.zeros((used_width, slots), F32)
    cls = jnp.full(cls_ref.shape, classes, I32)
    copies[0].wait()
    copies[1].wait()
    for j in range(2 * boxes):
        target = (me if j < boxes else me ^ 1) * boxes + j % boxes
        src = src_ref[0, pl.ds(target, 1), :]
        tid = tid_ref[0, pl.ds(target, 1), :]
        mask = (((src - halo + region_boxes) // boxes) % dir_count) ^ me
        beyond = (src < halo) | (src >= halo + region_boxes)
        late = beyond & ((mask & top) != 0) & ((mask & (top - 2)) != 0)
        even = (mask & 1) == 0
        here = (src >= 0) & ((even | late) if j < boxes else (even & ~late))
        seen = jnp.where((class_at == tid) & here, 1.0, seen)
        parts = jnp.where(row_at == 0, tid // 16, jnp.where(row_at == 1, tid % 16, 1))
        found = lookup(parts, jnp.where(ext_at == src, 1.0, 0.0))
        value = jnp.where(found[2:3] > 0, found[0:1] * 16 + found[1:2], classes)
        cls = jnp.where(out_row == j, value, cls)
    cls_ref[...] = cls
    is_used = jnp.minimum(lookup(jnp.ones((ROWS, slots), I32), seen), 1)
    down = lax.broadcasted_iota(I32, (used_width, used_width), 0)
    across = lax.broadcasted_iota(I32, (used_width, used_width), 1)
    rank = lookup(is_used, jnp.where(across < down, 1.0, 0.0))
    here = (down == rank[0:1]) & (is_used[0:1] > 0)
    lane = lax.broadcasted_iota(I32, (ROWS, used_width), 1)
    list_row = lax.broadcasted_iota(I32, (ROWS, used_width), 0)
    found = lookup(jnp.where(list_row == 0, lane // 16, lane % 16), jnp.where(here, 1.0, 0.0))
    ordered = found[0:1] * 16 + found[1:2]
    rank = jnp.where(lane == classes, classes, rank)
    count = jnp.sum(is_used[0:1].astype(F32), axis=1, keepdims=True).astype(I32)
    listed = jnp.where(list_row == 0, ordered, jnp.where(list_row == 1, rank, count))
    listed_ref[...] = listed
    to_smem = pltpu.make_async_copy(listed_ref, list_ref, sems.at[len(pairs)])
    to_smem.start()
    copies[2].wait()
    position = lax.broadcasted_iota(I32, (1, directions), 1)
    band_size = jnp.ones((1, directions), I32)
    bands = off_ref.shape[0] - 1
    for d in range(bands):
        start, end = off_ref[d], off_ref[d + 1]
        band_size = jnp.where((position >= start) & (position < end), end - start, band_size)
    weight = directions / (bands * band_size.astype(F32))
    copies[3].wait()
    weighted_ref[...] = (recv_ref[...].astype(F32) * weight).astype(BF16)
    copies[4].wait()
    rows_ref[...] = table_ref[...].astype(F32)
    to_smem.wait()
    count = list_ref[2, 0]
    copies[5].wait()
    fill_operators(0, jnp.minimum(count, first_count), list_ref, rows_ref, weighted_ref, rad_ref, t_ref)


def second_kernel(
    near_shift,
    list_ref,
    rows_ref,
    weighted_ref,
    rad_ref,
    near_src_ref,
    near_src_other_ref,
    near_hbm,
    near_other_hbm,
    low_ref,
    t_ref,
    near_ref,
    near_map_ref,
    sems,
):
    boxes, near_slots = near_hbm.shape[1:3]
    copies = []
    for i, array in enumerate((near_hbm, near_other_hbm)):
        for j in range(boxes):
            row = i * boxes + j
            copies.append(
                pltpu.make_async_copy(array.at[0, j], near_ref.at[row, pl.ds(0, near_slots)], sems.at[row])
            )
            copies[-1].start()
    first_count = low_ref.shape[0]
    copies.append(pltpu.make_async_copy(low_ref, t_ref.at[pl.ds(0, first_count)], sems.at[2 * boxes]))
    copies[-1].start()
    t_ref[t_ref.shape[0] - 1] = jnp.zeros(t_ref.shape[1:], BF16)
    for row in range(2 * boxes):
        near_ref[row, near_slots] = jnp.zeros(near_ref.shape[2:], BF16)
    width = near_map_ref.shape[1]
    near_at = lax.broadcasted_iota(I32, (width, near_slots), 0)
    row_at = lax.broadcasted_iota(I32, (ROWS, near_slots), 0)
    lane_at = lax.broadcasted_iota(I32, (ROWS, near_slots), 1)
    out_row = lax.broadcasted_iota(I32, near_map_ref.shape, 0)
    near_map = jnp.full(near_map_ref.shape, near_slots, I32)
    for j in range(2 * boxes):
        near = (near_src_ref if j < boxes else near_src_other_ref)[j % boxes]
        found = lookup(jnp.where(row_at == 0, lane_at, 1), jnp.where((near_at == near + near_shift) & (near >= 0), 1.0, 0.0))
        value = jnp.where(found[1:2] > 0, found[0:1], near_slots)
        near_map = jnp.where(out_row == j, value, near_map)
    near_map_ref[...] = near_map
    fill_operators(first_count, list_ref[2, 0], list_ref, rows_ref, weighted_ref, rad_ref, t_ref)
    for copy in copies:
        copy.wait()


def apply_kernel(
    places, first_row, boxes, halo, with_total, with_other, dtype, cls_ref, near_map_ref, list_ref, t_ref, near_ref, *rest
):
    source_refs, rest = rest[: sum(parts for _, _, parts in places)], rest[sum(parts for _, _, parts in places) :]
    if with_total:
        sum_ref, *rest = rest
    if with_other:
        other_ref, *rest = rest
    (out_ref,) = rest
    me = lax.axis_index("dir")
    region_boxes = boxes * lax.axis_size("dir")
    groups = []
    at = 0
    for rim, mask, parts in places:
        owner = me ^ mask
        base = owner * boxes + halo
        if rim:
            base = base + jnp.where(owner * boxes >= halo, -region_boxes, region_boxes)
        groups.append((base, source_refs[at : at + parts]))
        at += parts
    for j in range(boxes):
        row = first_row + j
        total = sum_ref[j] if with_total else None
        if with_other:
            other = other_ref[j].astype(F32)
            total = other if total is None else total + other
        for base, refs in groups:
            blocks = []
            for b in range(boxes):
                n = list_ref[1, cls_ref[row, base + b]]
                blocks.append(t_ref[n] + near_ref[row, near_map_ref[row, base + b]])
            values = [ref[...].reshape(-1, ref.shape[-1]) for ref in refs]
            rhs = values[0] if len(values) == 1 else jnp.concatenate(values, 0)
            added = jnp.dot(jnp.concatenate(blocks, 1), rhs, preferred_element_type=F32)
            total = added if total is None else total + added
        if len(out_ref.shape) == 4:
            out_ref[0, j] = total.astype(dtype)
        else:
            out_ref[j] = total.astype(dtype)


def shards(
    currents,
    radiate,
    receive,
    transfer_table,
    near_blocks,
    dir_offsets,
    trans_src,
    trans_tid,
    near_src,
):
    dir_count = lax.axis_size("dir")
    region_count = lax.axis_size("region")
    own = currents[0]
    boxes, unknowns, incidences = own.shape
    near_slots = near_src.shape[2]
    near_src = near_src.reshape(boxes, 1, near_slots)
    region_boxes = boxes * dir_count
    halo = region_boxes // 2
    near_halo = region_boxes // 4
    classes, directions = transfer_table.shape
    first_count = pad_to(classes // 4, UNROLL)
    top = dir_count // 2
    inner = range(2, top, 2)
    split = boxes // 2
    targets = 2 * boxes

    def partner(array, mask):
        return lax.ppermute(array, "dir", [(i, i ^ mask) for i in range(dir_count)])

    along = []
    for i in range(dir_count):
        for z in range(region_count):
            target = z + 1 if i >= top else z - 1
            if 0 <= target < region_count:
                along.append((i * region_count + z, i * region_count + target))

    def beyond(array):
        return lax.ppermute(array, ("dir", "region"), along)

    def pinned(array):
        return pltpu.with_memory_space_constraint(array, pltpu.VMEM)

    def in_hbm(array):
        return pltpu.with_memory_space_constraint(array, pltpu.HBM)

    width = pad_to(region_boxes + 2 * halo, LANES)
    map_shape = (pad_to(targets, ROWS), width)
    table_shape = (classes + 1, unknowns, unknowns)
    low_shape = (first_count, unknowns, unknowns)
    list_shape = (ROWS, pad_to(classes + 1, LANES))
    vmem, smem, hbm = whole(pltpu.VMEM), whole(pltpu.SMEM), whole(pltpu.HBM)
    operator_cost = pl.CostEstimate(
        flops=classes * unknowns * unknowns * directions, bytes_accessed=MIB, transcendentals=0
    )

    field = {0: own}
    rim = {}
    for m in inner:
        field[m] = partner(own, m)
    field[top] = partner(own, top)
    rim[0] = beyond(own)
    near_other = partner(near_blocks, 1)
    near_src_other = partner(near_src, 1)
    low, weighted, rad_here, rows, cls, listed = pl.pallas_call(
        functools.partial(first_kernel, first_count, boxes, halo, region_boxes),
        in_specs=[hbm] * 6,
        out_specs=[vmem] * 6,
        out_shape=(
            pltpu.VMEM(low_shape, BF16),
            pltpu.VMEM((unknowns, directions), BF16),
            pltpu.VMEM((directions, unknowns), BF16),
            pltpu.VMEM((classes, directions), F32),
            pltpu.VMEM(map_shape, I32),
            pltpu.VMEM(list_shape, I32),
        ),
        scratch_shapes=[
            pltpu.SMEM(dir_offsets.shape, I32),
            pltpu.VMEM(trans_src.shape, I32),
            pltpu.VMEM(trans_tid.shape, I32),
            pltpu.VMEM(transfer_table.shape, BF16),
            pltpu.VMEM(receive.shape, BF16),
            pltpu.SMEM(list_shape, I32),
            pltpu.SemaphoreType.DMA((7,)),
        ],
        compiler_params=pltpu.CompilerParams(vmem_limit_bytes=8 * MIB),
        cost_estimate=operator_cost,
    )(*[in_hbm(a) for a in (dir_offsets, trans_src, trans_tid, transfer_table, receive, radiate)])

    tied = lax.optimization_barrier((low, [field[m] for m in inner], field[top], rim[0]))
    low, inner_fields, field[top], rim[0] = tied
    for m, value in zip(inner, inner_fields):
        field[m] = value
    for m in inner:
        field[top + m] = partner(field[top], m)
    rim[top] = partner(rim[0], top)
    for m in inner:
        rim[m] = beyond(field[m])

    table, near_here, near_map = pl.pallas_call(
        functools.partial(second_kernel, halo - near_halo),
        in_specs=[smem] + [vmem] * 5 + [hbm] * 2 + [vmem],
        out_specs=[vmem] * 3,
        out_shape=(
            pltpu.VMEM(table_shape, BF16),
            pltpu.VMEM((targets, near_slots + 1, unknowns, unknowns), BF16),
            pltpu.VMEM(map_shape, I32),
        ),
        scratch_shapes=[pltpu.SemaphoreType.DMA((targets + 1,))],
        compiler_params=pltpu.CompilerParams(vmem_limit_bytes=8 * MIB),
        cost_estimate=operator_cost,
    )(
        listed,
        pinned(rows),
        pinned(weighted),
        pinned(rad_here),
        near_src,
        near_src_other,
        in_hbm(near_blocks),
        near_other,
        pinned(low),
    )

    def apply(places, first_row, total, other, dtype, shape):
        full = (boxes, unknowns, incidences)
        if len(places) > GROUP:
            total = apply(places[:GROUP], first_row, total, None, F32, full)
            return apply(places[GROUP:], first_row, total, other, dtype, shape)
        parts = [part for _, _, group in places for part in group]
        args = [cls, near_map, listed, pinned(table), pinned(near_here)] + [pinned(part) for part in parts]
        args += [pinned(extra) for extra in (total, other) if extra is not None]
        specs = [smem] * 3 + [vmem] * (len(args) - 3)
        layout = [(outside, mask, len(group)) for outside, mask, group in places]
        kernel = functools.partial(
            apply_kernel, layout, first_row, boxes, halo, total is not None, other is not None, dtype
        )
        return pl.pallas_call(
            kernel,
            in_specs=specs,
            out_specs=vmem,
            out_shape=pltpu.VMEM(shape, dtype) if len(shape) == 3 else jax.ShapeDtypeStruct(shape, dtype),
            compiler_params=pltpu.CompilerParams(vmem_limit_bytes=12 * MIB),
            cost_estimate=pl.CostEstimate(flops=MIB, bytes_accessed=MIB, transcendentals=0),
        )(*args)

    tied = lax.optimization_barrier(
        (table, [field[top + m] for m in inner], [rim[m] for m in inner], rim[top])
    )
    table, far_fields, inner_rims, rim[top] = tied
    for m, value, other in zip(inner, far_fields, inner_rims):
        field[top + m], rim[m] = value, other
    last = {m: [partner(rim[top][:split], m), partner(rim[m][split:], top)] for m in inner}

    full = (boxes, unknowns, incidences)
    early = [(False, m, [field[m]]) for m in (0, *inner, top)] + [(True, 0, [rim[0]])]
    middle = [(False, top + m, [field[top + m]]) for m in inner]
    middle += [(True, m, [rim[m]]) for m in (*inner, top)]
    for_other = apply(early + middle, boxes, None, None, BF16, full)

    from_other = partner(for_other, 1)
    total = apply(early, 0, None, None, F32, full)

    total, last = lax.optimization_barrier((total, last))
    turned = {m: [partner(part, 1) for part in last[m]] for m in inner}
    total = apply(middle, 0, total, from_other, F32, full)
    late = [(True, top + m, last[m]) for m in inner] + [(True, top + m + 1, turned[m]) for m in inner]
    return apply(late, 0, total, None, BF16, currents.shape)


def solution(mesh):
    placed = (
        P("region", "dir", None, None),
        P(),
        P(),
        P(),
        P("region", "dir", None, None, None),
        P(),
        P("region", None, None),
        P("region", None, None),
        P("region", "dir", None),
    )
    return jax.shard_map(
        shards,
        mesh=mesh,
        in_specs=placed,
        out_specs=P("region", "dir", None, None),
        check_vma=False,
    )
```

```python
import functools

import jax
import jax.numpy as jnp
from jax import lax
from jax.experimental import pallas as pl
from jax.experimental.pallas import tpu as pltpu
from jax.sharding import PartitionSpec as P

BF16, F32, I32 = jnp.bfloat16, jnp.float32, jnp.int32
NT_DIMS = (((1,), (1,)), ((), ()))
LANES = 128
ROWS = 8
UNROLL = 16
TAIL = 4
GROUP = 8
MIB = 2**20


def pad_to(size, tile):
    return -(-size // tile) * tile


def whole(memory_space):
    return pl.BlockSpec(memory_space=memory_space)


def lookup(parts, hot):
    return lax.dot_general(parts.astype(F32).astype(BF16), hot.astype(BF16), NT_DIMS, preferred_element_type=F32).astype(I32)


def fill_operators(begin, end, list_ref, rows_ref, weighted_ref, rad_ref, out_ref):
    def step(at, wide):
        for u in range(wide):
            place = jnp.minimum(at + u, end - 1)
            row = rows_ref[pl.ds(list_ref[0, place], 1), :].astype(BF16)
            product = weighted_ref[...] * row
            out_ref[place] = jnp.dot(product, rad_ref[...], preferred_element_type=F32).astype(BF16)

    def main_step(i, carry):
        step(begin + i * UNROLL, UNROLL)
        return carry

    def tail_step(i, carry):
        step(begin + main * UNROLL + i * TAIL, TAIL)
        return carry

    count = jnp.maximum(end - begin, 0)
    main = count // UNROLL
    lax.fori_loop(0, main, main_step, 0)
    lax.fori_loop(0, (count - main * UNROLL + TAIL - 1) // TAIL, tail_step, 0)


def first_kernel(
    shared,
    boxes,
    halo,
    region_boxes,
    off_hbm,
    src_hbm,
    tid_hbm,
    table_hbm,
    recv_hbm,
    rad_hbm,
    t_ref,
    weighted_ref,
    rad_ref,
    rows_ref,
    cls_ref,
    listed_ref,
    off_ref,
    src_ref,
    tid_ref,
    table_ref,
    recv_ref,
    list_ref,
    sems,
):
    pairs = [
        (src_hbm, src_ref),
        (tid_hbm, tid_ref),
        (off_hbm, off_ref),
        (recv_hbm, recv_ref),
        (table_hbm, table_ref),
        (rad_hbm, rad_ref),
    ]
    copies = [pltpu.make_async_copy(a, b, sems.at[i]) for i, (a, b) in enumerate(pairs)]
    for copy in copies:
        copy.start()
    classes = table_ref.shape[0]
    directions = recv_ref.shape[1]
    me = lax.axis_index("dir")
    dir_count = region_boxes // boxes
    top = dir_count // 2
    slots = src_ref.shape[2]
    width = cls_ref.shape[1]
    used_width = listed_ref.shape[1]
    ext_at = lax.broadcasted_iota(I32, (width, slots), 0)
    class_at = lax.broadcasted_iota(I32, (used_width, slots), 0)
    row_at = lax.broadcasted_iota(I32, (ROWS, slots), 0)
    out_row = lax.broadcasted_iota(I32, cls_ref.shape, 0)
    seen = jnp.zeros((used_width, slots), F32)
    seen_by_chip = seen
    cls = jnp.full(cls_ref.shape, classes, I32)
    copies[0].wait()
    copies[1].wait()
    for j in range(2 * boxes):
        target = (me if j < boxes else me ^ 1) * boxes + j % boxes
        src = src_ref[0, pl.ds(target, 1), :]
        tid = tid_ref[0, pl.ds(target, 1), :]
        mask = (((src - halo + region_boxes) // boxes) % dir_count) ^ me
        beyond = (src < halo) | (src >= halo + region_boxes)
        late = beyond & ((mask & top) != 0) & ((mask & (top - 2)) != 0)
        even = (mask & 1) == 0
        here = (src >= 0) & ((even | late) if j < boxes else (even & ~late))
        seen = jnp.where((class_at == tid) & here, 1.0, seen)
        seen_by_chip = jnp.where((class_at == tid) & (src >= 0), 1.0, seen_by_chip)
        parts = jnp.where(row_at == 0, tid // 16, jnp.where(row_at == 1, tid % 16, 1))
        found = lookup(parts, jnp.where(ext_at == src, 1.0, 0.0))
        value = jnp.where(found[2:3] > 0, found[0:1] * 16 + found[1:2], classes)
        cls = jnp.where(out_row == j, value, cls)
    cls_ref[...] = cls
    lane = lax.broadcasted_iota(I32, (ROWS, used_width), 1)
    list_row = lax.broadcasted_iota(I32, (ROWS, used_width), 0)
    ones = jnp.ones((ROWS, slots), I32)
    by_chip = jnp.where(lane < shared, jnp.minimum(lookup(ones, seen_by_chip), 1), 0)
    by_core = jnp.where(lane >= shared, jnp.minimum(lookup(ones, seen), 1), 0)
    is_used = jnp.where(list_row == 0, by_chip, by_core)
    down = lax.broadcasted_iota(I32, (used_width, used_width), 0)
    across = lax.broadcasted_iota(I32, (used_width, used_width), 1)
    rank = lookup(is_used, jnp.where(across < down, 1.0, 0.0))
    shared_rank, own_rank = rank[0:1], rank[1:2]
    one_lane = lane[0:1]
    capacity = (shared + 1) // 2
    empty = capacity + classes - shared
    other = (shared_rank ^ me) & 1
    shared_place = shared_rank // 2 + other * (empty + 1)
    place = jnp.where(one_lane < shared, shared_place, capacity + own_rank)
    place = jnp.where(one_lane == classes, empty, place)
    listed_here = jnp.where(one_lane < shared, is_used[0:1] * (1 - other), is_used[1:2])
    here = down == jnp.where(listed_here > 0, place, -1)
    found = lookup(jnp.where(list_row == 0, lane // 16, lane % 16), jnp.where(here, 1.0, 0.0))
    ordered = found[0:1] * 16 + found[1:2]
    count = jnp.sum(is_used.astype(F32), axis=1, keepdims=True).astype(I32)
    first_end = (count[0:1] - (me & 1) + 1) // 2
    ends = jnp.where(one_lane == 0, first_end, capacity + count[1:2])
    listed = jnp.where(list_row == 0, ordered, jnp.where(list_row == 1, place, ends))
    listed_ref[...] = listed
    to_smem = pltpu.make_async_copy(listed_ref, list_ref, sems.at[len(pairs)])
    to_smem.start()
    copies[2].wait()
    position = lax.broadcasted_iota(I32, (1, directions), 1)
    band_size = jnp.ones((1, directions), I32)
    bands = off_ref.shape[0] - 1
    for d in range(bands):
        start, end = off_ref[d], off_ref[d + 1]
        band_size = jnp.where((position >= start) & (position < end), end - start, band_size)
    weight = directions / (bands * band_size.astype(F32))
    copies[3].wait()
    weighted_ref[...] = (recv_ref[...].astype(F32) * weight).astype(BF16)
    copies[4].wait()
    rows_ref[...] = table_ref[...].astype(F32)
    to_smem.wait()
    copies[5].wait()
    fill_operators(0, list_ref[2, 0], list_ref, rows_ref, weighted_ref, rad_ref, t_ref)


def second_kernel(
    near_shift,
    list_ref,
    rows_ref,
    weighted_ref,
    rad_ref,
    near_src_ref,
    near_src_other_ref,
    near_hbm,
    near_other_hbm,
    low_ref,
    t_ref,
    near_ref,
    near_map_ref,
    sems,
):
    boxes, near_slots = near_hbm.shape[1:3]
    copies = []
    for i, array in enumerate((near_hbm, near_other_hbm)):
        for j in range(boxes):
            row = i * boxes + j
            copies.append(
                pltpu.make_async_copy(array.at[0, j], near_ref.at[row, pl.ds(0, near_slots)], sems.at[row])
            )
            copies[-1].start()
    first_count = low_ref.shape[0]
    copies.append(pltpu.make_async_copy(low_ref, t_ref.at[pl.ds(0, first_count)], sems.at[2 * boxes]))
    copies[-1].start()
    t_ref[t_ref.shape[0] - 1] = jnp.zeros(t_ref.shape[1:], BF16)
    for row in range(2 * boxes):
        near_ref[row, near_slots] = jnp.zeros(near_ref.shape[2:], BF16)
    width = near_map_ref.shape[1]
    near_at = lax.broadcasted_iota(I32, (width, near_slots), 0)
    row_at = lax.broadcasted_iota(I32, (ROWS, near_slots), 0)
    lane_at = lax.broadcasted_iota(I32, (ROWS, near_slots), 1)
    out_row = lax.broadcasted_iota(I32, near_map_ref.shape, 0)
    near_map = jnp.full(near_map_ref.shape, near_slots, I32)
    for j in range(2 * boxes):
        near = (near_src_ref if j < boxes else near_src_other_ref)[j % boxes]
        found = lookup(jnp.where(row_at == 0, lane_at, 1), jnp.where((near_at == near + near_shift) & (near >= 0), 1.0, 0.0))
        value = jnp.where(found[1:2] > 0, found[0:1], near_slots)
        near_map = jnp.where(out_row == j, value, near_map)
    near_map_ref[...] = near_map
    fill_operators(first_count, list_ref[2, 1], list_ref, rows_ref, weighted_ref, rad_ref, t_ref)
    for copy in copies:
        copy.wait()


def apply_kernel(
    places, first_row, boxes, halo, with_total, with_other, dtype, cls_ref, near_map_ref, list_ref, t_ref, low_ref, near_ref, *rest
):
    source_refs, rest = rest[: sum(parts for _, _, parts in places)], rest[sum(parts for _, _, parts in places) :]
    if with_total:
        sum_ref, *rest = rest
    if with_other:
        other_ref, *rest = rest
    (out_ref,) = rest
    me = lax.axis_index("dir")
    region_boxes = boxes * lax.axis_size("dir")
    empty = t_ref.shape[0] - 1
    groups = []
    at = 0
    for rim, mask, parts in places:
        owner = me ^ mask
        base = owner * boxes + halo
        if rim:
            base = base + jnp.where(owner * boxes >= halo, -region_boxes, region_boxes)
        groups.append((base, source_refs[at : at + parts]))
        at += parts
    for j in range(boxes):
        row = first_row + j
        total = sum_ref[j] if with_total else None
        if with_other:
            other = other_ref[j].astype(F32)
            total = other if total is None else total + other
        for base, refs in groups:
            blocks = []
            for b in range(boxes):
                n = list_ref[1, cls_ref[row, base + b]]
                here = t_ref[jnp.minimum(n, empty)]
                there = low_ref[jnp.maximum(n - empty - 1, 0)]
                block = jnp.where(n > empty, there, here)
                blocks.append(block + near_ref[row, near_map_ref[row, base + b]])
            values = [ref[...].reshape(-1, ref.shape[-1]) for ref in refs]
            rhs = values[0] if len(values) == 1 else jnp.concatenate(values, 0)
            added = jnp.dot(jnp.concatenate(blocks, 1), rhs, preferred_element_type=F32)
            total = added if total is None else total + added
        if len(out_ref.shape) == 4:
            out_ref[0, j] = total.astype(dtype)
        else:
            out_ref[j] = total.astype(dtype)


def shards(
    currents,
    radiate,
    receive,
    transfer_table,
    near_blocks,
    dir_offsets,
    trans_src,
    trans_tid,
    near_src,
):
    dir_count = lax.axis_size("dir")
    region_count = lax.axis_size("region")
    own = currents[0]
    boxes, unknowns, incidences = own.shape
    near_slots = near_src.shape[2]
    near_src = near_src.reshape(boxes, 1, near_slots)
    region_boxes = boxes * dir_count
    halo = region_boxes // 2
    near_halo = region_boxes // 4
    classes, directions = transfer_table.shape
    shared = classes * 5 // 8
    capacity = (shared + 1) // 2
    top = dir_count // 2
    inner = range(2, top, 2)
    split = boxes // 2
    targets = 2 * boxes

    def partner(array, mask):
        return lax.ppermute(array, "dir", [(i, i ^ mask) for i in range(dir_count)])

    along = []
    for i in range(dir_count):
        for z in range(region_count):
            target = z + 1 if i >= top else z - 1
            if 0 <= target < region_count:
                along.append((i * region_count + z, i * region_count + target))

    def beyond(array):
        return lax.ppermute(array, ("dir", "region"), along)

    def pinned(array):
        return pltpu.with_memory_space_constraint(array, pltpu.VMEM)

    def in_hbm(array):
        return pltpu.with_memory_space_constraint(array, pltpu.HBM)

    width = pad_to(region_boxes + 2 * halo, LANES)
    map_shape = (pad_to(targets, ROWS), width)
    table_shape = (capacity + classes - shared + 1, unknowns, unknowns)
    low_shape = (capacity, unknowns, unknowns)
    list_shape = (ROWS, pad_to(classes + 1, LANES))
    vmem, smem, hbm = whole(pltpu.VMEM), whole(pltpu.SMEM), whole(pltpu.HBM)
    operator_cost = pl.CostEstimate(
        flops=classes * unknowns * unknowns * directions, bytes_accessed=MIB, transcendentals=0
    )

    field = {0: own}
    rim = {}
    for m in inner:
        field[m] = partner(own, m)
    field[top] = partner(own, top)
    rim[0] = beyond(own)
    near_other = partner(near_blocks, 1)
    near_src_other = partner(near_src, 1)
    low, weighted, rad_here, rows, cls, listed = pl.pallas_call(
        functools.partial(first_kernel, shared, boxes, halo, region_boxes),
        in_specs=[hbm] * 6,
        out_specs=[vmem] * 6,
        out_shape=(
            pltpu.VMEM(low_shape, BF16),
            pltpu.VMEM((unknowns, directions), BF16),
            pltpu.VMEM((directions, unknowns), BF16),
            pltpu.VMEM((classes, directions), F32),
            pltpu.VMEM(map_shape, I32),
            pltpu.VMEM(list_shape, I32),
        ),
        scratch_shapes=[
            pltpu.SMEM(dir_offsets.shape, I32),
            pltpu.VMEM(trans_src.shape, I32),
            pltpu.VMEM(trans_tid.shape, I32),
            pltpu.VMEM(transfer_table.shape, BF16),
            pltpu.VMEM(receive.shape, BF16),
            pltpu.SMEM(list_shape, I32),
            pltpu.SemaphoreType.DMA((7,)),
        ],
        compiler_params=pltpu.CompilerParams(vmem_limit_bytes=8 * MIB),
        cost_estimate=operator_cost,
    )(*[in_hbm(a) for a in (dir_offsets, trans_src, trans_tid, transfer_table, receive, radiate)])

    tied = lax.optimization_barrier((low, [field[m] for m in inner], field[top], rim[0]))
    low, inner_fields, field[top], rim[0] = tied
    for m, value in zip(inner, inner_fields):
        field[m] = value
    low_other = partner(low, 1)
    for m in inner:
        field[top + m] = partner(field[top], m)
    rim[top] = partner(rim[0], top)
    for m in inner:
        rim[m] = beyond(field[m])

    table, near_here, near_map = pl.pallas_call(
        functools.partial(second_kernel, halo - near_halo),
        in_specs=[smem] + [vmem] * 5 + [hbm] * 2 + [vmem],
        out_specs=[vmem] * 3,
        out_shape=(
            pltpu.VMEM(table_shape, BF16),
            pltpu.VMEM((targets, near_slots + 1, unknowns, unknowns), BF16),
            pltpu.VMEM(map_shape, I32),
        ),
        scratch_shapes=[pltpu.SemaphoreType.DMA((targets + 1,))],
        compiler_params=pltpu.CompilerParams(vmem_limit_bytes=8 * MIB),
        cost_estimate=operator_cost,
    )(
        listed,
        pinned(rows),
        pinned(weighted),
        pinned(rad_here),
        near_src,
        near_src_other,
        in_hbm(near_blocks),
        near_other,
        pinned(low),
    )

    def apply(places, first_row, total, other, dtype, shape):
        full = (boxes, unknowns, incidences)
        if len(places) > GROUP:
            total = apply(places[:GROUP], first_row, total, None, F32, full)
            return apply(places[GROUP:], first_row, total, other, dtype, shape)
        parts = [part for _, _, group in places for part in group]
        args = [cls, near_map, listed, pinned(table), pinned(low_other), pinned(near_here)] + [pinned(part) for part in parts]
        args += [pinned(extra) for extra in (total, other) if extra is not None]
        specs = [smem] * 3 + [vmem] * (len(args) - 3)
        layout = [(outside, mask, len(group)) for outside, mask, group in places]
        kernel = functools.partial(
            apply_kernel, layout, first_row, boxes, halo, total is not None, other is not None, dtype
        )
        return pl.pallas_call(
            kernel,
            in_specs=specs,
            out_specs=vmem,
            out_shape=pltpu.VMEM(shape, dtype) if len(shape) == 3 else jax.ShapeDtypeStruct(shape, dtype),
            compiler_params=pltpu.CompilerParams(vmem_limit_bytes=12 * MIB),
            cost_estimate=pl.CostEstimate(flops=MIB, bytes_accessed=MIB, transcendentals=0),
        )(*args)

    tied = lax.optimization_barrier(
        (table, [field[top + m] for m in inner], [rim[m] for m in inner], rim[top])
    )
    table, far_fields, inner_rims, rim[top] = tied
    for m, value, other in zip(inner, far_fields, inner_rims):
        field[top + m], rim[m] = value, other
    last = {m: [partner(rim[top][:split], m), partner(rim[m][split:], top)] for m in inner}

    full = (boxes, unknowns, incidences)
    early = [(False, m, [field[m]]) for m in (0, *inner, top)] + [(True, 0, [rim[0]])]
    middle = [(False, top + m, [field[top + m]]) for m in inner]
    middle += [(True, m, [rim[m]]) for m in (*inner, top)]
    for_other = apply(early + middle, boxes, None, None, BF16, full)

    from_other = partner(for_other, 1)
    total = apply(early, 0, None, None, F32, full)

    total, last = lax.optimization_barrier((total, last))
    turned = {m: [partner(part, 1) for part in last[m]] for m in inner}
    total = apply(middle, 0, total, from_other, F32, full)
    late = [(True, top + m, last[m]) for m in inner] + [(True, top + m + 1, turned[m]) for m in inner]
    return apply(late, 0, total, None, BF16, currents.shape)


def solution(mesh):
    placed = (
        P("region", "dir", None, None),
        P(),
        P(),
        P(),
        P("region", "dir", None, None, None),
        P(),
        P("region", None, None),
        P("region", None, None),
        P("region", "dir", None),
    )
    return jax.shard_map(
        shards,
        mesh=mesh,
        in_specs=placed,
        out_specs=P("region", "dir", None, None),
        check_vma=False,
    )
```

```python
import functools

import jax
import jax.numpy as jnp
from jax import lax
from jax.experimental import pallas as pl
from jax.experimental.pallas import tpu as pltpu
from jax.sharding import PartitionSpec as P

BF16, F32, I32 = jnp.bfloat16, jnp.float32, jnp.int32
NT_DIMS = (((1,), (1,)), ((), ()))
LANES = 128
ROWS = 8
UNROLL = 16
TAIL = 4
GROUP = 8
MIB = 2**20


def pad_to(size, tile):
    return -(-size // tile) * tile


def whole(memory_space):
    return pl.BlockSpec(memory_space=memory_space)


def lookup(parts, hot):
    return lax.dot_general(parts.astype(F32).astype(BF16), hot.astype(BF16), NT_DIMS, preferred_element_type=F32).astype(I32)


def fill_operators(begin, end, list_ref, rows_ref, weighted_ref, rad_ref, out_ref):
    def step(at, wide):
        for u in range(wide):
            place = jnp.minimum(at + u, end - 1)
            row = rows_ref[pl.ds(list_ref[0, place], 1), :].astype(BF16)
            product = weighted_ref[...] * row
            out_ref[place] = jnp.dot(product, rad_ref[...], preferred_element_type=F32).astype(BF16)

    def main_step(i, carry):
        step(begin + i * UNROLL, UNROLL)
        return carry

    def tail_step(i, carry):
        step(begin + main * UNROLL + i * TAIL, TAIL)
        return carry

    count = jnp.maximum(end - begin, 0)
    main = count // UNROLL
    lax.fori_loop(0, main, main_step, 0)
    lax.fori_loop(0, (count - main * UNROLL + TAIL - 1) // TAIL, tail_step, 0)


def first_kernel(
    first_count,
    boxes,
    halo,
    region_boxes,
    off_hbm,
    src_hbm,
    tid_hbm,
    table_hbm,
    recv_hbm,
    rad_hbm,
    t_ref,
    weighted_ref,
    rad_ref,
    rows_ref,
    cls_ref,
    listed_ref,
    off_ref,
    src_ref,
    tid_ref,
    table_ref,
    recv_ref,
    list_ref,
    sems,
):
    pairs = [
        (src_hbm, src_ref),
        (tid_hbm, tid_ref),
        (off_hbm, off_ref),
        (recv_hbm, recv_ref),
        (table_hbm, table_ref),
        (rad_hbm, rad_ref),
    ]
    copies = [pltpu.make_async_copy(a, b, sems.at[i]) for i, (a, b) in enumerate(pairs)]
    for copy in copies:
        copy.start()
    classes = table_ref.shape[0]
    directions = recv_ref.shape[1]
    me = lax.axis_index("dir")
    dir_count = region_boxes // boxes
    top = dir_count // 2
    slots = src_ref.shape[2]
    width = cls_ref.shape[1]
    used_width = listed_ref.shape[1]
    ext_at = lax.broadcasted_iota(I32, (width, slots), 0)
    class_at = lax.broadcasted_iota(I32, (used_width, slots), 0)
    row_at = lax.broadcasted_iota(I32, (ROWS, slots), 0)
    out_row = lax.broadcasted_iota(I32, cls_ref.shape, 0)
    seen = jnp.zeros((used_width, slots), F32)
    cls = jnp.full(cls_ref.shape, classes, I32)
    copies[0].wait()
    copies[1].wait()
    for j in range(2 * boxes):
        target = (me if j < boxes else me ^ 1) * boxes + j % boxes
        src = src_ref[0, pl.ds(target, 1), :]
        tid = tid_ref[0, pl.ds(target, 1), :]
        mask = (((src - halo + region_boxes) // boxes) % dir_count) ^ me
        beyond = (src < halo) | (src >= halo + region_boxes)
        late = beyond & ((mask & top) != 0) & ((mask & (top - 2)) != 0)
        even = (mask & 1) == 0
        here = (src >= 0) & ((even | late) if j < boxes else (even & ~late))
        seen = jnp.where((class_at == tid) & here, 1.0, seen)
        parts = jnp.where(row_at == 0, tid // 16, jnp.where(row_at == 1, tid % 16, 1))
        found = lookup(parts, jnp.where(ext_at == src, 1.0, 0.0))
        value = jnp.where(found[2:3] > 0, found[0:1] * 16 + found[1:2], classes)
        cls = jnp.where(out_row == j, value, cls)
    cls_ref[...] = cls
    is_used = jnp.minimum(lookup(jnp.ones((ROWS, slots), I32), seen), 1)
    down = lax.broadcasted_iota(I32, (used_width, used_width), 0)
    across = lax.broadcasted_iota(I32, (used_width, used_width), 1)
    rank = lookup(is_used, jnp.where(across < down, 1.0, 0.0))
    here = (down == rank[0:1]) & (is_used[0:1] > 0)
    lane = lax.broadcasted_iota(I32, (ROWS, used_width), 1)
    list_row = lax.broadcasted_iota(I32, (ROWS, used_width), 0)
    found = lookup(jnp.where(list_row == 0, lane // 16, lane % 16), jnp.where(here, 1.0, 0.0))
    ordered = found[0:1] * 16 + found[1:2]
    rank = jnp.where(lane == classes, classes, rank)
    count = jnp.sum(is_used[0:1].astype(F32), axis=1, keepdims=True).astype(I32)
    listed = jnp.where(list_row == 0, ordered, jnp.where(list_row == 1, rank, count))
    listed_ref[...] = listed
    to_smem = pltpu.make_async_copy(listed_ref, list_ref, sems.at[len(pairs)])
    to_smem.start()
    copies[2].wait()
    position = lax.broadcasted_iota(I32, (1, directions), 1)
    band_size = jnp.ones((1, directions), I32)
    bands = off_ref.shape[0] - 1
    for d in range(bands):
        start, end = off_ref[d], off_ref[d + 1]
        band_size = jnp.where((position >= start) & (position < end), end - start, band_size)
    weight = directions / (bands * band_size.astype(F32))
    copies[3].wait()
    weighted_ref[...] = (recv_ref[...].astype(F32) * weight).astype(BF16)
    copies[4].wait()
    rows_ref[...] = table_ref[...].astype(F32)
    to_smem.wait()
    count = list_ref[2, 0]
    copies[5].wait()
    fill_operators(0, jnp.minimum(count, first_count), list_ref, rows_ref, weighted_ref, rad_ref, t_ref)


def second_kernel(
    near_shift,
    list_ref,
    rows_ref,
    weighted_ref,
    rad_ref,
    near_src_ref,
    near_src_other_ref,
    near_hbm,
    near_other_hbm,
    low_ref,
    t_ref,
    near_ref,
    near_map_ref,
    sems,
):
    boxes, near_slots = near_hbm.shape[1:3]
    copies = []
    for i, array in enumerate((near_hbm, near_other_hbm)):
        for j in range(boxes):
            row = i * boxes + j
            copies.append(
                pltpu.make_async_copy(array.at[0, j], near_ref.at[row, pl.ds(0, near_slots)], sems.at[row])
            )
            copies[-1].start()
    first_count = low_ref.shape[0]
    copies.append(pltpu.make_async_copy(low_ref, t_ref.at[pl.ds(0, first_count)], sems.at[2 * boxes]))
    copies[-1].start()
    t_ref[t_ref.shape[0] - 1] = jnp.zeros(t_ref.shape[1:], BF16)
    for row in range(2 * boxes):
        near_ref[row, near_slots] = jnp.zeros(near_ref.shape[2:], BF16)
    width = near_map_ref.shape[1]
    near_at = lax.broadcasted_iota(I32, (width, near_slots), 0)
    row_at = lax.broadcasted_iota(I32, (ROWS, near_slots), 0)
    lane_at = lax.broadcasted_iota(I32, (ROWS, near_slots), 1)
    out_row = lax.broadcasted_iota(I32, near_map_ref.shape, 0)
    near_map = jnp.full(near_map_ref.shape, near_slots, I32)
    for j in range(2 * boxes):
        near = (near_src_ref if j < boxes else near_src_other_ref)[j % boxes]
        found = lookup(jnp.where(row_at == 0, lane_at, 1), jnp.where((near_at == near + near_shift) & (near >= 0), 1.0, 0.0))
        value = jnp.where(found[1:2] > 0, found[0:1], near_slots)
        near_map = jnp.where(out_row == j, value, near_map)
    near_map_ref[...] = near_map
    fill_operators(first_count, list_ref[2, 0], list_ref, rows_ref, weighted_ref, rad_ref, t_ref)
    for copy in copies:
        copy.wait()


def apply_kernel(
    places, first_row, boxes, halo, with_total, with_other, dtype, cls_ref, near_map_ref, list_ref, t_ref, near_ref, *rest
):
    source_refs, rest = rest[: sum(parts for _, _, parts in places)], rest[sum(parts for _, _, parts in places) :]
    if with_total:
        sum_ref, *rest = rest
    if with_other:
        other_ref, *rest = rest
    (out_ref,) = rest
    me = lax.axis_index("dir")
    region_boxes = boxes * lax.axis_size("dir")
    groups = []
    at = 0
    for rim, mask, parts in places:
        owner = me ^ mask
        base = owner * boxes + halo
        if rim:
            base = base + jnp.where(owner * boxes >= halo, -region_boxes, region_boxes)
        groups.append((base, source_refs[at : at + parts]))
        at += parts
    for j in range(boxes):
        row = first_row + j
        total = sum_ref[j] if with_total else None
        if with_other:
            other = other_ref[j].astype(F32)
            total = other if total is None else total + other
        for base, refs in groups:
            blocks = []
            for b in range(boxes):
                n = list_ref[1, cls_ref[row, base + b]]
                blocks.append(t_ref[n] + near_ref[row, near_map_ref[row, base + b]])
            values = [ref[...].reshape(-1, ref.shape[-1]) for ref in refs]
            rhs = values[0] if len(values) == 1 else jnp.concatenate(values, 0)
            added = jnp.dot(jnp.concatenate(blocks, 1), rhs, preferred_element_type=F32)
            total = added if total is None else total + added
        if len(out_ref.shape) == 4:
            out_ref[0, j] = total.astype(dtype)
        else:
            out_ref[j] = total.astype(dtype)


def shards(
    currents,
    radiate,
    receive,
    transfer_table,
    near_blocks,
    dir_offsets,
    trans_src,
    trans_tid,
    near_src,
):
    dir_count = lax.axis_size("dir")
    region_count = lax.axis_size("region")
    own = currents[0]
    boxes, unknowns, incidences = own.shape
    near_slots = near_src.shape[2]
    near_src = near_src.reshape(boxes, 1, near_slots)
    region_boxes = boxes * dir_count
    halo = region_boxes // 2
    near_halo = region_boxes // 4
    classes, directions = transfer_table.shape
    first_count = pad_to(classes // 4, UNROLL)
    top = dir_count // 2
    inner = range(2, top, 2)
    targets = 2 * boxes

    def partner(array, mask):
        return lax.ppermute(array, "dir", [(i, i ^ mask) for i in range(dir_count)])

    along = []
    for i in range(dir_count):
        for z in range(region_count):
            target = z + 1 if i >= top else z - 1
            if 0 <= target < region_count:
                along.append((i * region_count + z, i * region_count + target))

    def beyond(array):
        return lax.ppermute(array, ("dir", "region"), along)

    def pinned(array):
        return pltpu.with_memory_space_constraint(array, pltpu.VMEM)

    def in_hbm(array):
        return pltpu.with_memory_space_constraint(array, pltpu.HBM)

    width = pad_to(region_boxes + 2 * halo, LANES)
    map_shape = (pad_to(targets, ROWS), width)
    table_shape = (classes + 1, unknowns, unknowns)
    low_shape = (first_count, unknowns, unknowns)
    list_shape = (ROWS, pad_to(classes + 1, LANES))
    vmem, smem, hbm = whole(pltpu.VMEM), whole(pltpu.SMEM), whole(pltpu.HBM)
    operator_cost = pl.CostEstimate(
        flops=classes * unknowns * unknowns * directions, bytes_accessed=MIB, transcendentals=0
    )

    field = {0: own}
    rim = {}
    for m in inner:
        field[m] = partner(own, m)
    field[top] = partner(own, top)
    rim[0] = beyond(own)
    near_other = partner(near_blocks, 1)
    near_src_other = partner(near_src, 1)
    low, weighted, rad_here, rows, cls, listed = pl.pallas_call(
        functools.partial(first_kernel, first_count, boxes, halo, region_boxes),
        in_specs=[hbm] * 6,
        out_specs=[vmem] * 6,
        out_shape=(
            pltpu.VMEM(low_shape, BF16),
            pltpu.VMEM((unknowns, directions), BF16),
            pltpu.VMEM((directions, unknowns), BF16),
            pltpu.VMEM((classes, directions), F32),
            pltpu.VMEM(map_shape, I32),
            pltpu.VMEM(list_shape, I32),
        ),
        scratch_shapes=[
            pltpu.SMEM(dir_offsets.shape, I32),
            pltpu.VMEM(trans_src.shape, I32),
            pltpu.VMEM(trans_tid.shape, I32),
            pltpu.VMEM(transfer_table.shape, BF16),
            pltpu.VMEM(receive.shape, BF16),
            pltpu.SMEM(list_shape, I32),
            pltpu.SemaphoreType.DMA((7,)),
        ],
        compiler_params=pltpu.CompilerParams(vmem_limit_bytes=8 * MIB),
        cost_estimate=operator_cost,
    )(*[in_hbm(a) for a in (dir_offsets, trans_src, trans_tid, transfer_table, receive, radiate)])

    tied = lax.optimization_barrier((low, [field[m] for m in inner], field[top], rim[0]))
    low, inner_fields, field[top], rim[0] = tied
    for m, value in zip(inner, inner_fields):
        field[m] = value
    for m in inner:
        field[top + m] = partner(field[top], m)
    rim[top] = partner(rim[0], top)
    for m in inner:
        rim[m] = beyond(field[m])
    rim[0], near_other = lax.optimization_barrier((rim[0], near_other))
    for m in inner:
        rim[top + m] = partner(rim[0], top + m)

    table, near_here, near_map = pl.pallas_call(
        functools.partial(second_kernel, halo - near_halo),
        in_specs=[smem] + [vmem] * 5 + [hbm] * 2 + [vmem],
        out_specs=[vmem] * 3,
        out_shape=(
            pltpu.VMEM(table_shape, BF16),
            pltpu.VMEM((targets, near_slots + 1, unknowns, unknowns), BF16),
            pltpu.VMEM(map_shape, I32),
        ),
        scratch_shapes=[pltpu.SemaphoreType.DMA((targets + 1,))],
        compiler_params=pltpu.CompilerParams(vmem_limit_bytes=8 * MIB),
        cost_estimate=operator_cost,
    )(
        listed,
        pinned(rows),
        pinned(weighted),
        pinned(rad_here),
        near_src,
        near_src_other,
        in_hbm(near_blocks),
        near_other,
        pinned(low),
    )

    def apply(places, first_row, total, other, dtype, shape):
        full = (boxes, unknowns, incidences)
        if len(places) > GROUP:
            total = apply(places[:GROUP], first_row, total, None, F32, full)
            return apply(places[GROUP:], first_row, total, other, dtype, shape)
        parts = [part for _, _, group in places for part in group]
        args = [cls, near_map, listed, pinned(table), pinned(near_here)] + [pinned(part) for part in parts]
        args += [pinned(extra) for extra in (total, other) if extra is not None]
        specs = [smem] * 3 + [vmem] * (len(args) - 3)
        layout = [(outside, mask, len(group)) for outside, mask, group in places]
        kernel = functools.partial(
            apply_kernel, layout, first_row, boxes, halo, total is not None, other is not None, dtype
        )
        return pl.pallas_call(
            kernel,
            in_specs=specs,
            out_specs=vmem,
            out_shape=pltpu.VMEM(shape, dtype) if len(shape) == 3 else jax.ShapeDtypeStruct(shape, dtype),
            compiler_params=pltpu.CompilerParams(vmem_limit_bytes=12 * MIB),
            cost_estimate=pl.CostEstimate(flops=MIB, bytes_accessed=MIB, transcendentals=0),
        )(*args)

    full = (boxes, unknowns, incidences)
    early = [(False, m, [field[m]]) for m in (0, *inner, top)] + [(True, 0, [rim[0]])]
    middle = [(False, top + m, [field[top + m]]) for m in inner]
    middle += [(True, m, [rim[m]]) for m in (*inner, top)]
    for_other = apply(early + middle, boxes, None, None, BF16, full)

    from_other = partner(for_other, 1)
    total = apply(early, 0, None, None, F32, full)

    total, last = lax.optimization_barrier((total, [rim[top + m] for m in inner]))
    turned = [partner(part, 1) for part in last]
    total = apply(middle, 0, total, from_other, F32, full)
    late = [(True, top + m, [part]) for m, part in zip(inner, last)]
    late += [(True, top + m + 1, [part]) for m, part in zip(inner, turned)]
    return apply(late, 0, total, None, BF16, currents.shape)


def solution(mesh):
    placed = (
        P("region", "dir", None, None),
        P(),
        P(),
        P(),
        P("region", "dir", None, None, None),
        P(),
        P("region", None, None),
        P("region", None, None),
        P("region", "dir", None),
    )
    return jax.shard_map(
        shards,
        mesh=mesh,
        in_specs=placed,
        out_specs=P("region", "dir", None, None),
        check_vma=False,
    )
```

```python
import functools

import jax
import jax.numpy as jnp
from jax import lax
from jax.experimental import pallas as pl
from jax.experimental.pallas import tpu as pltpu
from jax.sharding import PartitionSpec as P

BF16, F32, I32 = jnp.bfloat16, jnp.float32, jnp.int32
NT_DIMS = (((1,), (1,)), ((), ()))
LANES = 128
ROWS = 8
UNROLL = 16
TAIL = 4
GROUP = 8
MIB = 2**20


def pad_to(size, tile):
    return -(-size // tile) * tile


def whole(memory_space):
    return pl.BlockSpec(memory_space=memory_space)


def lookup(parts, hot):
    return lax.dot_general(parts.astype(F32).astype(BF16), hot.astype(BF16), NT_DIMS, preferred_element_type=F32).astype(I32)


def fill_operators(begin, end, list_ref, rows_ref, weighted_ref, rad_ref, out_ref):
    def step(at, wide):
        for u in range(wide):
            place = jnp.minimum(at + u, end - 1)
            row = rows_ref[pl.ds(list_ref[0, place], 1), :].astype(BF16)
            product = weighted_ref[...] * row
            out_ref[place] = jnp.dot(product, rad_ref[...], preferred_element_type=F32).astype(BF16)

    def main_step(i, carry):
        step(begin + i * UNROLL, UNROLL)
        return carry

    def tail_step(i, carry):
        step(begin + main * UNROLL + i * TAIL, TAIL)
        return carry

    count = jnp.maximum(end - begin, 0)
    main = count // UNROLL
    lax.fori_loop(0, main, main_step, 0)
    lax.fori_loop(0, (count - main * UNROLL + TAIL - 1) // TAIL, tail_step, 0)


def first_kernel(
    first_count,
    boxes,
    halo,
    region_boxes,
    off_hbm,
    src_hbm,
    tid_hbm,
    table_hbm,
    recv_hbm,
    rad_hbm,
    t_ref,
    weighted_ref,
    rad_ref,
    rows_ref,
    cls_ref,
    listed_ref,
    off_ref,
    src_ref,
    tid_ref,
    table_ref,
    recv_ref,
    list_ref,
    sems,
):
    pairs = [
        (src_hbm, src_ref),
        (tid_hbm, tid_ref),
        (off_hbm, off_ref),
        (recv_hbm, recv_ref),
        (table_hbm, table_ref),
        (rad_hbm, rad_ref),
    ]
    copies = [pltpu.make_async_copy(a, b, sems.at[i]) for i, (a, b) in enumerate(pairs)]
    for copy in copies:
        copy.start()
    classes = table_ref.shape[0]
    directions = recv_ref.shape[1]
    me = lax.axis_index("dir")
    dir_count = region_boxes // boxes
    top = dir_count // 2
    slots = src_ref.shape[2]
    width = cls_ref.shape[1]
    used_width = listed_ref.shape[1]
    ext_at = lax.broadcasted_iota(I32, (width, slots), 0)
    class_at = lax.broadcasted_iota(I32, (used_width, slots), 0)
    row_at = lax.broadcasted_iota(I32, (ROWS, slots), 0)
    out_row = lax.broadcasted_iota(I32, cls_ref.shape, 0)
    seen = jnp.zeros((used_width, slots), F32)
    cls = jnp.full(cls_ref.shape, classes, I32)
    copies[0].wait()
    copies[1].wait()
    for j in range(2 * boxes):
        target = (me if j < boxes else me ^ 1) * boxes + j % boxes
        src = src_ref[0, pl.ds(target, 1), :]
        tid = tid_ref[0, pl.ds(target, 1), :]
        mask = (((src - halo + region_boxes) // boxes) % dir_count) ^ me
        beyond = (src < halo) | (src >= halo + region_boxes)
        late = beyond & ((mask & top) != 0) & ((mask & (top - 2)) != 0)
        even = (mask & 1) == 0
        here = (src >= 0) & ((even | late) if j < boxes else (even & ~late))
        seen = jnp.where((class_at == tid) & here, 1.0, seen)
        parts = jnp.where(row_at == 0, tid // 16, jnp.where(row_at == 1, tid % 16, 1))
        found = lookup(parts, jnp.where(ext_at == src, 1.0, 0.0))
        value = jnp.where(found[2:3] > 0, found[0:1] * 16 + found[1:2], classes)
        cls = jnp.where(out_row == j, value, cls)
    cls_ref[...] = cls
    is_used = jnp.minimum(lookup(jnp.ones((ROWS, slots), I32), seen), 1)
    down = lax.broadcasted_iota(I32, (used_width, used_width), 0)
    across = lax.broadcasted_iota(I32, (used_width, used_width), 1)
    rank = lookup(is_used, jnp.where(across < down, 1.0, 0.0))
    here = (down == rank[0:1]) & (is_used[0:1] > 0)
    lane = lax.broadcasted_iota(I32, (ROWS, used_width), 1)
    list_row = lax.broadcasted_iota(I32, (ROWS, used_width), 0)
    found = lookup(jnp.where(list_row == 0, lane // 16, lane % 16), jnp.where(here, 1.0, 0.0))
    ordered = found[0:1] * 16 + found[1:2]
    rank = jnp.where(lane == classes, classes, rank)
    count = jnp.sum(is_used[0:1].astype(F32), axis=1, keepdims=True).astype(I32)
    listed = jnp.where(list_row == 0, ordered, jnp.where(list_row == 1, rank, count))
    listed_ref[...] = listed
    to_smem = pltpu.make_async_copy(listed_ref, list_ref, sems.at[len(pairs)])
    to_smem.start()
    copies[2].wait()
    position = lax.broadcasted_iota(I32, (1, directions), 1)
    band_size = jnp.ones((1, directions), I32)
    bands = off_ref.shape[0] - 1
    for d in range(bands):
        start, end = off_ref[d], off_ref[d + 1]
        band_size = jnp.where((position >= start) & (position < end), end - start, band_size)
    weight = directions / (bands * band_size.astype(F32))
    copies[3].wait()
    weighted_ref[...] = (recv_ref[...].astype(F32) * weight).astype(BF16)
    copies[4].wait()
    rows_ref[...] = table_ref[...].astype(F32)
    to_smem.wait()
    count = list_ref[2, 0]
    copies[5].wait()
    fill_operators(0, jnp.minimum(count, first_count), list_ref, rows_ref, weighted_ref, rad_ref, t_ref)


def second_kernel(
    second_end,
    near_shift,
    list_ref,
    rows_ref,
    weighted_ref,
    rad_ref,
    near_src_ref,
    near_src_other_ref,
    near_hbm,
    near_other_hbm,
    low_ref,
    t_ref,
    near_ref,
    near_map_ref,
    sems,
):
    boxes, near_slots = near_hbm.shape[1:3]
    copies = []
    for i, array in enumerate((near_hbm, near_other_hbm)):
        for j in range(boxes):
            row = i * boxes + j
            copies.append(
                pltpu.make_async_copy(array.at[0, j], near_ref.at[row, pl.ds(0, near_slots)], sems.at[row])
            )
            copies[-1].start()
    first_count = low_ref.shape[0]
    copies.append(pltpu.make_async_copy(low_ref, t_ref.at[pl.ds(0, first_count)], sems.at[2 * boxes]))
    copies[-1].start()
    t_ref[t_ref.shape[0] - 1] = jnp.zeros(t_ref.shape[1:], BF16)
    for row in range(2 * boxes):
        near_ref[row, near_slots] = jnp.zeros(near_ref.shape[2:], BF16)
    width = near_map_ref.shape[1]
    near_at = lax.broadcasted_iota(I32, (width, near_slots), 0)
    row_at = lax.broadcasted_iota(I32, (ROWS, near_slots), 0)
    lane_at = lax.broadcasted_iota(I32, (ROWS, near_slots), 1)
    out_row = lax.broadcasted_iota(I32, near_map_ref.shape, 0)
    near_map = jnp.full(near_map_ref.shape, near_slots, I32)
    for j in range(2 * boxes):
        near = (near_src_ref if j < boxes else near_src_other_ref)[j % boxes]
        found = lookup(jnp.where(row_at == 0, lane_at, 1), jnp.where((near_at == near + near_shift) & (near >= 0), 1.0, 0.0))
        value = jnp.where(found[1:2] > 0, found[0:1], near_slots)
        near_map = jnp.where(out_row == j, value, near_map)
    near_map_ref[...] = near_map
    end = jnp.minimum(list_ref[2, 0], second_end)
    fill_operators(first_count, end, list_ref, rows_ref, weighted_ref, rad_ref, t_ref)
    for copy in copies:
        copy.wait()


def add_products(places, first_row, boxes, halo, cls_ref, near_map_ref, list_ref, t_ref, near_ref, source_refs, start, store):
    me = lax.axis_index("dir")
    region_boxes = boxes * lax.axis_size("dir")
    bases, groups, at = [], [], 0
    for rim, mask, parts in places:
        groups.append(source_refs[at : at + parts])
        at += parts
        owner = me ^ mask
        base = owner * boxes + halo
        if rim:
            base = base + jnp.where(owner * boxes >= halo, -region_boxes, region_boxes)
        bases.append(base)
    for j in range(boxes):
        row = first_row + j
        total = start(j)
        for base, refs in zip(bases, groups):
            blocks = []
            for b in range(boxes):
                n = list_ref[1, cls_ref[row, base + b]]
                blocks.append(t_ref[n] + near_ref[row, near_map_ref[row, base + b]])
            values = [ref[...].reshape(-1, ref.shape[-1]) for ref in refs]
            rhs = values[0] if len(values) == 1 else jnp.concatenate(values, 0)
            added = jnp.dot(jnp.concatenate(blocks, 1), rhs, preferred_element_type=F32)
            total = added if total is None else total + added
        store(j, total)


def third_kernel(
    second_end,
    places,
    early,
    boxes,
    halo,
    list_ref,
    cls_ref,
    near_map_ref,
    rows_ref,
    weighted_ref,
    rad_ref,
    near_ref,
    *rest,
):
    source_count = sum(parts for _, _, parts in places)
    source_refs, (_, t_ref, other_ref, own_ref) = rest[:source_count], rest[source_count:]
    fill_operators(second_end, list_ref[2, 0], list_ref, rows_ref, weighted_ref, rad_ref, t_ref)

    def store_other(j, total):
        other_ref[j] = total.astype(other_ref.dtype)

    def store_own(j, total):
        own_ref[j] = total

    refs = (cls_ref, near_map_ref, list_ref, t_ref, near_ref)
    add_products(places, boxes, boxes, halo, *refs, source_refs, lambda j: None, store_other)
    add_products(places[:early], 0, boxes, halo, *refs, source_refs, lambda j: None, store_own)


def apply_kernel(
    places, first_row, boxes, halo, with_total, with_other, cls_ref, near_map_ref, list_ref, t_ref, near_ref, *rest
):
    source_count = sum(parts for _, _, parts in places)
    source_refs, rest = rest[:source_count], rest[source_count:]
    if with_total:
        sum_ref, *rest = rest
    if with_other:
        other_ref, *rest = rest
    (out_ref,) = rest

    def start(j):
        total = sum_ref[j] if with_total else None
        if with_other:
            other = other_ref[j].astype(F32)
            total = other if total is None else total + other
        return total

    def store(j, total):
        if len(out_ref.shape) == 4:
            out_ref[0, j] = total.astype(out_ref.dtype)
        else:
            out_ref[j] = total.astype(out_ref.dtype)

    refs = (cls_ref, near_map_ref, list_ref, t_ref, near_ref)
    add_products(places, first_row, boxes, halo, *refs, source_refs, start, store)


def shards(
    currents,
    radiate,
    receive,
    transfer_table,
    near_blocks,
    dir_offsets,
    trans_src,
    trans_tid,
    near_src,
):
    dir_count = lax.axis_size("dir")
    region_count = lax.axis_size("region")
    own = currents[0]
    boxes, unknowns, incidences = own.shape
    near_slots = near_src.shape[2]
    near_src = near_src.reshape(boxes, 1, near_slots)
    region_boxes = boxes * dir_count
    halo = region_boxes // 2
    near_halo = region_boxes // 4
    classes, directions = transfer_table.shape
    first_count = pad_to(classes // 4, UNROLL)
    second_end = first_count + pad_to(classes // 5, UNROLL)
    top = dir_count // 2
    inner = range(2, top, 2)
    split = boxes // 2
    targets = 2 * boxes

    def partner(array, mask):
        return lax.ppermute(array, "dir", [(i, i ^ mask) for i in range(dir_count)])

    along = []
    for i in range(dir_count):
        for z in range(region_count):
            target = z + 1 if i >= top else z - 1
            if 0 <= target < region_count:
                along.append((i * region_count + z, i * region_count + target))

    def beyond(array):
        return lax.ppermute(array, ("dir", "region"), along)

    def pinned(array):
        return pltpu.with_memory_space_constraint(array, pltpu.VMEM)

    def in_hbm(array):
        return pltpu.with_memory_space_constraint(array, pltpu.HBM)

    width = pad_to(region_boxes + 2 * halo, LANES)
    map_shape = (pad_to(targets, ROWS), width)
    table_shape = (classes + 1, unknowns, unknowns)
    low_shape = (first_count, unknowns, unknowns)
    list_shape = (ROWS, pad_to(classes + 1, LANES))
    vmem, smem, hbm = whole(pltpu.VMEM), whole(pltpu.SMEM), whole(pltpu.HBM)
    operator_cost = pl.CostEstimate(
        flops=classes * unknowns * unknowns * directions, bytes_accessed=MIB, transcendentals=0
    )

    field = {0: own}
    rim = {}
    for m in inner:
        field[m] = partner(own, m)
    field[top] = partner(own, top)
    rim[0] = beyond(own)
    near_other = partner(near_blocks, 1)
    near_src_other = partner(near_src, 1)
    low, weighted, rad_here, rows, cls, listed = pl.pallas_call(
        functools.partial(first_kernel, first_count, boxes, halo, region_boxes),
        in_specs=[hbm] * 6,
        out_specs=[vmem] * 6,
        out_shape=(
            pltpu.VMEM(low_shape, BF16),
            pltpu.VMEM((unknowns, directions), BF16),
            pltpu.VMEM((directions, unknowns), BF16),
            pltpu.VMEM((classes, directions), F32),
            pltpu.VMEM(map_shape, I32),
            pltpu.VMEM(list_shape, I32),
        ),
        scratch_shapes=[
            pltpu.SMEM(dir_offsets.shape, I32),
            pltpu.VMEM(trans_src.shape, I32),
            pltpu.VMEM(trans_tid.shape, I32),
            pltpu.VMEM(transfer_table.shape, BF16),
            pltpu.VMEM(receive.shape, BF16),
            pltpu.SMEM(list_shape, I32),
            pltpu.SemaphoreType.DMA((7,)),
        ],
        compiler_params=pltpu.CompilerParams(vmem_limit_bytes=8 * MIB),
        cost_estimate=operator_cost,
    )(*[in_hbm(a) for a in (dir_offsets, trans_src, trans_tid, transfer_table, receive, radiate)])

    tied = lax.optimization_barrier((low, [field[m] for m in inner], field[top], rim[0]))
    low, inner_fields, field[top], rim[0] = tied
    for m, value in zip(inner, inner_fields):
        field[m] = value
    for m in inner:
        field[top + m] = partner(field[top], m)
    rim[top] = partner(rim[0], top)
    for m in inner:
        rim[m] = beyond(field[m])

    table, near_here, near_map = pl.pallas_call(
        functools.partial(second_kernel, second_end, halo - near_halo),
        in_specs=[smem] + [vmem] * 5 + [hbm] * 2 + [vmem],
        out_specs=[vmem] * 3,
        out_shape=(
            pltpu.VMEM(table_shape, BF16),
            pltpu.VMEM((targets, near_slots + 1, unknowns, unknowns), BF16),
            pltpu.VMEM(map_shape, I32),
        ),
        scratch_shapes=[pltpu.SemaphoreType.DMA((targets + 1,))],
        compiler_params=pltpu.CompilerParams(vmem_limit_bytes=8 * MIB),
        cost_estimate=operator_cost,
    )(
        listed,
        pinned(rows),
        pinned(weighted),
        pinned(rad_here),
        near_src,
        near_src_other,
        in_hbm(near_blocks),
        near_other,
        pinned(low),
    )

    def apply(places, first_row, total, other, dtype, shape):
        if len(places) > GROUP:
            total = apply(places[:GROUP], first_row, total, None, F32, full)
            return apply(places[GROUP:], first_row, total, other, dtype, shape)
        args = [cls, near_map, listed, pinned(table), pinned(near_here)] + [pinned(part) for _, _, parts in places for part in parts]
        args += [pinned(extra) for extra in (total, other) if extra is not None]
        specs = [smem] * 3 + [vmem] * (len(args) - 3)
        layout = [(outside, mask, len(parts)) for outside, mask, parts in places]
        kernel = functools.partial(
            apply_kernel, layout, first_row, boxes, halo, total is not None, other is not None
        )
        return pl.pallas_call(
            kernel,
            in_specs=specs,
            out_specs=vmem,
            out_shape=pltpu.VMEM(shape, dtype) if len(shape) == 3 else jax.ShapeDtypeStruct(shape, dtype),
            compiler_params=pltpu.CompilerParams(vmem_limit_bytes=12 * MIB),
            cost_estimate=pl.CostEstimate(flops=MIB, bytes_accessed=MIB, transcendentals=0),
        )(*args)

    tied = lax.optimization_barrier(
        (table, [field[top + m] for m in inner], [rim[m] for m in inner], rim[top])
    )
    table, far_fields, inner_rims, rim[top] = tied
    for m, value, other in zip(inner, far_fields, inner_rims):
        field[top + m], rim[m] = value, other
    last = {m: [partner(rim[top][:split], m), partner(rim[m][split:], top)] for m in inner}

    full = (boxes, unknowns, incidences)
    early = [(False, m, [field[m]]) for m in (0, *inner, top)] + [(True, 0, [rim[0]])]
    middle = [(False, top + m, [field[top + m]]) for m in inner]
    middle += [(True, m, [rim[m]]) for m in (*inner, top)]
    ready = (early + middle)[:GROUP]
    left = (early + middle)[GROUP:]
    count = min(len(early), GROUP)
    table, for_other, total = pl.pallas_call(
        functools.partial(
            third_kernel, second_end, [(outside, mask, 1) for outside, mask, _ in ready], count, boxes, halo
        ),
        in_specs=[smem] * 3 + [vmem] * (5 + len(ready)),
        out_specs=[vmem] * 3,
        out_shape=(
            pltpu.VMEM(table_shape, BF16),
            pltpu.VMEM(full, F32 if left else BF16),
            pltpu.VMEM(full, F32),
        ),
        input_output_aliases={7 + len(ready): 0},
        compiler_params=pltpu.CompilerParams(vmem_limit_bytes=12 * MIB),
        cost_estimate=pl.CostEstimate(flops=MIB, bytes_accessed=MIB, transcendentals=0),
    )(
        listed,
        cls,
        near_map,
        *[pinned(a) for a in (rows, weighted, rad_here, near_here, *[parts[0] for _, _, parts in ready], table)],
    )
    if left:
        for_other = apply(left, boxes, for_other, None, BF16, full)
    from_other = partner(for_other, 1)

    total, last = lax.optimization_barrier((total, last))
    turned = {m: [partner(part, 1) for part in last[m]] for m in inner}
    total = apply((early + middle)[count:], 0, total, from_other, F32, full)
    late = [(True, top + m, last[m]) for m in inner]
    late += [(True, top + m + 1, turned[m]) for m in inner]
    return apply(late, 0, total, None, BF16, currents.shape)


def solution(mesh):
    placed = (
        P("region", "dir", None, None),
        P(),
        P(),
        P(),
        P("region", "dir", None, None, None),
        P(),
        P("region", None, None),
        P("region", None, None),
        P("region", "dir", None),
    )
    return jax.shard_map(
        shards,
        mesh=mesh,
        in_specs=placed,
        out_specs=P("region", "dir", None, None),
        check_vma=False,
    )
```

```python
import functools

import jax
import jax.numpy as jnp
from jax import lax
from jax.experimental import pallas as pl
from jax.experimental.pallas import tpu as pltpu
from jax.sharding import PartitionSpec as P

BF16, F32, I32 = jnp.bfloat16, jnp.float32, jnp.int32
NT_DIMS = (((1,), (1,)), ((), ()))
LANES = 128
ROWS = 8
UNROLL = 16
TAIL = 4
GROUP = 8
MIB = 2**20


def pad_to(size, tile):
    return -(-size // tile) * tile


def whole(memory_space):
    return pl.BlockSpec(memory_space=memory_space)


def lookup(parts, hot):
    return lax.dot_general(parts.astype(F32).astype(BF16), hot.astype(BF16), NT_DIMS, preferred_element_type=F32).astype(I32)


def fill_operators(begin, end, list_ref, rows_ref, weighted_ref, rad_ref, out_ref):
    def step(at, wide):
        for u in range(wide):
            place = jnp.minimum(at + u, end - 1)
            row = rows_ref[pl.ds(list_ref[0, place], 1), :].astype(BF16)
            product = weighted_ref[...] * row
            out_ref[place] = jnp.dot(product, rad_ref[...], preferred_element_type=F32).astype(BF16)

    def main_step(i, carry):
        step(begin + i * UNROLL, UNROLL)
        return carry

    def tail_step(i, carry):
        step(begin + main * UNROLL + i * TAIL, TAIL)
        return carry

    count = jnp.maximum(end - begin, 0)
    main = count // UNROLL
    lax.fori_loop(0, main, main_step, 0)
    lax.fori_loop(0, (count - main * UNROLL + TAIL - 1) // TAIL, tail_step, 0)


def first_kernel(
    shared,
    boxes,
    halo,
    region_boxes,
    off_hbm,
    src_hbm,
    tid_hbm,
    table_hbm,
    recv_hbm,
    rad_hbm,
    t_ref,
    weighted_ref,
    rad_ref,
    rows_ref,
    cls_ref,
    listed_ref,
    off_ref,
    src_ref,
    tid_ref,
    table_ref,
    recv_ref,
    list_ref,
    sems,
):
    pairs = [
        (src_hbm, src_ref),
        (tid_hbm, tid_ref),
        (off_hbm, off_ref),
        (recv_hbm, recv_ref),
        (table_hbm, table_ref),
        (rad_hbm, rad_ref),
    ]
    copies = [pltpu.make_async_copy(a, b, sems.at[i]) for i, (a, b) in enumerate(pairs)]
    for copy in copies:
        copy.start()
    classes = table_ref.shape[0]
    directions = recv_ref.shape[1]
    me = lax.axis_index("dir")
    dir_count = region_boxes // boxes
    top = dir_count // 2
    slots = src_ref.shape[2]
    width = cls_ref.shape[1]
    used_width = listed_ref.shape[1]
    ext_at = lax.broadcasted_iota(I32, (width, slots), 0)
    class_at = lax.broadcasted_iota(I32, (used_width, slots), 0)
    row_at = lax.broadcasted_iota(I32, (ROWS, slots), 0)
    out_row = lax.broadcasted_iota(I32, cls_ref.shape, 0)
    seen = jnp.zeros((used_width, slots), F32)
    seen_by_chip = seen
    cls = jnp.full(cls_ref.shape, classes, I32)
    copies[0].wait()
    copies[1].wait()
    for j in range(2 * boxes):
        target = (me if j < boxes else me ^ 1) * boxes + j % boxes
        src = src_ref[0, pl.ds(target, 1), :]
        tid = tid_ref[0, pl.ds(target, 1), :]
        mask = (((src - halo + region_boxes) // boxes) % dir_count) ^ me
        beyond = (src < halo) | (src >= halo + region_boxes)
        late = beyond & ((mask & top) != 0) & ((mask & (top - 2)) != 0)
        even = (mask & 1) == 0
        here = (src >= 0) & ((even | late) if j < boxes else (even & ~late))
        seen = jnp.where((class_at == tid) & here, 1.0, seen)
        seen_by_chip = jnp.where((class_at == tid) & (src >= 0), 1.0, seen_by_chip)
        parts = jnp.where(row_at == 0, tid // 16, jnp.where(row_at == 1, tid % 16, 1))
        found = lookup(parts, jnp.where(ext_at == src, 1.0, 0.0))
        value = jnp.where(found[2:3] > 0, found[0:1] * 16 + found[1:2], classes)
        cls = jnp.where(out_row == j, value, cls)
    cls_ref[...] = cls
    lane = lax.broadcasted_iota(I32, (ROWS, used_width), 1)
    list_row = lax.broadcasted_iota(I32, (ROWS, used_width), 0)
    ones = jnp.ones((ROWS, slots), I32)
    by_chip = jnp.where(lane < shared, jnp.minimum(lookup(ones, seen_by_chip), 1), 0)
    by_core = jnp.where(lane >= shared, jnp.minimum(lookup(ones, seen), 1), 0)
    is_used = jnp.where(list_row == 0, by_chip, by_core)
    down = lax.broadcasted_iota(I32, (used_width, used_width), 0)
    across = lax.broadcasted_iota(I32, (used_width, used_width), 1)
    rank = lookup(is_used, jnp.where(across < down, 1.0, 0.0))
    shared_rank, own_rank = rank[0:1], rank[1:2]
    one_lane = lane[0:1]
    capacity = (shared + 1) // 2
    empty = capacity + classes - shared
    other = (shared_rank ^ me) & 1
    shared_place = shared_rank // 2 + other * (empty + 1)
    place = jnp.where(one_lane < shared, shared_place, capacity + own_rank)
    place = jnp.where(one_lane == classes, empty, place)
    listed_here = jnp.where(one_lane < shared, is_used[0:1] * (1 - other), is_used[1:2])
    here = down == jnp.where(listed_here > 0, place, -1)
    found = lookup(jnp.where(list_row == 0, lane // 16, lane % 16), jnp.where(here, 1.0, 0.0))
    ordered = found[0:1] * 16 + found[1:2]
    count = jnp.sum(is_used.astype(F32), axis=1, keepdims=True).astype(I32)
    first_end = (count[0:1] - (me & 1) + 1) // 2
    ends = jnp.where(one_lane == 0, first_end, capacity + count[1:2])
    listed = jnp.where(list_row == 0, ordered, jnp.where(list_row == 1, place, ends))
    listed_ref[...] = listed
    to_smem = pltpu.make_async_copy(listed_ref, list_ref, sems.at[len(pairs)])
    to_smem.start()
    copies[2].wait()
    position = lax.broadcasted_iota(I32, (1, directions), 1)
    band_size = jnp.ones((1, directions), I32)
    bands = off_ref.shape[0] - 1
    for d in range(bands):
        start, end = off_ref[d], off_ref[d + 1]
        band_size = jnp.where((position >= start) & (position < end), end - start, band_size)
    weight = directions / (bands * band_size.astype(F32))
    copies[3].wait()
    weighted_ref[...] = (recv_ref[...].astype(F32) * weight).astype(BF16)
    copies[4].wait()
    rows_ref[...] = table_ref[...].astype(F32)
    to_smem.wait()
    copies[5].wait()
    fill_operators(0, list_ref[2, 0], list_ref, rows_ref, weighted_ref, rad_ref, t_ref)


def second_kernel(
    second_end,
    empty,
    near_shift,
    list_ref,
    rows_ref,
    weighted_ref,
    rad_ref,
    near_src_ref,
    near_src_other_ref,
    near_hbm,
    near_other_hbm,
    low_ref,
    t_ref,
    near_ref,
    near_map_ref,
    sems,
):
    boxes, near_slots = near_hbm.shape[1:3]
    copies = []
    for i, array in enumerate((near_hbm, near_other_hbm)):
        for j in range(boxes):
            row = i * boxes + j
            copies.append(
                pltpu.make_async_copy(array.at[0, j], near_ref.at[row, pl.ds(0, near_slots)], sems.at[row])
            )
            copies[-1].start()
    first_count = low_ref.shape[0]
    copies.append(pltpu.make_async_copy(low_ref, t_ref.at[pl.ds(0, first_count)], sems.at[2 * boxes]))
    copies[-1].start()
    t_ref[empty] = jnp.zeros(t_ref.shape[1:], BF16)
    for row in range(2 * boxes):
        near_ref[row, near_slots] = jnp.zeros(near_ref.shape[2:], BF16)
    width = near_map_ref.shape[1]
    near_at = lax.broadcasted_iota(I32, (width, near_slots), 0)
    row_at = lax.broadcasted_iota(I32, (ROWS, near_slots), 0)
    lane_at = lax.broadcasted_iota(I32, (ROWS, near_slots), 1)
    out_row = lax.broadcasted_iota(I32, near_map_ref.shape, 0)
    near_map = jnp.full(near_map_ref.shape, near_slots, I32)
    for j in range(2 * boxes):
        near = (near_src_ref if j < boxes else near_src_other_ref)[j % boxes]
        found = lookup(jnp.where(row_at == 0, lane_at, 1), jnp.where((near_at == near + near_shift) & (near >= 0), 1.0, 0.0))
        value = jnp.where(found[1:2] > 0, found[0:1], near_slots)
        near_map = jnp.where(out_row == j, value, near_map)
    near_map_ref[...] = near_map
    end = jnp.minimum(list_ref[2, 1], second_end)
    fill_operators(first_count, end, list_ref, rows_ref, weighted_ref, rad_ref, t_ref)
    for copy in copies:
        copy.wait()


def add_products(places, first_row, boxes, halo, cls_ref, near_map_ref, list_ref, t_ref, near_ref, source_refs, start, store):
    me = lax.axis_index("dir")
    region_boxes = boxes * lax.axis_size("dir")
    bases, groups, at = [], [], 0
    for rim, mask, parts in places:
        groups.append(source_refs[at : at + parts])
        at += parts
        owner = me ^ mask
        base = owner * boxes + halo
        if rim:
            base = base + jnp.where(owner * boxes >= halo, -region_boxes, region_boxes)
        bases.append(base)
    for j in range(boxes):
        row = first_row + j
        total = start(j)
        for base, refs in zip(bases, groups):
            blocks = []
            for b in range(boxes):
                n = list_ref[1, cls_ref[row, base + b]]
                blocks.append(t_ref[n] + near_ref[row, near_map_ref[row, base + b]])
            values = [ref[...].reshape(-1, ref.shape[-1]) for ref in refs]
            rhs = values[0] if len(values) == 1 else jnp.concatenate(values, 0)
            added = jnp.dot(jnp.concatenate(blocks, 1), rhs, preferred_element_type=F32)
            total = added if total is None else total + added
        store(j, total)


def third_kernel(
    second_end,
    empty,
    places,
    early,
    boxes,
    halo,
    list_ref,
    cls_ref,
    near_map_ref,
    rows_ref,
    weighted_ref,
    rad_ref,
    near_ref,
    low_ref,
    *rest,
):
    source_count = sum(parts for _, _, parts in places)
    source_refs, (_, t_ref, other_ref, own_ref, sem) = rest[:source_count], rest[source_count:]
    copy = pltpu.make_async_copy(low_ref, t_ref.at[pl.ds(empty + 1, low_ref.shape[0])], sem)
    copy.start()
    fill_operators(second_end, list_ref[2, 1], list_ref, rows_ref, weighted_ref, rad_ref, t_ref)
    copy.wait()

    def store_other(j, total):
        other_ref[j] = total.astype(other_ref.dtype)

    def store_own(j, total):
        own_ref[j] = total

    refs = (cls_ref, near_map_ref, list_ref, t_ref, near_ref)
    add_products(places, boxes, boxes, halo, *refs, source_refs, lambda j: None, store_other)
    add_products(places[:early], 0, boxes, halo, *refs, source_refs, lambda j: None, store_own)


def apply_kernel(
    places, first_row, boxes, halo, with_total, with_other, cls_ref, near_map_ref, list_ref, t_ref, near_ref, *rest
):
    source_count = sum(parts for _, _, parts in places)
    source_refs, rest = rest[:source_count], rest[source_count:]
    if with_total:
        sum_ref, *rest = rest
    if with_other:
        other_ref, *rest = rest
    (out_ref,) = rest

    def start(j):
        total = sum_ref[j] if with_total else None
        if with_other:
            other = other_ref[j].astype(F32)
            total = other if total is None else total + other
        return total

    def store(j, total):
        if len(out_ref.shape) == 4:
            out_ref[0, j] = total.astype(out_ref.dtype)
        else:
            out_ref[j] = total.astype(out_ref.dtype)

    refs = (cls_ref, near_map_ref, list_ref, t_ref, near_ref)
    add_products(places, first_row, boxes, halo, *refs, source_refs, start, store)


def shards(
    currents,
    radiate,
    receive,
    transfer_table,
    near_blocks,
    dir_offsets,
    trans_src,
    trans_tid,
    near_src,
):
    dir_count = lax.axis_size("dir")
    region_count = lax.axis_size("region")
    own = currents[0]
    boxes, unknowns, incidences = own.shape
    near_slots = near_src.shape[2]
    near_src = near_src.reshape(boxes, 1, near_slots)
    region_boxes = boxes * dir_count
    halo = region_boxes // 2
    near_halo = region_boxes // 4
    classes, directions = transfer_table.shape
    shared = classes * 5 // 8
    capacity = (shared + 1) // 2
    empty = capacity + classes - shared
    second_end = capacity + pad_to(classes // 5, UNROLL)
    top = dir_count // 2
    inner = range(2, top, 2)
    split = boxes // 2
    targets = 2 * boxes

    def partner(array, mask):
        return lax.ppermute(array, "dir", [(i, i ^ mask) for i in range(dir_count)])

    along = []
    for i in range(dir_count):
        for z in range(region_count):
            target = z + 1 if i >= top else z - 1
            if 0 <= target < region_count:
                along.append((i * region_count + z, i * region_count + target))

    def beyond(array):
        return lax.ppermute(array, ("dir", "region"), along)

    def pinned(array):
        return pltpu.with_memory_space_constraint(array, pltpu.VMEM)

    def in_hbm(array):
        return pltpu.with_memory_space_constraint(array, pltpu.HBM)

    width = pad_to(region_boxes + 2 * halo, LANES)
    map_shape = (pad_to(targets, ROWS), width)
    table_shape = (empty + 1 + capacity, unknowns, unknowns)
    low_shape = (capacity, unknowns, unknowns)
    list_shape = (ROWS, pad_to(classes + 1, LANES))
    vmem, smem, hbm = whole(pltpu.VMEM), whole(pltpu.SMEM), whole(pltpu.HBM)
    operator_cost = pl.CostEstimate(
        flops=classes * unknowns * unknowns * directions, bytes_accessed=MIB, transcendentals=0
    )

    field = {0: own}
    rim = {}
    for m in inner:
        field[m] = partner(own, m)
    field[top] = partner(own, top)
    rim[0] = beyond(own)
    near_other = partner(near_blocks, 1)
    near_src_other = partner(near_src, 1)
    low, weighted, rad_here, rows, cls, listed = pl.pallas_call(
        functools.partial(first_kernel, shared, boxes, halo, region_boxes),
        in_specs=[hbm] * 6,
        out_specs=[vmem] * 6,
        out_shape=(
            pltpu.VMEM(low_shape, BF16),
            pltpu.VMEM((unknowns, directions), BF16),
            pltpu.VMEM((directions, unknowns), BF16),
            pltpu.VMEM((classes, directions), F32),
            pltpu.VMEM(map_shape, I32),
            pltpu.VMEM(list_shape, I32),
        ),
        scratch_shapes=[
            pltpu.SMEM(dir_offsets.shape, I32),
            pltpu.VMEM(trans_src.shape, I32),
            pltpu.VMEM(trans_tid.shape, I32),
            pltpu.VMEM(transfer_table.shape, BF16),
            pltpu.VMEM(receive.shape, BF16),
            pltpu.SMEM(list_shape, I32),
            pltpu.SemaphoreType.DMA((7,)),
        ],
        compiler_params=pltpu.CompilerParams(vmem_limit_bytes=8 * MIB),
        cost_estimate=operator_cost,
    )(*[in_hbm(a) for a in (dir_offsets, trans_src, trans_tid, transfer_table, receive, radiate)])

    tied = lax.optimization_barrier((low, [field[m] for m in inner], field[top], rim[0]))
    low, inner_fields, field[top], rim[0] = tied
    for m, value in zip(inner, inner_fields):
        field[m] = value
    low, near_other, near_src_other = lax.optimization_barrier((low, near_other, near_src_other))
    low_other = partner(low, 1)
    for m in inner:
        field[top + m] = partner(field[top], m)
    rim[top] = partner(rim[0], top)
    for m in inner:
        rim[m] = beyond(field[m])

    table, near_here, near_map = pl.pallas_call(
        functools.partial(second_kernel, second_end, empty, halo - near_halo),
        in_specs=[smem] + [vmem] * 5 + [hbm] * 2 + [vmem],
        out_specs=[vmem] * 3,
        out_shape=(
            pltpu.VMEM(table_shape, BF16),
            pltpu.VMEM((targets, near_slots + 1, unknowns, unknowns), BF16),
            pltpu.VMEM(map_shape, I32),
        ),
        scratch_shapes=[pltpu.SemaphoreType.DMA((targets + 1,))],
        compiler_params=pltpu.CompilerParams(vmem_limit_bytes=8 * MIB),
        cost_estimate=operator_cost,
    )(
        listed,
        pinned(rows),
        pinned(weighted),
        pinned(rad_here),
        near_src,
        near_src_other,
        in_hbm(near_blocks),
        near_other,
        pinned(low),
    )

    def apply(places, first_row, total, other, dtype, shape):
        if len(places) > GROUP:
            total = apply(places[:GROUP], first_row, total, None, F32, full)
            return apply(places[GROUP:], first_row, total, other, dtype, shape)
        args = [cls, near_map, listed, pinned(table), pinned(near_here)] + [pinned(part) for _, _, parts in places for part in parts]
        args += [pinned(extra) for extra in (total, other) if extra is not None]
        specs = [smem] * 3 + [vmem] * (len(args) - 3)
        layout = [(outside, mask, len(parts)) for outside, mask, parts in places]
        kernel = functools.partial(
            apply_kernel, layout, first_row, boxes, halo, total is not None, other is not None
        )
        return pl.pallas_call(
            kernel,
            in_specs=specs,
            out_specs=vmem,
            out_shape=pltpu.VMEM(shape, dtype) if len(shape) == 3 else jax.ShapeDtypeStruct(shape, dtype),
            compiler_params=pltpu.CompilerParams(vmem_limit_bytes=12 * MIB),
            cost_estimate=pl.CostEstimate(flops=MIB, bytes_accessed=MIB, transcendentals=0),
        )(*args)

    tied = lax.optimization_barrier(
        (table, [field[top + m] for m in inner], [rim[m] for m in inner], rim[top])
    )
    table, far_fields, inner_rims, rim[top] = tied
    for m, value, other in zip(inner, far_fields, inner_rims):
        field[top + m], rim[m] = value, other
    last = {m: [partner(rim[top][:split], m), partner(rim[m][split:], top)] for m in inner}

    full = (boxes, unknowns, incidences)
    early = [(False, m, [field[m]]) for m in (0, *inner, top)] + [(True, 0, [rim[0]])]
    middle = [(False, top + m, [field[top + m]]) for m in inner]
    middle += [(True, m, [rim[m]]) for m in (*inner, top)]
    ready = (early + middle)[:GROUP]
    left = (early + middle)[GROUP:]
    count = min(len(early), GROUP)
    table, for_other, total = pl.pallas_call(
        functools.partial(
            third_kernel, second_end, empty, [(outside, mask, 1) for outside, mask, _ in ready], count, boxes, halo
        ),
        in_specs=[smem] * 3 + [vmem] * (6 + len(ready)),
        out_specs=[vmem] * 3,
        out_shape=(
            pltpu.VMEM(table_shape, BF16),
            pltpu.VMEM(full, F32 if left else BF16),
            pltpu.VMEM(full, F32),
        ),
        input_output_aliases={8 + len(ready): 0},
        scratch_shapes=[pltpu.SemaphoreType.DMA],
        compiler_params=pltpu.CompilerParams(vmem_limit_bytes=12 * MIB),
        cost_estimate=pl.CostEstimate(flops=MIB, bytes_accessed=MIB, transcendentals=0),
    )(
        listed,
        cls,
        near_map,
        *[pinned(a) for a in (rows, weighted, rad_here, near_here, low_other, *[parts[0] for _, _, parts in ready], table)],
    )
    if left:
        for_other = apply(left, boxes, for_other, None, BF16, full)
    from_other = partner(for_other, 1)

    total, last = lax.optimization_barrier((total, last))
    turned = {m: [partner(part, 1) for part in last[m]] for m in inner}
    total = apply((early + middle)[count:], 0, total, from_other, F32, full)
    late = [(True, top + m, last[m]) for m in inner]
    late += [(True, top + m + 1, turned[m]) for m in inner]
    return apply(late, 0, total, None, BF16, currents.shape)


def solution(mesh):
    placed = (
        P("region", "dir", None, None),
        P(),
        P(),
        P(),
        P("region", "dir", None, None, None),
        P(),
        P("region", None, None),
        P("region", None, None),
        P("region", "dir", None),
    )
    return jax.shard_map(
        shards,
        mesh=mesh,
        in_specs=placed,
        out_specs=P("region", "dir", None, None),
        check_vma=False,
    )
```

```python
import functools

import jax
import jax.numpy as jnp
from jax import lax
from jax.experimental import pallas as pl
from jax.experimental.pallas import tpu as pltpu
from jax.sharding import PartitionSpec as P

BF16, F32, I32 = jnp.bfloat16, jnp.float32, jnp.int32
NT_DIMS = (((1,), (1,)), ((), ()))
LANES = 128
ROWS = 8
UNROLL = 16
TAIL = 4
GROUP = 8
MIB = 2**20


def pad_to(size, tile):
    return -(-size // tile) * tile


def whole(memory_space):
    return pl.BlockSpec(memory_space=memory_space)


def lookup(parts, hot):
    return lax.dot_general(parts.astype(F32).astype(BF16), hot.astype(BF16), NT_DIMS, preferred_element_type=F32).astype(I32)


def fill_operators(begin, end, list_ref, rows_ref, weighted_ref, rad_ref, out_ref):
    def step(at, wide):
        for u in range(wide):
            place = jnp.minimum(at + u, end - 1)
            row = rows_ref[pl.ds(list_ref[0, place], 1), :].astype(BF16)
            product = weighted_ref[...] * row
            out_ref[place] = jnp.dot(product, rad_ref[...], preferred_element_type=F32).astype(BF16)

    def main_step(i, carry):
        step(begin + i * UNROLL, UNROLL)
        return carry

    def tail_step(i, carry):
        step(begin + main * UNROLL + i * TAIL, TAIL)
        return carry

    count = jnp.maximum(end - begin, 0)
    main = count // UNROLL
    lax.fori_loop(0, main, main_step, 0)
    lax.fori_loop(0, (count - main * UNROLL + TAIL - 1) // TAIL, tail_step, 0)


def first_kernel(
    shared,
    boxes,
    halo,
    region_boxes,
    off_hbm,
    src_hbm,
    tid_hbm,
    table_hbm,
    recv_hbm,
    rad_hbm,
    t_ref,
    weighted_ref,
    rad_ref,
    rows_ref,
    cls_ref,
    listed_ref,
    off_ref,
    src_ref,
    tid_ref,
    table_ref,
    recv_ref,
    list_ref,
    sems,
):
    pairs = [
        (src_hbm, src_ref),
        (tid_hbm, tid_ref),
        (off_hbm, off_ref),
        (recv_hbm, recv_ref),
        (table_hbm, table_ref),
        (rad_hbm, rad_ref),
    ]
    copies = [pltpu.make_async_copy(a, b, sems.at[i]) for i, (a, b) in enumerate(pairs)]
    for copy in copies:
        copy.start()
    classes = table_ref.shape[0]
    directions = recv_ref.shape[1]
    me = lax.axis_index("dir")
    dir_count = region_boxes // boxes
    top = dir_count // 2
    slots = src_ref.shape[2]
    width = cls_ref.shape[1]
    used_width = listed_ref.shape[1]
    ext_at = lax.broadcasted_iota(I32, (width, slots), 0)
    class_at = lax.broadcasted_iota(I32, (used_width, slots), 0)
    row_at = lax.broadcasted_iota(I32, (ROWS, slots), 0)
    out_row = lax.broadcasted_iota(I32, cls_ref.shape, 0)
    seen = jnp.zeros((used_width, slots), F32)
    cls = jnp.full(cls_ref.shape, classes, I32)
    copies[0].wait()
    copies[1].wait()
    for j in range(2 * boxes):
        target = (me if j < boxes else me ^ 1) * boxes + j % boxes
        src = src_ref[0, pl.ds(target, 1), :]
        tid = tid_ref[0, pl.ds(target, 1), :]
        mask = (((src - halo + region_boxes) // boxes) % dir_count) ^ me
        beyond = (src < halo) | (src >= halo + region_boxes)
        late = beyond & ((mask & top) != 0) & ((mask & (top - 2)) != 0)
        even = (mask & 1) == 0
        here = (src >= 0) & ((even | late) if j < boxes else (even & ~late))
        seen = jnp.maximum(seen, jnp.where(class_at == tid, jnp.where(here, 2.0, jnp.where(src >= 0, 1.0, 0.0)), 0.0))
        parts = jnp.where(row_at == 0, tid // 16, jnp.where(row_at == 1, tid % 16, 1))
        found = lookup(parts, jnp.where(ext_at == src, 1.0, 0.0))
        value = jnp.where(found[2:3] > 0, found[0:1] * 16 + found[1:2], classes)
        cls = jnp.where(out_row == j, value, cls)
    cls_ref[...] = cls
    lane = lax.broadcasted_iota(I32, (ROWS, used_width), 1)
    list_row = lax.broadcasted_iota(I32, (ROWS, used_width), 0)
    ones = jnp.ones((ROWS, slots), I32)
    by_chip = jnp.where(lane < shared, jnp.minimum(lookup(ones, jnp.where(seen > 0.0, 1.0, 0.0)), 1), 0)
    by_core = jnp.where(lane >= shared, jnp.minimum(lookup(ones, jnp.where(seen > 1.0, 1.0, 0.0)), 1), 0)
    is_used = jnp.where(list_row == 0, by_chip, by_core)
    down = lax.broadcasted_iota(I32, (used_width, used_width), 0)
    across = lax.broadcasted_iota(I32, (used_width, used_width), 1)
    rank = lookup(is_used, jnp.where(across < down, 1.0, 0.0))
    shared_rank, own_rank = rank[0:1], rank[1:2]
    one_lane = lane[0:1]
    capacity = (shared + 1) // 2
    empty = capacity + classes - shared
    other = (shared_rank ^ me) & 1
    shared_place = shared_rank // 2 + other * (empty + 1)
    place = jnp.where(one_lane < shared, shared_place, capacity + own_rank)
    place = jnp.where(one_lane == classes, empty, place)
    listed_here = jnp.where(one_lane < shared, is_used[0:1] * (1 - other), is_used[1:2])
    here = down == jnp.where(listed_here > 0, place, -1)
    found = lookup(jnp.where(list_row == 0, lane // 16, lane % 16), jnp.where(here, 1.0, 0.0))
    ordered = found[0:1] * 16 + found[1:2]
    count = jnp.sum(is_used.astype(F32), axis=1, keepdims=True).astype(I32)
    first_end = (count[0:1] - (me & 1) + 1) // 2
    ends = jnp.where(one_lane == 0, first_end, capacity + count[1:2])
    listed = jnp.where(list_row == 0, ordered, jnp.where(list_row == 1, place, ends))
    listed_ref[...] = listed
    to_smem = pltpu.make_async_copy(listed_ref, list_ref, sems.at[len(pairs)])
    to_smem.start()
    copies[2].wait()
    position = lax.broadcasted_iota(I32, (1, directions), 1)
    band_size = jnp.ones((1, directions), I32)
    bands = off_ref.shape[0] - 1
    for d in range(bands):
        start, end = off_ref[d], off_ref[d + 1]
        band_size = jnp.where((position >= start) & (position < end), end - start, band_size)
    weight = directions / (bands * band_size.astype(F32))
    copies[3].wait()
    weighted_ref[...] = (recv_ref[...].astype(F32) * weight).astype(BF16)
    copies[4].wait()
    rows_ref[...] = table_ref[...].astype(F32)
    to_smem.wait()
    copies[5].wait()
    fill_operators(0, list_ref[2, 0], list_ref, rows_ref, weighted_ref, rad_ref, t_ref)


def second_kernel(
    second_end,
    empty,
    near_shift,
    list_ref,
    rows_ref,
    weighted_ref,
    rad_ref,
    near_src_ref,
    near_src_other_ref,
    near_hbm,
    near_other_hbm,
    low_ref,
    t_ref,
    near_ref,
    near_map_ref,
    sems,
):
    boxes, near_slots = near_hbm.shape[1:3]
    copies = []
    for i, array in enumerate((near_hbm, near_other_hbm)):
        for j in range(boxes):
            row = i * boxes + j
            copies.append(
                pltpu.make_async_copy(array.at[0, j], near_ref.at[row, pl.ds(0, near_slots)], sems.at[row])
            )
            copies[-1].start()
    first_count = low_ref.shape[0]
    copies.append(pltpu.make_async_copy(low_ref, t_ref.at[pl.ds(0, first_count)], sems.at[2 * boxes]))
    copies[-1].start()
    t_ref[empty] = jnp.zeros(t_ref.shape[1:], BF16)
    for row in range(2 * boxes):
        near_ref[row, near_slots] = jnp.zeros(near_ref.shape[2:], BF16)
    width = near_map_ref.shape[1]
    near_at = lax.broadcasted_iota(I32, (width, near_slots), 0)
    row_at = lax.broadcasted_iota(I32, (ROWS, near_slots), 0)
    lane_at = lax.broadcasted_iota(I32, (ROWS, near_slots), 1)
    out_row = lax.broadcasted_iota(I32, near_map_ref.shape, 0)
    near_map = jnp.full(near_map_ref.shape, near_slots, I32)
    for j in range(2 * boxes):
        near = (near_src_ref if j < boxes else near_src_other_ref)[j % boxes]
        found = lookup(jnp.where(row_at == 0, lane_at, 1), jnp.where((near_at == near + near_shift) & (near >= 0), 1.0, 0.0))
        value = jnp.where(found[1:2] > 0, found[0:1], near_slots)
        near_map = jnp.where(out_row == j, value, near_map)
    near_map_ref[...] = near_map
    end = jnp.minimum(list_ref[2, 1], second_end)
    fill_operators(first_count, end, list_ref, rows_ref, weighted_ref, rad_ref, t_ref)
    for copy in copies:
        copy.wait()


def add_products(places, first_row, boxes, halo, cls_ref, near_map_ref, list_ref, t_ref, near_ref, source_refs, start, store):
    me = lax.axis_index("dir")
    region_boxes = boxes * lax.axis_size("dir")
    bases, groups, at = [], [], 0
    for rim, mask, parts in places:
        groups.append(source_refs[at : at + parts])
        at += parts
        owner = me ^ mask
        base = owner * boxes + halo
        if rim:
            base = base + jnp.where(owner * boxes >= halo, -region_boxes, region_boxes)
        bases.append(base)
    for j in range(boxes):
        row = first_row + j
        total = start(j)
        for base, refs in zip(bases, groups):
            blocks = []
            for b in range(boxes):
                n = list_ref[1, cls_ref[row, base + b]]
                blocks.append(t_ref[n] + near_ref[row, near_map_ref[row, base + b]])
            values = [ref[...].reshape(-1, ref.shape[-1]) for ref in refs]
            rhs = values[0] if len(values) == 1 else jnp.concatenate(values, 0)
            added = jnp.dot(jnp.concatenate(blocks, 1), rhs, preferred_element_type=F32)
            total = added if total is None else total + added
        store(j, total)


def third_kernel(
    second_end,
    empty,
    places,
    early,
    boxes,
    halo,
    list_ref,
    cls_ref,
    near_map_ref,
    rows_ref,
    weighted_ref,
    rad_ref,
    near_ref,
    low_ref,
    *rest,
):
    source_count = sum(parts for _, _, parts in places)
    source_refs, (_, t_ref, other_ref, own_ref, sem) = rest[:source_count], rest[source_count:]
    copy = pltpu.make_async_copy(low_ref, t_ref.at[pl.ds(empty + 1, low_ref.shape[0])], sem)
    copy.start()
    fill_operators(second_end, list_ref[2, 1], list_ref, rows_ref, weighted_ref, rad_ref, t_ref)
    copy.wait()

    def store_other(j, total):
        other_ref[j] = total.astype(other_ref.dtype)

    def store_own(j, total):
        own_ref[j] = total

    refs = (cls_ref, near_map_ref, list_ref, t_ref, near_ref)
    add_products(places, boxes, boxes, halo, *refs, source_refs, lambda j: None, store_other)
    add_products(places[:early], 0, boxes, halo, *refs, source_refs, lambda j: None, store_own)


def apply_kernel(
    places, first_row, boxes, halo, with_total, with_other, cls_ref, near_map_ref, list_ref, t_ref, near_ref, *rest
):
    source_count = sum(parts for _, _, parts in places)
    source_refs, rest = rest[:source_count], rest[source_count:]
    if with_total:
        sum_ref, *rest = rest
    if with_other:
        other_ref, *rest = rest
    (out_ref,) = rest

    def start(j):
        total = sum_ref[j] if with_total else None
        if with_other:
            other = other_ref[j].astype(F32)
            total = other if total is None else total + other
        return total

    def store(j, total):
        if len(out_ref.shape) == 4:
            out_ref[0, j] = total.astype(out_ref.dtype)
        else:
            out_ref[j] = total.astype(out_ref.dtype)

    refs = (cls_ref, near_map_ref, list_ref, t_ref, near_ref)
    add_products(places, first_row, boxes, halo, *refs, source_refs, start, store)


def shards(
    currents,
    radiate,
    receive,
    transfer_table,
    near_blocks,
    dir_offsets,
    trans_src,
    trans_tid,
    near_src,
):
    dir_count = lax.axis_size("dir")
    region_count = lax.axis_size("region")
    own = currents[0]
    boxes, unknowns, incidences = own.shape
    near_slots = near_src.shape[2]
    near_src = near_src.reshape(boxes, 1, near_slots)
    region_boxes = boxes * dir_count
    halo = region_boxes // 2
    near_halo = region_boxes // 4
    classes, directions = transfer_table.shape
    shared = classes * 5 // 8
    capacity = (shared + 1) // 2
    empty = capacity + classes - shared
    second_end = capacity + pad_to(classes // 8, UNROLL)
    top = dir_count // 2
    inner = range(2, top, 2)
    split = boxes // 2
    targets = 2 * boxes

    def partner(array, mask):
        return lax.ppermute(array, "dir", [(i, i ^ mask) for i in range(dir_count)])

    along = []
    for i in range(dir_count):
        for z in range(region_count):
            target = z + 1 if i >= top else z - 1
            if 0 <= target < region_count:
                along.append((i * region_count + z, i * region_count + target))

    def beyond(array):
        return lax.ppermute(array, ("dir", "region"), along)

    def pinned(array):
        return pltpu.with_memory_space_constraint(array, pltpu.VMEM)

    def in_hbm(array):
        return pltpu.with_memory_space_constraint(array, pltpu.HBM)

    width = pad_to(region_boxes + 2 * halo, LANES)
    map_shape = (pad_to(targets, ROWS), width)
    table_shape = (empty + 1 + capacity, unknowns, unknowns)
    low_shape = (capacity, unknowns, unknowns)
    list_shape = (ROWS, pad_to(classes + 1, LANES))
    vmem, smem, hbm = whole(pltpu.VMEM), whole(pltpu.SMEM), whole(pltpu.HBM)
    operator_cost = pl.CostEstimate(
        flops=classes * unknowns * unknowns * directions, bytes_accessed=MIB, transcendentals=0
    )

    field = {0: own}
    rim = {}
    for m in inner:
        field[m] = partner(own, m)
    field[top] = partner(own, top)
    rim[0] = beyond(own)
    near_other = partner(near_blocks, 1)
    near_src_other = partner(near_src, 1)
    low, weighted, rad_here, rows, cls, listed = pl.pallas_call(
        functools.partial(first_kernel, shared, boxes, halo, region_boxes),
        in_specs=[hbm] * 6,
        out_specs=[vmem] * 6,
        out_shape=(
            pltpu.VMEM(low_shape, BF16),
            pltpu.VMEM((unknowns, directions), BF16),
            pltpu.VMEM((directions, unknowns), BF16),
            pltpu.VMEM((classes, directions), F32),
            pltpu.VMEM(map_shape, I32),
            pltpu.VMEM(list_shape, I32),
        ),
        scratch_shapes=[
            pltpu.SMEM(dir_offsets.shape, I32),
            pltpu.VMEM(trans_src.shape, I32),
            pltpu.VMEM(trans_tid.shape, I32),
            pltpu.VMEM(transfer_table.shape, BF16),
            pltpu.VMEM(receive.shape, BF16),
            pltpu.SMEM(list_shape, I32),
            pltpu.SemaphoreType.DMA((7,)),
        ],
        compiler_params=pltpu.CompilerParams(vmem_limit_bytes=8 * MIB),
        cost_estimate=operator_cost,
    )(*[in_hbm(a) for a in (dir_offsets, trans_src, trans_tid, transfer_table, receive, radiate)])

    tied = lax.optimization_barrier((low, [field[m] for m in inner], field[top], rim[0]))
    low, inner_fields, field[top], rim[0] = tied
    for m, value in zip(inner, inner_fields):
        field[m] = value
    low, near_other, near_src_other = lax.optimization_barrier((low, near_other, near_src_other))
    low_other = partner(low, 1)
    for m in inner:
        field[top + m] = partner(field[top], m)
    rim[top] = partner(rim[0], top)
    for m in inner:
        rim[m] = beyond(field[m])

    table, near_here, near_map = pl.pallas_call(
        functools.partial(second_kernel, second_end, empty, halo - near_halo),
        in_specs=[smem] + [vmem] * 5 + [hbm] * 2 + [vmem],
        out_specs=[vmem] * 3,
        out_shape=(
            pltpu.VMEM(table_shape, BF16),
            pltpu.VMEM((targets, near_slots + 1, unknowns, unknowns), BF16),
            pltpu.VMEM(map_shape, I32),
        ),
        scratch_shapes=[pltpu.SemaphoreType.DMA((targets + 1,))],
        compiler_params=pltpu.CompilerParams(vmem_limit_bytes=8 * MIB),
        cost_estimate=operator_cost,
    )(
        listed,
        pinned(rows),
        pinned(weighted),
        pinned(rad_here),
        near_src,
        near_src_other,
        in_hbm(near_blocks),
        near_other,
        pinned(low),
    )

    def apply(places, first_row, total, other, dtype, shape):
        if len(places) > GROUP:
            total = apply(places[:GROUP], first_row, total, None, F32, full)
            return apply(places[GROUP:], first_row, total, other, dtype, shape)
        args = [cls, near_map, listed, pinned(table), pinned(near_here)] + [pinned(part) for _, _, parts in places for part in parts]
        args += [pinned(extra) for extra in (total, other) if extra is not None]
        specs = [smem] * 3 + [vmem] * (len(args) - 3)
        layout = [(outside, mask, len(parts)) for outside, mask, parts in places]
        kernel = functools.partial(
            apply_kernel, layout, first_row, boxes, halo, total is not None, other is not None
        )
        return pl.pallas_call(
            kernel,
            in_specs=specs,
            out_specs=vmem,
            out_shape=pltpu.VMEM(shape, dtype) if len(shape) == 3 else jax.ShapeDtypeStruct(shape, dtype),
            compiler_params=pltpu.CompilerParams(vmem_limit_bytes=12 * MIB),
            cost_estimate=pl.CostEstimate(flops=MIB, bytes_accessed=MIB, transcendentals=0),
        )(*args)

    tied = lax.optimization_barrier(
        (table, [field[top + m] for m in inner], [rim[m] for m in inner], rim[top])
    )
    table, far_fields, inner_rims, rim[top] = tied
    for m, value, other in zip(inner, far_fields, inner_rims):
        field[top + m], rim[m] = value, other
    last = {m: [partner(rim[top][:split], m), partner(rim[m][split:], top)] for m in inner}

    full = (boxes, unknowns, incidences)
    early = [(False, m, [field[m]]) for m in (0, *inner, top)] + [(True, 0, [rim[0]])]
    middle = [(False, top + m, [field[top + m]]) for m in inner]
    middle += [(True, m, [rim[m]]) for m in (*inner, top)]
    ready = (early + middle)[:GROUP]
    left = (early + middle)[GROUP:]
    count = min(len(early), GROUP)
    table, for_other, total = pl.pallas_call(
        functools.partial(
            third_kernel, second_end, empty, [(outside, mask, 1) for outside, mask, _ in ready], count, boxes, halo
        ),
        in_specs=[smem] * 3 + [vmem] * (6 + len(ready)),
        out_specs=[vmem] * 3,
        out_shape=(
            pltpu.VMEM(table_shape, BF16),
            pltpu.VMEM(full, F32 if left else BF16),
            pltpu.VMEM(full, F32),
        ),
        input_output_aliases={8 + len(ready): 0},
        scratch_shapes=[pltpu.SemaphoreType.DMA],
        compiler_params=pltpu.CompilerParams(vmem_limit_bytes=12 * MIB),
        cost_estimate=pl.CostEstimate(flops=MIB, bytes_accessed=MIB, transcendentals=0),
    )(
        listed,
        cls,
        near_map,
        *[pinned(a) for a in (rows, weighted, rad_here, near_here, low_other, *[parts[0] for _, _, parts in ready], table)],
    )
    if left:
        for_other = apply(left, boxes, for_other, None, BF16, full)
    from_other = partner(for_other, 1)

    total, last = lax.optimization_barrier((total, last))
    turned = {m: [partner(part, 1) for part in last[m]] for m in inner}
    total = apply((early + middle)[count:], 0, total, None, F32, full)
    late = [(True, top + m, last[m]) for m in inner]
    late += [(True, top + m + 1, turned[m]) for m in inner]
    return apply(late, 0, total, from_other, BF16, currents.shape)


def solution(mesh):
    placed = (
        P("region", "dir", None, None),
        P(),
        P(),
        P(),
        P("region", "dir", None, None, None),
        P(),
        P("region", None, None),
        P("region", None, None),
        P("region", "dir", None),
    )
    return jax.shard_map(
        shards,
        mesh=mesh,
        in_specs=placed,
        out_specs=P("region", "dir", None, None),
        check_vma=False,
    )
```

```python
import functools

import jax
import jax.numpy as jnp
from jax import lax
from jax.experimental import pallas as pl
from jax.experimental.pallas import tpu as pltpu
from jax.sharding import PartitionSpec as P

BF16, F32, I32 = jnp.bfloat16, jnp.float32, jnp.int32
NT_DIMS = (((1,), (1,)), ((), ()))
LANES = 128
ROWS = 8
UNROLL = 16
TAIL = 4
GROUP = 8
MIB = 2**20


def pad_to(size, tile):
    return -(-size // tile) * tile


def whole(memory_space):
    return pl.BlockSpec(memory_space=memory_space)


def lookup(parts, hot):
    return lax.dot_general(parts.astype(F32).astype(BF16), hot.astype(BF16), NT_DIMS, preferred_element_type=F32).astype(I32)


def fill_operators(begin, end, list_ref, rows_ref, weighted_ref, rad_ref, out_ref):
    def step(at, wide):
        for u in range(wide):
            place = jnp.minimum(at + u, end - 1)
            row = rows_ref[pl.ds(list_ref[0, place], 1), :].astype(BF16)
            product = weighted_ref[...] * row
            out_ref[place] = jnp.dot(product, rad_ref[...], preferred_element_type=F32).astype(BF16)

    def main_step(i, carry):
        step(begin + i * UNROLL, UNROLL)
        return carry

    def tail_step(i, carry):
        step(begin + main * UNROLL + i * TAIL, TAIL)
        return carry

    count = jnp.maximum(end - begin, 0)
    main = count // UNROLL
    lax.fori_loop(0, main, main_step, 0)
    lax.fori_loop(0, (count - main * UNROLL + TAIL - 1) // TAIL, tail_step, 0)


def first_kernel(
    shared,
    boxes,
    halo,
    region_boxes,
    off_hbm,
    src_hbm,
    tid_hbm,
    table_hbm,
    recv_hbm,
    rad_hbm,
    t_ref,
    weighted_ref,
    rad_ref,
    rows_ref,
    cls_ref,
    listed_ref,
    off_ref,
    src_ref,
    tid_ref,
    table_ref,
    recv_ref,
    list_ref,
    sems,
):
    pairs = [
        (src_hbm, src_ref),
        (tid_hbm, tid_ref),
        (off_hbm, off_ref),
        (recv_hbm, recv_ref),
        (table_hbm, table_ref),
        (rad_hbm, rad_ref),
    ]
    copies = [pltpu.make_async_copy(a, b, sems.at[i]) for i, (a, b) in enumerate(pairs)]
    for copy in copies:
        copy.start()
    classes = table_ref.shape[0]
    directions = recv_ref.shape[1]
    me = lax.axis_index("dir")
    dir_count = region_boxes // boxes
    top = dir_count // 2
    slots = src_ref.shape[2]
    width = cls_ref.shape[1]
    used_width = listed_ref.shape[1]
    ext_at = lax.broadcasted_iota(I32, (width, slots), 0)
    class_at = lax.broadcasted_iota(I32, (used_width, slots), 0)
    row_at = lax.broadcasted_iota(I32, (ROWS, slots), 0)
    out_row = lax.broadcasted_iota(I32, cls_ref.shape, 0)
    seen = jnp.zeros((used_width, slots), F32)
    cls = jnp.full(cls_ref.shape, classes, I32)
    copies[0].wait()
    copies[1].wait()
    for j in range(2 * boxes):
        target = (me if j < boxes else me ^ 1) * boxes + j % boxes
        src = src_ref[0, pl.ds(target, 1), :]
        tid = tid_ref[0, pl.ds(target, 1), :]
        mask = (((src - halo + region_boxes) // boxes) % dir_count) ^ me
        beyond = (src < halo) | (src >= halo + region_boxes)
        late = beyond & ((mask & top) != 0) & ((mask & (top - 2)) != 0)
        even = (mask & 1) == 0
        here = (src >= 0) & ((even | late) if j < boxes else (even & ~late))
        seen = jnp.maximum(seen, jnp.where(class_at == tid, jnp.where(here, 2.0, jnp.where(src >= 0, 1.0, 0.0)), 0.0))
        parts = jnp.where(row_at == 0, tid // 16, jnp.where(row_at == 1, tid % 16, 1))
        found = lookup(parts, jnp.where(ext_at == src, 1.0, 0.0))
        value = jnp.where(found[2:3] > 0, found[0:1] * 16 + found[1:2], classes)
        cls = jnp.where(out_row == j, value, cls)
    cls_ref[...] = cls
    lane = lax.broadcasted_iota(I32, (ROWS, used_width), 1)
    list_row = lax.broadcasted_iota(I32, (ROWS, used_width), 0)
    ones = jnp.ones((ROWS, slots), I32)
    by_chip = jnp.where(lane < shared, jnp.minimum(lookup(ones, jnp.where(seen > 0.0, 1.0, 0.0)), 1), 0)
    by_core = jnp.where(lane >= shared, jnp.minimum(lookup(ones, jnp.where(seen > 1.0, 1.0, 0.0)), 1), 0)
    is_used = jnp.where(list_row == 0, by_chip, by_core)
    down = lax.broadcasted_iota(I32, (used_width, used_width), 0)
    across = lax.broadcasted_iota(I32, (used_width, used_width), 1)
    rank = lookup(is_used, jnp.where(across < down, 1.0, 0.0))
    shared_rank, own_rank = rank[0:1], rank[1:2]
    one_lane = lane[0:1]
    capacity = (shared + 1) // 2
    empty = capacity + classes - shared
    other = (shared_rank ^ me) & 1
    shared_place = shared_rank // 2 + other * (empty + 1)
    place = jnp.where(one_lane < shared, shared_place, capacity + own_rank)
    place = jnp.where(one_lane == classes, empty, place)
    listed_here = jnp.where(one_lane < shared, is_used[0:1] * (1 - other), is_used[1:2])
    here = down == jnp.where(listed_here > 0, place, -1)
    found = lookup(jnp.where(list_row == 0, lane // 16, lane % 16), jnp.where(here, 1.0, 0.0))
    ordered = found[0:1] * 16 + found[1:2]
    count = jnp.sum(is_used.astype(F32), axis=1, keepdims=True).astype(I32)
    first_end = (count[0:1] - (me & 1) + 1) // 2
    ends = jnp.where(one_lane == 0, first_end, capacity + count[1:2])
    listed = jnp.where(list_row == 0, ordered, jnp.where(list_row == 1, place, ends))
    listed_ref[...] = listed
    to_smem = pltpu.make_async_copy(listed_ref, list_ref, sems.at[len(pairs)])
    to_smem.start()
    copies[2].wait()
    position = lax.broadcasted_iota(I32, (1, directions), 1)
    band_size = jnp.ones((1, directions), I32)
    bands = off_ref.shape[0] - 1
    for d in range(bands):
        start, end = off_ref[d], off_ref[d + 1]
        band_size = jnp.where((position >= start) & (position < end), end - start, band_size)
    weight = directions / (bands * band_size.astype(F32))
    copies[3].wait()
    weighted_ref[...] = (recv_ref[...].astype(F32) * weight).astype(BF16)
    copies[4].wait()
    rows_ref[...] = table_ref[...].astype(F32)
    to_smem.wait()
    copies[5].wait()
    fill_operators(0, list_ref[2, 0], list_ref, rows_ref, weighted_ref, rad_ref, t_ref)


def second_kernel(
    second_end,
    empty,
    near_shift,
    list_ref,
    rows_ref,
    weighted_ref,
    rad_ref,
    near_src_ref,
    near_src_other_ref,
    near_hbm,
    near_other_hbm,
    low_ref,
    t_ref,
    near_ref,
    near_map_ref,
    sems,
):
    boxes, near_slots = near_hbm.shape[1:3]
    copies = []
    for i, array in enumerate((near_hbm, near_other_hbm)):
        for j in range(boxes):
            row = i * boxes + j
            copies.append(
                pltpu.make_async_copy(array.at[0, j], near_ref.at[row, pl.ds(0, near_slots)], sems.at[row])
            )
            copies[-1].start()
    first_count = low_ref.shape[0]
    copies.append(pltpu.make_async_copy(low_ref, t_ref.at[pl.ds(0, first_count)], sems.at[2 * boxes]))
    copies[-1].start()
    t_ref[empty] = jnp.zeros(t_ref.shape[1:], BF16)
    for row in range(2 * boxes):
        near_ref[row, near_slots] = jnp.zeros(near_ref.shape[2:], BF16)
    width = near_map_ref.shape[1]
    near_at = lax.broadcasted_iota(I32, (width, near_slots), 0)
    row_at = lax.broadcasted_iota(I32, (ROWS, near_slots), 0)
    lane_at = lax.broadcasted_iota(I32, (ROWS, near_slots), 1)
    out_row = lax.broadcasted_iota(I32, near_map_ref.shape, 0)
    near_map = jnp.full(near_map_ref.shape, near_slots, I32)
    for j in range(2 * boxes):
        near = (near_src_ref if j < boxes else near_src_other_ref)[j % boxes]
        found = lookup(jnp.where(row_at == 0, lane_at, 1), jnp.where((near_at == near + near_shift) & (near >= 0), 1.0, 0.0))
        value = jnp.where(found[1:2] > 0, found[0:1], near_slots)
        near_map = jnp.where(out_row == j, value, near_map)
    near_map_ref[...] = near_map
    end = jnp.minimum(list_ref[2, 1], second_end)
    fill_operators(first_count, end, list_ref, rows_ref, weighted_ref, rad_ref, t_ref)
    for copy in copies:
        copy.wait()


def add_products(places, first_row, boxes, halo, cls_ref, near_map_ref, list_ref, t_ref, near_ref, source_refs, start, store):
    me = lax.axis_index("dir")
    region_boxes = boxes * lax.axis_size("dir")
    bases, groups, at = [], [], 0
    for rim, mask, parts in places:
        groups.append(source_refs[at : at + parts])
        at += parts
        owner = me ^ mask
        base = owner * boxes + halo
        if rim:
            base = base + jnp.where(owner * boxes >= halo, -region_boxes, region_boxes)
        bases.append(base)
    for j in range(boxes):
        row = first_row + j
        total = start(j)
        for base, refs in zip(bases, groups):
            blocks = []
            for b in range(boxes):
                n = list_ref[1, cls_ref[row, base + b]]
                blocks.append(t_ref[n] + near_ref[row, near_map_ref[row, base + b]])
            values = [ref[...].reshape(-1, ref.shape[-1]) for ref in refs]
            rhs = values[0] if len(values) == 1 else jnp.concatenate(values, 0)
            added = jnp.dot(jnp.concatenate(blocks, 1), rhs, preferred_element_type=F32)
            total = added if total is None else total + added
        store(j, total)


def third_kernel(
    second_end,
    empty,
    places,
    early,
    boxes,
    halo,
    list_ref,
    cls_ref,
    near_map_ref,
    rows_ref,
    weighted_ref,
    rad_ref,
    near_ref,
    low_ref,
    *rest,
):
    source_count = sum(parts for _, _, parts in places)
    source_refs, (_, t_ref, other_ref, own_ref, sem) = rest[:source_count], rest[source_count:]
    copy = pltpu.make_async_copy(low_ref, t_ref.at[pl.ds(empty + 1, low_ref.shape[0])], sem)
    copy.start()
    fill_operators(second_end, list_ref[2, 1], list_ref, rows_ref, weighted_ref, rad_ref, t_ref)
    copy.wait()

    def store_other(j, total):
        other_ref[j] = total.astype(other_ref.dtype)

    def store_own(j, total):
        own_ref[j] = total

    refs = (cls_ref, near_map_ref, list_ref, t_ref, near_ref)
    add_products(places, boxes, boxes, halo, *refs, source_refs, lambda j: None, store_other)
    add_products(places[:early], 0, boxes, halo, *refs, source_refs, lambda j: None, store_own)


def apply_kernel(
    places, first_row, boxes, halo, with_total, with_other, cls_ref, near_map_ref, list_ref, t_ref, near_ref, *rest
):
    source_count = sum(parts for _, _, parts in places)
    source_refs, rest = rest[:source_count], rest[source_count:]
    if with_total:
        sum_ref, *rest = rest
    if with_other:
        other_ref, *rest = rest
    (out_ref,) = rest

    def start(j):
        total = sum_ref[j] if with_total else None
        if with_other:
            other = other_ref[j].astype(F32)
            total = other if total is None else total + other
        return total

    def store(j, total):
        if len(out_ref.shape) == 4:
            out_ref[0, j] = total.astype(out_ref.dtype)
        else:
            out_ref[j] = total.astype(out_ref.dtype)

    refs = (cls_ref, near_map_ref, list_ref, t_ref, near_ref)
    add_products(places, first_row, boxes, halo, *refs, source_refs, start, store)


def shards(
    currents,
    radiate,
    receive,
    transfer_table,
    near_blocks,
    dir_offsets,
    trans_src,
    trans_tid,
    near_src,
):
    dir_count = lax.axis_size("dir")
    region_count = lax.axis_size("region")
    own = currents[0]
    boxes, unknowns, incidences = own.shape
    near_slots = near_src.shape[2]
    near_src = near_src.reshape(boxes, 1, near_slots)
    region_boxes = boxes * dir_count
    halo = region_boxes // 2
    near_halo = region_boxes // 4
    classes, directions = transfer_table.shape
    shared = classes // 2
    capacity = (shared + 1) // 2
    empty = capacity + classes - shared
    second_end = capacity + pad_to(classes // 5, UNROLL)
    top = dir_count // 2
    inner = range(2, top, 2)
    targets = 2 * boxes

    def partner(array, mask):
        return lax.ppermute(array, "dir", [(i, i ^ mask) for i in range(dir_count)])

    along = []
    for i in range(dir_count):
        for z in range(region_count):
            target = z + 1 if i >= top else z - 1
            if 0 <= target < region_count:
                along.append((i * region_count + z, i * region_count + target))

    def beyond(array):
        return lax.ppermute(array, ("dir", "region"), along)

    def pinned(array):
        return pltpu.with_memory_space_constraint(array, pltpu.VMEM)

    def in_hbm(array):
        return pltpu.with_memory_space_constraint(array, pltpu.HBM)

    width = pad_to(region_boxes + 2 * halo, LANES)
    map_shape = (pad_to(targets, ROWS), width)
    table_shape = (empty + 1 + capacity, unknowns, unknowns)
    low_shape = (capacity, unknowns, unknowns)
    list_shape = (ROWS, pad_to(classes + 1, LANES))
    vmem, smem, hbm = whole(pltpu.VMEM), whole(pltpu.SMEM), whole(pltpu.HBM)
    operator_cost = pl.CostEstimate(
        flops=classes * unknowns * unknowns * directions, bytes_accessed=MIB, transcendentals=0
    )

    field = {0: own}
    rim = {}
    for m in inner:
        field[m] = partner(own, m)
    field[top] = partner(own, top)
    rim[0] = beyond(own)
    near_other = partner(near_blocks, 1)
    near_src_other = partner(near_src, 1)
    low, weighted, rad_here, rows, cls, listed = pl.pallas_call(
        functools.partial(first_kernel, shared, boxes, halo, region_boxes),
        in_specs=[hbm] * 6,
        out_specs=[vmem] * 6,
        out_shape=(
            pltpu.VMEM(low_shape, BF16),
            pltpu.VMEM((unknowns, directions), BF16),
            pltpu.VMEM((directions, unknowns), BF16),
            pltpu.VMEM((classes, directions), F32),
            pltpu.VMEM(map_shape, I32),
            pltpu.VMEM(list_shape, I32),
        ),
        scratch_shapes=[
            pltpu.SMEM(dir_offsets.shape, I32),
            pltpu.VMEM(trans_src.shape, I32),
            pltpu.VMEM(trans_tid.shape, I32),
            pltpu.VMEM(transfer_table.shape, BF16),
            pltpu.VMEM(receive.shape, BF16),
            pltpu.SMEM(list_shape, I32),
            pltpu.SemaphoreType.DMA((7,)),
        ],
        compiler_params=pltpu.CompilerParams(vmem_limit_bytes=8 * MIB),
        cost_estimate=operator_cost,
    )(*[in_hbm(a) for a in (dir_offsets, trans_src, trans_tid, transfer_table, receive, radiate)])

    tied = lax.optimization_barrier((low, [field[m] for m in inner], field[top], rim[0]))
    low, inner_fields, field[top], rim[0] = tied
    for m, value in zip(inner, inner_fields):
        field[m] = value
    low, near_other, near_src_other = lax.optimization_barrier((low, near_other, near_src_other))
    low_other = partner(low, 1)
    for m in inner:
        field[top + m] = partner(field[top], m)
    rim[top] = partner(rim[0], top)
    for m in inner:
        rim[m] = beyond(field[m])

    table, near_here, near_map = pl.pallas_call(
        functools.partial(second_kernel, second_end, empty, halo - near_halo),
        in_specs=[smem] + [vmem] * 5 + [hbm] * 2 + [vmem],
        out_specs=[vmem] * 3,
        out_shape=(
            pltpu.VMEM(table_shape, BF16),
            pltpu.VMEM((targets, near_slots + 1, unknowns, unknowns), BF16),
            pltpu.VMEM(map_shape, I32),
        ),
        scratch_shapes=[pltpu.SemaphoreType.DMA((targets + 1,))],
        compiler_params=pltpu.CompilerParams(vmem_limit_bytes=8 * MIB),
        cost_estimate=operator_cost,
    )(
        listed,
        pinned(rows),
        pinned(weighted),
        pinned(rad_here),
        near_src,
        near_src_other,
        in_hbm(near_blocks),
        near_other,
        pinned(low),
    )

    def apply(places, first_row, total, other, dtype, shape):
        if len(places) > GROUP:
            total = apply(places[:GROUP], first_row, total, None, F32, full)
            return apply(places[GROUP:], first_row, total, other, dtype, shape)
        args = [cls, near_map, listed, pinned(table), pinned(near_here)] + [pinned(part) for _, _, parts in places for part in parts]
        args += [pinned(extra) for extra in (total, other) if extra is not None]
        specs = [smem] * 3 + [vmem] * (len(args) - 3)
        layout = [(outside, mask, len(parts)) for outside, mask, parts in places]
        kernel = functools.partial(
            apply_kernel, layout, first_row, boxes, halo, total is not None, other is not None
        )
        return pl.pallas_call(
            kernel,
            in_specs=specs,
            out_specs=vmem,
            out_shape=pltpu.VMEM(shape, dtype) if len(shape) == 3 else jax.ShapeDtypeStruct(shape, dtype),
            compiler_params=pltpu.CompilerParams(vmem_limit_bytes=12 * MIB),
            cost_estimate=pl.CostEstimate(flops=MIB, bytes_accessed=MIB, transcendentals=0),
        )(*args)

    table, inner_rims = lax.optimization_barrier((table, [rim[m] for m in inner]))
    for m, value in zip(inner, inner_rims):
        rim[m] = value
    last = {m: partner(rim[m], top) for m in inner}

    full = (boxes, unknowns, incidences)
    early = [(False, m, [field[m]]) for m in (0, *inner, top)] + [(True, 0, [rim[0]])]
    middle = [(False, top + m, [field[top + m]]) for m in inner]
    middle += [(True, m, [rim[m]]) for m in (*inner, top)]
    ready = (early + middle)[:GROUP]
    left = (early + middle)[GROUP:]
    count = min(len(early), GROUP)
    table, for_other, total = pl.pallas_call(
        functools.partial(
            third_kernel, second_end, empty, [(outside, mask, 1) for outside, mask, _ in ready], count, boxes, halo
        ),
        in_specs=[smem] * 3 + [vmem] * (6 + len(ready)),
        out_specs=[vmem] * 3,
        out_shape=(
            pltpu.VMEM(table_shape, BF16),
            pltpu.VMEM(full, F32 if left else BF16),
            pltpu.VMEM(full, F32),
        ),
        input_output_aliases={8 + len(ready): 0},
        scratch_shapes=[pltpu.SemaphoreType.DMA],
        compiler_params=pltpu.CompilerParams(vmem_limit_bytes=12 * MIB),
        cost_estimate=pl.CostEstimate(flops=MIB, bytes_accessed=MIB, transcendentals=0),
    )(
        listed,
        cls,
        near_map,
        *[pinned(a) for a in (rows, weighted, rad_here, near_here, low_other, *[parts[0] for _, _, parts in ready], table)],
    )
    if left:
        for_other = apply(left, boxes, for_other, None, BF16, full)
    from_other = partner(for_other, 1)

    total, last = lax.optimization_barrier((total, last))
    turned = {m: partner(last[m], 1) for m in inner}
    total = apply((early + middle)[count:], 0, total, None, F32, full)
    late = [(True, top + m, [last[m]]) for m in inner]
    late += [(True, top + m + 1, [turned[m]]) for m in inner]
    return apply(late, 0, total, from_other, BF16, currents.shape)


def solution(mesh):
    placed = (
        P("region", "dir", None, None),
        P(),
        P(),
        P(),
        P("region", "dir", None, None, None),
        P(),
        P("region", None, None),
        P("region", None, None),
        P("region", "dir", None),
    )
    return jax.shard_map(
        shards,
        mesh=mesh,
        in_specs=placed,
        out_specs=P("region", "dir", None, None),
        check_vma=False,
    )
```

```python
import functools

import jax
import jax.numpy as jnp
from jax import lax
from jax.experimental import pallas as pl
from jax.experimental.pallas import tpu as pltpu
from jax.sharding import PartitionSpec as P

BF16, F32, I32 = jnp.bfloat16, jnp.float32, jnp.int32
NT_DIMS = (((1,), (1,)), ((), ()))
LANES = 128
ROWS = 8
UNROLL = 16
TAIL = 4
GROUP = 8
MIB = 2**20


def pad_to(size, tile):
    return -(-size // tile) * tile


def whole(memory_space):
    return pl.BlockSpec(memory_space=memory_space)


def lookup(parts, hot):
    return lax.dot_general(parts.astype(F32).astype(BF16), hot.astype(BF16), NT_DIMS, preferred_element_type=F32).astype(I32)


def fill_operators(begin, end, list_ref, rows_ref, weighted_ref, rad_ref, out_ref):
    def step(at, wide):
        for u in range(wide):
            place = jnp.minimum(at + u, end - 1)
            row = rows_ref[pl.ds(list_ref[0, place], 1), :].astype(BF16)
            product = weighted_ref[...] * row
            out_ref[place] = jnp.dot(product, rad_ref[...], preferred_element_type=F32).astype(BF16)

    def main_step(i, carry):
        step(begin + i * UNROLL, UNROLL)
        return carry

    def tail_step(i, carry):
        step(begin + main * UNROLL + i * TAIL, TAIL)
        return carry

    count = jnp.maximum(end - begin, 0)
    main = count // UNROLL
    lax.fori_loop(0, main, main_step, 0)
    lax.fori_loop(0, (count - main * UNROLL + TAIL - 1) // TAIL, tail_step, 0)


def first_kernel(
    shared,
    boxes,
    halo,
    region_boxes,
    off_hbm,
    src_hbm,
    tid_hbm,
    table_hbm,
    recv_hbm,
    rad_hbm,
    t_ref,
    weighted_ref,
    rad_ref,
    rows_ref,
    cls_ref,
    listed_ref,
    off_ref,
    src_ref,
    tid_ref,
    table_ref,
    recv_ref,
    list_ref,
    sems,
):
    pairs = [
        (src_hbm, src_ref),
        (tid_hbm, tid_ref),
        (off_hbm, off_ref),
        (recv_hbm, recv_ref),
        (table_hbm, table_ref),
        (rad_hbm, rad_ref),
    ]
    copies = [pltpu.make_async_copy(a, b, sems.at[i]) for i, (a, b) in enumerate(pairs)]
    for copy in copies:
        copy.start()
    classes = table_ref.shape[0]
    directions = recv_ref.shape[1]
    me = lax.axis_index("dir")
    dir_count = region_boxes // boxes
    top = dir_count // 2
    slots = src_ref.shape[2]
    width = cls_ref.shape[1]
    used_width = listed_ref.shape[1]
    ext_at = lax.broadcasted_iota(I32, (width, slots), 0)
    class_at = lax.broadcasted_iota(I32, (used_width, slots), 0)
    row_at = lax.broadcasted_iota(I32, (ROWS, slots), 0)
    out_row = lax.broadcasted_iota(I32, cls_ref.shape, 0)
    seen = jnp.zeros((used_width, slots), F32)
    cls = jnp.full(cls_ref.shape, classes, I32)
    copies[0].wait()
    copies[1].wait()
    for j in range(2 * boxes):
        target = (me if j < boxes else me ^ 1) * boxes + j % boxes
        src = src_ref[0, pl.ds(target, 1), :]
        tid = tid_ref[0, pl.ds(target, 1), :]
        mask = (((src - halo + region_boxes) // boxes) % dir_count) ^ me
        beyond = (src < halo) | (src >= halo + region_boxes)
        late = beyond & ((mask & top) != 0) & ((mask & (top - 2)) != 0)
        even = (mask & 1) == 0
        here = (src >= 0) & ((even | late) if j < boxes else (even & ~late))
        seen = jnp.maximum(seen, jnp.where(class_at == tid, jnp.where(here, 2.0, jnp.where(src >= 0, 1.0, 0.0)), 0.0))
        parts = jnp.where(row_at == 0, tid // 16, jnp.where(row_at == 1, tid % 16, 1))
        found = lookup(parts, jnp.where(ext_at == src, 1.0, 0.0))
        value = jnp.where(found[2:3] > 0, found[0:1] * 16 + found[1:2], classes)
        cls = jnp.where(out_row == j, value, cls)
    cls_ref[...] = cls
    lane = lax.broadcasted_iota(I32, (ROWS, used_width), 1)
    list_row = lax.broadcasted_iota(I32, (ROWS, used_width), 0)
    ones = jnp.ones((ROWS, slots), I32)
    by_chip = jnp.where(lane < shared, jnp.minimum(lookup(ones, jnp.where(seen > 0.0, 1.0, 0.0)), 1), 0)
    by_core = jnp.where(lane >= shared, jnp.minimum(lookup(ones, jnp.where(seen > 1.0, 1.0, 0.0)), 1), 0)
    is_used = jnp.where(list_row == 0, by_chip, by_core)
    down = lax.broadcasted_iota(I32, (used_width, used_width), 0)
    across = lax.broadcasted_iota(I32, (used_width, used_width), 1)
    rank = lookup(is_used, jnp.where(across < down, 1.0, 0.0))
    shared_rank, own_rank = rank[0:1], rank[1:2]
    one_lane = lane[0:1]
    capacity = (shared + 1) // 2
    empty = capacity + classes - shared
    other = (shared_rank ^ me) & 1
    shared_place = shared_rank // 2 + other * (empty + 1)
    place = jnp.where(one_lane < shared, shared_place, capacity + own_rank)
    place = jnp.where(one_lane == classes, empty, place)
    listed_here = jnp.where(one_lane < shared, is_used[0:1] * (1 - other), is_used[1:2])
    here = down == jnp.where(listed_here > 0, place, -1)
    found = lookup(jnp.where(list_row == 0, lane // 16, lane % 16), jnp.where(here, 1.0, 0.0))
    ordered = found[0:1] * 16 + found[1:2]
    count = jnp.sum(is_used.astype(F32), axis=1, keepdims=True).astype(I32)
    first_end = (count[0:1] - (me & 1) + 1) // 2
    ends = jnp.where(one_lane == 0, first_end, capacity + count[1:2])
    listed = jnp.where(list_row == 0, ordered, jnp.where(list_row == 1, place, ends))
    listed_ref[...] = listed
    to_smem = pltpu.make_async_copy(listed_ref, list_ref, sems.at[len(pairs)])
    to_smem.start()
    copies[2].wait()
    position = lax.broadcasted_iota(I32, (1, directions), 1)
    band_size = jnp.ones((1, directions), I32)
    bands = off_ref.shape[0] - 1
    for d in range(bands):
        start, end = off_ref[d], off_ref[d + 1]
        band_size = jnp.where((position >= start) & (position < end), end - start, band_size)
    weight = directions / (bands * band_size.astype(F32))
    copies[3].wait()
    weighted_ref[...] = (recv_ref[...].astype(F32) * weight).astype(BF16)
    copies[4].wait()
    rows_ref[...] = table_ref[...].astype(F32)
    to_smem.wait()
    copies[5].wait()
    fill_operators(0, list_ref[2, 0], list_ref, rows_ref, weighted_ref, rad_ref, t_ref)


def second_kernel(
    second_end,
    empty,
    near_shift,
    list_ref,
    rows_ref,
    weighted_ref,
    rad_ref,
    near_src_ref,
    near_src_other_ref,
    near_hbm,
    near_other_hbm,
    low_ref,
    t_ref,
    near_ref,
    near_map_ref,
    sems,
):
    boxes, near_slots = near_hbm.shape[1:3]
    copies = []
    for i, array in enumerate((near_hbm, near_other_hbm)):
        for j in range(boxes):
            row = i * boxes + j
            copies.append(
                pltpu.make_async_copy(array.at[0, j], near_ref.at[row, pl.ds(0, near_slots)], sems.at[row])
            )
            copies[-1].start()
    first_count = low_ref.shape[0]
    copies.append(pltpu.make_async_copy(low_ref, t_ref.at[pl.ds(0, first_count)], sems.at[2 * boxes]))
    copies[-1].start()
    t_ref[empty] = jnp.zeros(t_ref.shape[1:], BF16)
    for row in range(2 * boxes):
        near_ref[row, near_slots] = jnp.zeros(near_ref.shape[2:], BF16)
    width = near_map_ref.shape[1]
    near_at = lax.broadcasted_iota(I32, (width, near_slots), 0)
    row_at = lax.broadcasted_iota(I32, (ROWS, near_slots), 0)
    lane_at = lax.broadcasted_iota(I32, (ROWS, near_slots), 1)
    out_row = lax.broadcasted_iota(I32, near_map_ref.shape, 0)
    near_map = jnp.full(near_map_ref.shape, near_slots, I32)
    for j in range(2 * boxes):
        near = (near_src_ref if j < boxes else near_src_other_ref)[j % boxes]
        found = lookup(jnp.where(row_at == 0, lane_at, 1), jnp.where((near_at == near + near_shift) & (near >= 0), 1.0, 0.0))
        value = jnp.where(found[1:2] > 0, found[0:1], near_slots)
        near_map = jnp.where(out_row == j, value, near_map)
    near_map_ref[...] = near_map
    end = jnp.minimum(list_ref[2, 1], second_end)
    fill_operators(first_count, end, list_ref, rows_ref, weighted_ref, rad_ref, t_ref)
    for copy in copies:
        copy.wait()


def add_products(places, first_row, boxes, halo, cls_ref, near_map_ref, list_ref, t_ref, near_ref, source_refs, start, store):
    me = lax.axis_index("dir")
    region_boxes = boxes * lax.axis_size("dir")
    bases, groups, at = [], [], 0
    for rim, mask, parts in places:
        groups.append(source_refs[at : at + parts])
        at += parts
        owner = me ^ mask
        base = owner * boxes + halo
        if rim:
            base = base + jnp.where(owner * boxes >= halo, -region_boxes, region_boxes)
        bases.append(base)
    for j in range(boxes):
        row = first_row + j
        total = start(j)
        for base, refs in zip(bases, groups):
            blocks = []
            for b in range(boxes):
                n = list_ref[1, cls_ref[row, base + b]]
                blocks.append(t_ref[n] + near_ref[row, near_map_ref[row, base + b]])
            values = [ref[...].reshape(-1, ref.shape[-1]) for ref in refs]
            rhs = values[0] if len(values) == 1 else jnp.concatenate(values, 0)
            added = jnp.dot(jnp.concatenate(blocks, 1), rhs, preferred_element_type=F32)
            total = added if total is None else total + added
        store(j, total)


def third_kernel(
    second_end,
    empty,
    places,
    early,
    boxes,
    halo,
    list_ref,
    cls_ref,
    near_map_ref,
    rows_ref,
    weighted_ref,
    rad_ref,
    near_ref,
    low_ref,
    *rest,
):
    source_count = sum(parts for _, _, parts in places)
    source_refs, (_, t_ref, other_ref, own_ref, sem) = rest[:source_count], rest[source_count:]
    copy = pltpu.make_async_copy(low_ref, t_ref.at[pl.ds(empty + 1, low_ref.shape[0])], sem)
    copy.start()
    fill_operators(second_end, list_ref[2, 1], list_ref, rows_ref, weighted_ref, rad_ref, t_ref)
    copy.wait()

    def store_other(j, total):
        other_ref[j] = total.astype(other_ref.dtype)

    def store_own(j, total):
        own_ref[j] = total

    refs = (cls_ref, near_map_ref, list_ref, t_ref, near_ref)
    add_products(places, boxes, boxes, halo, *refs, source_refs, lambda j: None, store_other)
    add_products(places[:early], 0, boxes, halo, *refs, source_refs, lambda j: None, store_own)


def apply_kernel(
    places, first_row, boxes, halo, with_total, with_other, cls_ref, near_map_ref, list_ref, t_ref, near_ref, *rest
):
    source_count = sum(parts for _, _, parts in places)
    source_refs, rest = rest[:source_count], rest[source_count:]
    if with_total:
        sum_ref, *rest = rest
    if with_other:
        other_ref, *rest = rest
    (out_ref,) = rest

    def start(j):
        total = sum_ref[j] if with_total else None
        if with_other:
            other = other_ref[j].astype(F32)
            total = other if total is None else total + other
        return total

    def store(j, total):
        if len(out_ref.shape) == 4:
            out_ref[0, j] = total.astype(out_ref.dtype)
        else:
            out_ref[j] = total.astype(out_ref.dtype)

    refs = (cls_ref, near_map_ref, list_ref, t_ref, near_ref)
    add_products(places, first_row, boxes, halo, *refs, source_refs, start, store)


def shards(
    currents,
    radiate,
    receive,
    transfer_table,
    near_blocks,
    dir_offsets,
    trans_src,
    trans_tid,
    near_src,
):
    dir_count = lax.axis_size("dir")
    region_count = lax.axis_size("region")
    own = currents[0]
    boxes, unknowns, incidences = own.shape
    near_slots = near_src.shape[2]
    near_src = near_src.reshape(boxes, 1, near_slots)
    region_boxes = boxes * dir_count
    halo = region_boxes // 2
    near_halo = region_boxes // 4
    classes, directions = transfer_table.shape
    shared = classes // 2
    capacity = (shared + 1) // 2
    empty = capacity + classes - shared
    second_end = capacity + pad_to(classes // 8, UNROLL)
    top = dir_count // 2
    inner = range(2, top, 2)
    targets = 2 * boxes

    def partner(array, mask):
        return lax.ppermute(array, "dir", [(i, i ^ mask) for i in range(dir_count)])

    along = []
    for i in range(dir_count):
        for z in range(region_count):
            target = z + 1 if i >= top else z - 1
            if 0 <= target < region_count:
                along.append((i * region_count + z, i * region_count + target))

    def beyond(array):
        return lax.ppermute(array, ("dir", "region"), along)

    def pinned(array):
        return pltpu.with_memory_space_constraint(array, pltpu.VMEM)

    def in_hbm(array):
        return pltpu.with_memory_space_constraint(array, pltpu.HBM)

    width = pad_to(region_boxes + 2 * halo, LANES)
    map_shape = (pad_to(targets, ROWS), width)
    table_shape = (empty + 1 + capacity, unknowns, unknowns)
    low_shape = (capacity, unknowns, unknowns)
    list_shape = (ROWS, pad_to(classes + 1, LANES))
    vmem, smem, hbm = whole(pltpu.VMEM), whole(pltpu.SMEM), whole(pltpu.HBM)
    operator_cost = pl.CostEstimate(
        flops=classes * unknowns * unknowns * directions, bytes_accessed=MIB, transcendentals=0
    )

    field = {0: own}
    rim = {}
    for m in inner:
        field[m] = partner(own, m)
    field[top] = partner(own, top)
    rim[0] = beyond(own)
    near_other = partner(near_blocks, 1)
    near_src_other = partner(near_src, 1)
    low, weighted, rad_here, rows, cls, listed = pl.pallas_call(
        functools.partial(first_kernel, shared, boxes, halo, region_boxes),
        in_specs=[hbm] * 6,
        out_specs=[vmem] * 6,
        out_shape=(
            pltpu.VMEM(low_shape, BF16),
            pltpu.VMEM((unknowns, directions), BF16),
            pltpu.VMEM((directions, unknowns), BF16),
            pltpu.VMEM((classes, directions), F32),
            pltpu.VMEM(map_shape, I32),
            pltpu.VMEM(list_shape, I32),
        ),
        scratch_shapes=[
            pltpu.SMEM(dir_offsets.shape, I32),
            pltpu.VMEM(trans_src.shape, I32),
            pltpu.VMEM(trans_tid.shape, I32),
            pltpu.VMEM(transfer_table.shape, BF16),
            pltpu.VMEM(receive.shape, BF16),
            pltpu.SMEM(list_shape, I32),
            pltpu.SemaphoreType.DMA((7,)),
        ],
        compiler_params=pltpu.CompilerParams(vmem_limit_bytes=8 * MIB),
        cost_estimate=operator_cost,
    )(*[in_hbm(a) for a in (dir_offsets, trans_src, trans_tid, transfer_table, receive, radiate)])

    tied = lax.optimization_barrier((low, [field[m] for m in inner], field[top], rim[0]))
    low, inner_fields, field[top], rim[0] = tied
    for m, value in zip(inner, inner_fields):
        field[m] = value
    low, near_other, near_src_other = lax.optimization_barrier((low, near_other, near_src_other))
    low_other = partner(low, 1)
    for m in inner:
        field[top + m] = partner(field[top], m)
    rim[top] = partner(rim[0], top)
    for m in inner:
        rim[m] = beyond(field[m])

    table, near_here, near_map = pl.pallas_call(
        functools.partial(second_kernel, second_end, empty, halo - near_halo),
        in_specs=[smem] + [vmem] * 5 + [hbm] * 2 + [vmem],
        out_specs=[vmem] * 3,
        out_shape=(
            pltpu.VMEM(table_shape, BF16),
            pltpu.VMEM((targets, near_slots + 1, unknowns, unknowns), BF16),
            pltpu.VMEM(map_shape, I32),
        ),
        scratch_shapes=[pltpu.SemaphoreType.DMA((targets + 1,))],
        compiler_params=pltpu.CompilerParams(vmem_limit_bytes=8 * MIB),
        cost_estimate=operator_cost,
    )(
        listed,
        pinned(rows),
        pinned(weighted),
        pinned(rad_here),
        near_src,
        near_src_other,
        in_hbm(near_blocks),
        near_other,
        pinned(low),
    )

    def apply(places, first_row, total, other, dtype, shape):
        if len(places) > GROUP:
            total = apply(places[:GROUP], first_row, total, None, F32, full)
            return apply(places[GROUP:], first_row, total, other, dtype, shape)
        args = [cls, near_map, listed, pinned(table), pinned(near_here)] + [pinned(part) for _, _, parts in places for part in parts]
        args += [pinned(extra) for extra in (total, other) if extra is not None]
        specs = [smem] * 3 + [vmem] * (len(args) - 3)
        layout = [(outside, mask, len(parts)) for outside, mask, parts in places]
        kernel = functools.partial(
            apply_kernel, layout, first_row, boxes, halo, total is not None, other is not None
        )
        return pl.pallas_call(
            kernel,
            in_specs=specs,
            out_specs=vmem,
            out_shape=pltpu.VMEM(shape, dtype) if len(shape) == 3 else jax.ShapeDtypeStruct(shape, dtype),
            compiler_params=pltpu.CompilerParams(vmem_limit_bytes=12 * MIB),
            cost_estimate=pl.CostEstimate(flops=MIB, bytes_accessed=MIB, transcendentals=0),
        )(*args)

    table, inner_rims = lax.optimization_barrier((table, [rim[m] for m in inner]))
    for m, value in zip(inner, inner_rims):
        rim[m] = value
    last = {m: partner(rim[m], top) for m in inner}

    full = (boxes, unknowns, incidences)
    early = [(False, m, [field[m]]) for m in (0, *inner, top)] + [(True, 0, [rim[0]])]
    middle = [(False, top + m, [field[top + m]]) for m in inner]
    middle += [(True, m, [rim[m]]) for m in (*inner, top)]
    ready = (early + middle)[:GROUP]
    left = (early + middle)[GROUP:]
    count = min(len(early), GROUP)
    table, for_other, total = pl.pallas_call(
        functools.partial(
            third_kernel, second_end, empty, [(outside, mask, 1) for outside, mask, _ in ready], count, boxes, halo
        ),
        in_specs=[smem] * 3 + [vmem] * (6 + len(ready)),
        out_specs=[vmem] * 3,
        out_shape=(
            pltpu.VMEM(table_shape, BF16),
            pltpu.VMEM(full, F32 if left else BF16),
            pltpu.VMEM(full, F32),
        ),
        input_output_aliases={8 + len(ready): 0},
        scratch_shapes=[pltpu.SemaphoreType.DMA],
        compiler_params=pltpu.CompilerParams(vmem_limit_bytes=12 * MIB),
        cost_estimate=pl.CostEstimate(flops=MIB, bytes_accessed=MIB, transcendentals=0),
    )(
        listed,
        cls,
        near_map,
        *[pinned(a) for a in (rows, weighted, rad_here, near_here, low_other, *[parts[0] for _, _, parts in ready], table)],
    )
    if left:
        for_other = apply(left, boxes, for_other, None, BF16, full)
    from_other = partner(for_other, 1)

    total, last = lax.optimization_barrier((total, last))
    turned = {m: partner(last[m], 1) for m in inner}
    total = apply((early + middle)[count:], 0, total, None, F32, full)
    late = [(True, top + m, [last[m]]) for m in inner]
    late += [(True, top + m + 1, [turned[m]]) for m in inner]
    return apply(late, 0, total, from_other, BF16, currents.shape)


def solution(mesh):
    placed = (
        P("region", "dir", None, None),
        P(),
        P(),
        P(),
        P("region", "dir", None, None, None),
        P(),
        P("region", None, None),
        P("region", None, None),
        P("region", "dir", None),
    )
    return jax.shard_map(
        shards,
        mesh=mesh,
        in_specs=placed,
        out_specs=P("region", "dir", None, None),
        check_vma=False,
    )
```

```python
import functools

import jax
import jax.numpy as jnp
from jax import lax
from jax.experimental import pallas as pl
from jax.experimental.pallas import tpu as pltpu
from jax.sharding import PartitionSpec as P

BF16, F32, I32 = jnp.bfloat16, jnp.float32, jnp.int32
NT_DIMS = (((1,), (1,)), ((), ()))
LANES = 128
ROWS = 8
UNROLL = 16
TAIL = 4
GROUP = 8
MIB = 2**20


def pad_to(size, tile):
    return -(-size // tile) * tile


def whole(memory_space):
    return pl.BlockSpec(memory_space=memory_space)


def lookup(parts, hot):
    return lax.dot_general(parts.astype(F32).astype(BF16), hot.astype(BF16), NT_DIMS, preferred_element_type=F32).astype(I32)


def fill_operators(begin, end, list_ref, rows_ref, weighted_ref, rad_ref, out_ref):
    def step(at, wide):
        for u in range(wide):
            place = jnp.minimum(at + u, end - 1)
            row = rows_ref[pl.ds(list_ref[0, place], 1), :].astype(BF16)
            product = weighted_ref[...] * row
            out_ref[place] = jnp.dot(product, rad_ref[...], preferred_element_type=F32).astype(BF16)

    def main_step(i, carry):
        step(begin + i * UNROLL, UNROLL)
        return carry

    def tail_step(i, carry):
        step(begin + main * UNROLL + i * TAIL, TAIL)
        return carry

    count = jnp.maximum(end - begin, 0)
    main = count // UNROLL
    lax.fori_loop(0, main, main_step, 0)
    lax.fori_loop(0, (count - main * UNROLL + TAIL - 1) // TAIL, tail_step, 0)


def first_kernel(
    shared,
    boxes,
    halo,
    region_boxes,
    off_hbm,
    src_hbm,
    tid_hbm,
    table_hbm,
    recv_hbm,
    rad_hbm,
    t_ref,
    weighted_ref,
    rad_ref,
    rows_ref,
    cls_ref,
    listed_ref,
    off_ref,
    src_ref,
    tid_ref,
    table_ref,
    recv_ref,
    list_ref,
    sems,
):
    pairs = [
        (src_hbm, src_ref),
        (tid_hbm, tid_ref),
        (off_hbm, off_ref),
        (recv_hbm, recv_ref),
        (table_hbm, table_ref),
        (rad_hbm, rad_ref),
    ]
    copies = [pltpu.make_async_copy(a, b, sems.at[i]) for i, (a, b) in enumerate(pairs)]
    for copy in copies:
        copy.start()
    classes = table_ref.shape[0]
    directions = recv_ref.shape[1]
    me = lax.axis_index("dir")
    dir_count = region_boxes // boxes
    top = dir_count // 2
    slots = src_ref.shape[2]
    width = cls_ref.shape[1]
    used_width = listed_ref.shape[1]
    ext_at = lax.broadcasted_iota(I32, (width, slots), 0)
    class_at = lax.broadcasted_iota(I32, (used_width, slots), 0)
    row_at = lax.broadcasted_iota(I32, (ROWS, slots), 0)
    out_row = lax.broadcasted_iota(I32, cls_ref.shape, 0)
    seen = jnp.zeros((used_width, slots), F32)
    cls = jnp.full(cls_ref.shape, classes, I32)
    copies[0].wait()
    copies[1].wait()
    for j in range(2 * boxes):
        target = (me if j < boxes else me ^ 1) * boxes + j % boxes
        src = src_ref[0, pl.ds(target, 1), :]
        tid = tid_ref[0, pl.ds(target, 1), :]
        mask = (((src - halo + region_boxes) // boxes) % dir_count) ^ me
        beyond = (src < halo) | (src >= halo + region_boxes)
        late = beyond & ((mask & top) != 0) & ((mask & (top - 2)) != 0)
        even = (mask & 1) == 0
        here = (src >= 0) & ((even | late) if j < boxes else (even & ~late))
        seen = jnp.maximum(seen, jnp.where(class_at == tid, jnp.where(here, 2.0, jnp.where(src >= 0, 1.0, 0.0)), 0.0))
        parts = jnp.where(row_at == 0, tid // 16, jnp.where(row_at == 1, tid % 16, 1))
        found = lookup(parts, jnp.where(ext_at == src, 1.0, 0.0))
        value = jnp.where(found[2:3] > 0, found[0:1] * 16 + found[1:2], classes)
        cls = jnp.where(out_row == j, value, cls)
    cls_ref[...] = cls
    lane = lax.broadcasted_iota(I32, (ROWS, used_width), 1)
    list_row = lax.broadcasted_iota(I32, (ROWS, used_width), 0)
    ones = jnp.ones((ROWS, slots), I32)
    by_chip = jnp.where(lane < shared, jnp.minimum(lookup(ones, jnp.where(seen > 0.0, 1.0, 0.0)), 1), 0)
    by_core = jnp.where(lane >= shared, jnp.minimum(lookup(ones, jnp.where(seen > 1.0, 1.0, 0.0)), 1), 0)
    is_used = jnp.where(list_row == 0, by_chip, by_core)
    down = lax.broadcasted_iota(I32, (used_width, used_width), 0)
    across = lax.broadcasted_iota(I32, (used_width, used_width), 1)
    rank = lookup(is_used, jnp.where(across < down, 1.0, 0.0))
    shared_rank, own_rank = rank[0:1], rank[1:2]
    one_lane = lane[0:1]
    capacity = (shared + 1) // 2
    empty = capacity + classes - shared
    other = (shared_rank ^ me) & 1
    shared_place = shared_rank // 2 + other * (empty + 1)
    place = jnp.where(one_lane < shared, shared_place, capacity + own_rank)
    place = jnp.where(one_lane == classes, empty, place)
    listed_here = jnp.where(one_lane < shared, is_used[0:1] * (1 - other), is_used[1:2])
    here = down == jnp.where(listed_here > 0, place, -1)
    found = lookup(jnp.where(list_row == 0, lane // 16, lane % 16), jnp.where(here, 1.0, 0.0))
    ordered = found[0:1] * 16 + found[1:2]
    count = jnp.sum(is_used.astype(F32), axis=1, keepdims=True).astype(I32)
    first_end = (count[0:1] - (me & 1) + 1) // 2
    ends = jnp.where(one_lane == 0, first_end, capacity + count[1:2])
    listed = jnp.where(list_row == 0, ordered, jnp.where(list_row == 1, place, ends))
    listed_ref[...] = listed
    to_smem = pltpu.make_async_copy(listed_ref, list_ref, sems.at[len(pairs)])
    to_smem.start()
    copies[2].wait()
    position = lax.broadcasted_iota(I32, (1, directions), 1)
    band_size = jnp.ones((1, directions), I32)
    bands = off_ref.shape[0] - 1
    for d in range(bands):
        start, end = off_ref[d], off_ref[d + 1]
        band_size = jnp.where((position >= start) & (position < end), end - start, band_size)
    weight = directions / (bands * band_size.astype(F32))
    copies[3].wait()
    weighted_ref[...] = (recv_ref[...].astype(F32) * weight).astype(BF16)
    copies[4].wait()
    rows_ref[...] = table_ref[...].astype(F32)
    to_smem.wait()
    copies[5].wait()
    fill_operators(0, list_ref[2, 0], list_ref, rows_ref, weighted_ref, rad_ref, t_ref)


def second_kernel(
    second_end,
    empty,
    near_shift,
    list_ref,
    rows_ref,
    weighted_ref,
    rad_ref,
    near_src_ref,
    near_src_other_ref,
    near_hbm,
    near_other_hbm,
    low_ref,
    t_ref,
    near_ref,
    near_map_ref,
    sems,
):
    boxes, near_slots = near_hbm.shape[1:3]
    copies = []
    for i, array in enumerate((near_hbm, near_other_hbm)):
        for j in range(boxes):
            row = i * boxes + j
            copies.append(
                pltpu.make_async_copy(array.at[0, j], near_ref.at[row, pl.ds(0, near_slots)], sems.at[row])
            )
            copies[-1].start()
    first_count = low_ref.shape[0]
    copies.append(pltpu.make_async_copy(low_ref, t_ref.at[pl.ds(0, first_count)], sems.at[2 * boxes]))
    copies[-1].start()
    t_ref[empty] = jnp.zeros(t_ref.shape[1:], BF16)
    for row in range(2 * boxes):
        near_ref[row, near_slots] = jnp.zeros(near_ref.shape[2:], BF16)
    width = near_map_ref.shape[1]
    near_at = lax.broadcasted_iota(I32, (width, near_slots), 0)
    row_at = lax.broadcasted_iota(I32, (ROWS, near_slots), 0)
    lane_at = lax.broadcasted_iota(I32, (ROWS, near_slots), 1)
    out_row = lax.broadcasted_iota(I32, near_map_ref.shape, 0)
    near_map = jnp.full(near_map_ref.shape, near_slots, I32)
    for j in range(2 * boxes):
        near = (near_src_ref if j < boxes else near_src_other_ref)[j % boxes]
        found = lookup(jnp.where(row_at == 0, lane_at, 1), jnp.where((near_at == near + near_shift) & (near >= 0), 1.0, 0.0))
        value = jnp.where(found[1:2] > 0, found[0:1], near_slots)
        near_map = jnp.where(out_row == j, value, near_map)
    near_map_ref[...] = near_map
    end = jnp.minimum(list_ref[2, 1], second_end)
    fill_operators(first_count, end, list_ref, rows_ref, weighted_ref, rad_ref, t_ref)
    for copy in copies:
        copy.wait()


def add_products(places, first_row, boxes, halo, cls_ref, near_map_ref, list_ref, t_ref, near_ref, source_refs, start, store):
    me = lax.axis_index("dir")
    region_boxes = boxes * lax.axis_size("dir")
    bases, groups, at = [], [], 0
    for rim, mask, parts in places:
        groups.append(source_refs[at : at + parts])
        at += parts
        owner = me ^ mask
        base = owner * boxes + halo
        if rim:
            base = base + jnp.where(owner * boxes >= halo, -region_boxes, region_boxes)
        bases.append(base)
    for j in range(boxes):
        row = first_row + j
        total = start(j)
        for base, refs in zip(bases, groups):
            blocks = []
            for b in range(boxes):
                n = list_ref[1, cls_ref[row, base + b]]
                blocks.append(t_ref[n] + near_ref[row, near_map_ref[row, base + b]])
            values = [ref[...].reshape(-1, ref.shape[-1]) for ref in refs]
            rhs = values[0] if len(values) == 1 else jnp.concatenate(values, 0)
            added = jnp.dot(jnp.concatenate(blocks, 1), rhs, preferred_element_type=F32)
            total = added if total is None else total + added
        store(j, total)


def third_kernel(
    second_end,
    empty,
    places,
    early,
    boxes,
    halo,
    list_ref,
    cls_ref,
    near_map_ref,
    rows_ref,
    weighted_ref,
    rad_ref,
    near_ref,
    low_ref,
    *rest,
):
    source_count = sum(parts for _, _, parts in places)
    source_refs, (_, t_ref, other_ref, own_ref, sem) = rest[:source_count], rest[source_count:]
    copy = pltpu.make_async_copy(low_ref, t_ref.at[pl.ds(empty + 1, low_ref.shape[0])], sem)
    copy.start()
    fill_operators(second_end, list_ref[2, 1], list_ref, rows_ref, weighted_ref, rad_ref, t_ref)
    copy.wait()

    def store_other(j, total):
        other_ref[j] = total.astype(other_ref.dtype)

    def store_own(j, total):
        own_ref[j] = total

    refs = (cls_ref, near_map_ref, list_ref, t_ref, near_ref)
    add_products(places, boxes, boxes, halo, *refs, source_refs, lambda j: None, store_other)
    add_products(places[:early], 0, boxes, halo, *refs, source_refs, lambda j: None, store_own)


def apply_kernel(
    places, first_row, boxes, halo, with_total, with_other, cls_ref, near_map_ref, list_ref, t_ref, near_ref, *rest
):
    source_count = sum(parts for _, _, parts in places)
    source_refs, rest = rest[:source_count], rest[source_count:]
    if with_total:
        sum_ref, *rest = rest
    if with_other:
        other_ref, *rest = rest
    (out_ref,) = rest

    def start(j):
        total = sum_ref[j] if with_total else None
        if with_other:
            other = other_ref[j].astype(F32)
            total = other if total is None else total + other
        return total

    def store(j, total):
        if len(out_ref.shape) == 4:
            out_ref[0, j] = total.astype(out_ref.dtype)
        else:
            out_ref[j] = total.astype(out_ref.dtype)

    refs = (cls_ref, near_map_ref, list_ref, t_ref, near_ref)
    add_products(places, first_row, boxes, halo, *refs, source_refs, start, store)


def shards(
    currents,
    radiate,
    receive,
    transfer_table,
    near_blocks,
    dir_offsets,
    trans_src,
    trans_tid,
    near_src,
):
    dir_count = lax.axis_size("dir")
    region_count = lax.axis_size("region")
    own = currents[0]
    boxes, unknowns, incidences = own.shape
    near_slots = near_src.shape[2]
    near_src = near_src.reshape(boxes, 1, near_slots)
    region_boxes = boxes * dir_count
    halo = region_boxes // 2
    near_halo = region_boxes // 4
    classes, directions = transfer_table.shape
    shared = classes * 5 // 8
    capacity = (shared + 1) // 2
    empty = capacity + classes - shared
    second_end = capacity + pad_to(classes // 8, UNROLL)
    top = dir_count // 2
    inner = range(2, top, 2)
    targets = 2 * boxes

    def partner(array, mask):
        return lax.ppermute(array, "dir", [(i, i ^ mask) for i in range(dir_count)])

    along = []
    for i in range(dir_count):
        for z in range(region_count):
            target = z + 1 if i >= top else z - 1
            if 0 <= target < region_count:
                along.append((i * region_count + z, i * region_count + target))

    def beyond(array):
        return lax.ppermute(array, ("dir", "region"), along)

    def pinned(array):
        return pltpu.with_memory_space_constraint(array, pltpu.VMEM)

    def in_hbm(array):
        return pltpu.with_memory_space_constraint(array, pltpu.HBM)

    width = pad_to(region_boxes + 2 * halo, LANES)
    map_shape = (pad_to(targets, ROWS), width)
    table_shape = (empty + 1 + capacity, unknowns, unknowns)
    low_shape = (capacity, unknowns, unknowns)
    list_shape = (ROWS, pad_to(classes + 1, LANES))
    vmem, smem, hbm = whole(pltpu.VMEM), whole(pltpu.SMEM), whole(pltpu.HBM)
    operator_cost = pl.CostEstimate(
        flops=classes * unknowns * unknowns * directions, bytes_accessed=MIB, transcendentals=0
    )

    field = {0: own}
    rim = {}
    for m in inner:
        field[m] = partner(own, m)
    field[top] = partner(own, top)
    rim[0] = beyond(own)
    near_other = partner(near_blocks, 1)
    near_src_other = partner(near_src, 1)
    low, weighted, rad_here, rows, cls, listed = pl.pallas_call(
        functools.partial(first_kernel, shared, boxes, halo, region_boxes),
        in_specs=[hbm] * 6,
        out_specs=[vmem] * 6,
        out_shape=(
            pltpu.VMEM(low_shape, BF16),
            pltpu.VMEM((unknowns, directions), BF16),
            pltpu.VMEM((directions, unknowns), BF16),
            pltpu.VMEM((classes, directions), F32),
            pltpu.VMEM(map_shape, I32),
            pltpu.VMEM(list_shape, I32),
        ),
        scratch_shapes=[
            pltpu.SMEM(dir_offsets.shape, I32),
            pltpu.VMEM(trans_src.shape, I32),
            pltpu.VMEM(trans_tid.shape, I32),
            pltpu.VMEM(transfer_table.shape, BF16),
            pltpu.VMEM(receive.shape, BF16),
            pltpu.SMEM(list_shape, I32),
            pltpu.SemaphoreType.DMA((7,)),
        ],
        compiler_params=pltpu.CompilerParams(vmem_limit_bytes=8 * MIB),
        cost_estimate=operator_cost,
    )(*[in_hbm(a) for a in (dir_offsets, trans_src, trans_tid, transfer_table, receive, radiate)])

    tied = lax.optimization_barrier((low, [field[m] for m in inner], field[top], rim[0]))
    low, inner_fields, field[top], rim[0] = tied
    for m, value in zip(inner, inner_fields):
        field[m] = value
    low, near_other, near_src_other = lax.optimization_barrier((low, near_other, near_src_other))
    low_other = partner(low, 1)
    for m in inner:
        field[top + m] = partner(field[top], m)
    rim[top] = partner(rim[0], top)
    for m in inner:
        rim[m] = beyond(field[m])

    table, near_here, near_map = pl.pallas_call(
        functools.partial(second_kernel, second_end, empty, halo - near_halo),
        in_specs=[smem] + [vmem] * 5 + [hbm] * 2 + [vmem],
        out_specs=[vmem] * 3,
        out_shape=(
            pltpu.VMEM(table_shape, BF16),
            pltpu.VMEM((targets, near_slots + 1, unknowns, unknowns), BF16),
            pltpu.VMEM(map_shape, I32),
        ),
        scratch_shapes=[pltpu.SemaphoreType.DMA((targets + 1,))],
        compiler_params=pltpu.CompilerParams(vmem_limit_bytes=8 * MIB),
        cost_estimate=operator_cost,
    )(
        listed,
        pinned(rows),
        pinned(weighted),
        pinned(rad_here),
        near_src,
        near_src_other,
        in_hbm(near_blocks),
        near_other,
        pinned(low),
    )

    def apply(places, first_row, total, other, dtype, shape):
        if len(places) > GROUP:
            total = apply(places[:GROUP], first_row, total, None, F32, full)
            return apply(places[GROUP:], first_row, total, other, dtype, shape)
        args = [cls, near_map, listed, pinned(table), pinned(near_here)] + [pinned(part) for _, _, parts in places for part in parts]
        args += [pinned(extra) for extra in (total, other) if extra is not None]
        specs = [smem] * 3 + [vmem] * (len(args) - 3)
        layout = [(outside, mask, len(parts)) for outside, mask, parts in places]
        kernel = functools.partial(
            apply_kernel, layout, first_row, boxes, halo, total is not None, other is not None
        )
        return pl.pallas_call(
            kernel,
            in_specs=specs,
            out_specs=vmem,
            out_shape=pltpu.VMEM(shape, dtype) if len(shape) == 3 else jax.ShapeDtypeStruct(shape, dtype),
            compiler_params=pltpu.CompilerParams(vmem_limit_bytes=12 * MIB),
            cost_estimate=pl.CostEstimate(flops=MIB, bytes_accessed=MIB, transcendentals=0),
        )(*args)

    table, inner_rims = lax.optimization_barrier((table, [rim[m] for m in inner]))
    for m, value in zip(inner, inner_rims):
        rim[m] = value
    last = {m: partner(rim[m], top) for m in inner}

    full = (boxes, unknowns, incidences)
    early = [(False, m, [field[m]]) for m in (0, *inner, top)] + [(True, 0, [rim[0]])]
    middle = [(False, top + m, [field[top + m]]) for m in inner]
    middle += [(True, m, [rim[m]]) for m in (*inner, top)]
    ready = (early + middle)[:GROUP]
    left = (early + middle)[GROUP:]
    count = min(len(early), GROUP)
    table, for_other, total = pl.pallas_call(
        functools.partial(
            third_kernel, second_end, empty, [(outside, mask, 1) for outside, mask, _ in ready], count, boxes, halo
        ),
        in_specs=[smem] * 3 + [vmem] * (6 + len(ready)),
        out_specs=[vmem] * 3,
        out_shape=(
            pltpu.VMEM(table_shape, BF16),
            pltpu.VMEM(full, F32 if left else BF16),
            pltpu.VMEM(full, F32),
        ),
        input_output_aliases={8 + len(ready): 0},
        scratch_shapes=[pltpu.SemaphoreType.DMA],
        compiler_params=pltpu.CompilerParams(vmem_limit_bytes=12 * MIB),
        cost_estimate=pl.CostEstimate(flops=MIB, bytes_accessed=MIB, transcendentals=0),
    )(
        listed,
        cls,
        near_map,
        *[pinned(a) for a in (rows, weighted, rad_here, near_here, low_other, *[parts[0] for _, _, parts in ready], table)],
    )
    if left:
        for_other = apply(left, boxes, for_other, None, BF16, full)
    from_other = partner(for_other, 1)

    total, last = lax.optimization_barrier((total, last))
    turned = {m: partner(last[m], 1) for m in inner}
    total = apply((early + middle)[count:], 0, total, None, F32, full)
    late = [(True, top + m, [last[m]]) for m in inner]
    late += [(True, top + m + 1, [turned[m]]) for m in inner]
    return apply(late, 0, total, from_other, BF16, currents.shape)


def solution(mesh):
    placed = (
        P("region", "dir", None, None),
        P(),
        P(),
        P(),
        P("region", "dir", None, None, None),
        P(),
        P("region", None, None),
        P("region", None, None),
        P("region", "dir", None),
    )
    return jax.shard_map(
        shards,
        mesh=mesh,
        in_specs=placed,
        out_specs=P("region", "dir", None, None),
        check_vma=False,
    )
```

```python
import functools

import jax
import jax.numpy as jnp
from jax import lax
from jax.experimental import pallas as pl
from jax.experimental.pallas import tpu as pltpu
from jax.sharding import PartitionSpec as P

BF16, F32, I32 = jnp.bfloat16, jnp.float32, jnp.int32
NT_DIMS = (((1,), (1,)), ((), ()))
LANES = 128
ROWS = 8
UNROLL = 24
TAIL = 4
GROUP = 8
MIB = 2**20


def pad_to(size, tile):
    return -(-size // tile) * tile


def whole(memory_space):
    return pl.BlockSpec(memory_space=memory_space)


def lookup(parts, hot):
    return lax.dot_general(parts.astype(F32).astype(BF16), hot.astype(BF16), NT_DIMS, preferred_element_type=F32).astype(I32)


def fill_operators(begin, end, list_ref, rows_ref, weighted_ref, rad_ref, out_ref):
    def step(at, wide):
        for u in range(wide):
            place = jnp.minimum(at + u, end - 1)
            row = rows_ref[pl.ds(list_ref[0, place], 1), :].astype(BF16)
            product = weighted_ref[...] * row
            out_ref[place] = jnp.dot(product, rad_ref[...], preferred_element_type=F32).astype(BF16)

    def main_step(i, carry):
        step(begin + i * UNROLL, UNROLL)
        return carry

    def tail_step(i, carry):
        step(begin + main * UNROLL + i * TAIL, TAIL)
        return carry

    count = jnp.maximum(end - begin, 0)
    main = count // UNROLL
    lax.fori_loop(0, main, main_step, 0)
    lax.fori_loop(0, (count - main * UNROLL + TAIL - 1) // TAIL, tail_step, 0)


def first_kernel(
    shared,
    boxes,
    halo,
    region_boxes,
    off_hbm,
    src_hbm,
    tid_hbm,
    table_hbm,
    recv_hbm,
    rad_hbm,
    t_ref,
    weighted_ref,
    rad_ref,
    rows_ref,
    cls_ref,
    listed_ref,
    off_ref,
    src_ref,
    tid_ref,
    table_ref,
    recv_ref,
    list_ref,
    sems,
):
    pairs = [
        (src_hbm, src_ref),
        (tid_hbm, tid_ref),
        (off_hbm, off_ref),
        (recv_hbm, recv_ref),
        (table_hbm, table_ref),
        (rad_hbm, rad_ref),
    ]
    copies = [pltpu.make_async_copy(a, b, sems.at[i]) for i, (a, b) in enumerate(pairs)]
    for copy in copies:
        copy.start()
    classes = table_ref.shape[0]
    directions = recv_ref.shape[1]
    me = lax.axis_index("dir")
    dir_count = region_boxes // boxes
    top = dir_count // 2
    slots = src_ref.shape[2]
    width = cls_ref.shape[1]
    used_width = listed_ref.shape[1]
    ext_at = lax.broadcasted_iota(I32, (width, slots), 0)
    class_at = lax.broadcasted_iota(I32, (used_width, slots), 0)
    row_at = lax.broadcasted_iota(I32, (ROWS, slots), 0)
    out_row = lax.broadcasted_iota(I32, cls_ref.shape, 0)
    seen = jnp.zeros((used_width, slots), F32)
    cls = jnp.full(cls_ref.shape, classes, I32)
    copies[0].wait()
    copies[1].wait()
    for j in range(2 * boxes):
        target = (me if j < boxes else me ^ 1) * boxes + j % boxes
        src = src_ref[0, pl.ds(target, 1), :]
        tid = tid_ref[0, pl.ds(target, 1), :]
        mask = (((src - halo + region_boxes) // boxes) % dir_count) ^ me
        beyond = (src < halo) | (src >= halo + region_boxes)
        late = beyond & ((mask & top) != 0) & ((mask & (top - 2)) != 0)
        even = (mask & 1) == 0
        here = (src >= 0) & ((even | late) if j < boxes else (even & ~late))
        seen = jnp.maximum(seen, jnp.where(class_at == tid, jnp.where(here, 2.0, jnp.where(src >= 0, 1.0, 0.0)), 0.0))
        parts = jnp.where(row_at == 0, tid // 16, jnp.where(row_at == 1, tid % 16, 1))
        found = lookup(parts, jnp.where(ext_at == src, 1.0, 0.0))
        value = jnp.where(found[2:3] > 0, found[0:1] * 16 + found[1:2], classes)
        cls = jnp.where(out_row == j, value, cls)
    cls_ref[...] = cls
    lane = lax.broadcasted_iota(I32, (ROWS, used_width), 1)
    list_row = lax.broadcasted_iota(I32, (ROWS, used_width), 0)
    ones = jnp.ones((ROWS, slots), I32)
    by_chip = jnp.where(lane < shared, jnp.minimum(lookup(ones, jnp.where(seen > 0.0, 1.0, 0.0)), 1), 0)
    by_core = jnp.where(lane >= shared, jnp.minimum(lookup(ones, jnp.where(seen > 1.0, 1.0, 0.0)), 1), 0)
    is_used = jnp.where(list_row == 0, by_chip, by_core)
    down = lax.broadcasted_iota(I32, (used_width, used_width), 0)
    across = lax.broadcasted_iota(I32, (used_width, used_width), 1)
    rank = lookup(is_used, jnp.where(across < down, 1.0, 0.0))
    shared_rank, own_rank = rank[0:1], rank[1:2]
    one_lane = lane[0:1]
    capacity = (shared + 1) // 2
    empty = capacity + classes - shared
    other = (shared_rank ^ me) & 1
    shared_place = shared_rank // 2 + other * (empty + 1)
    place = jnp.where(one_lane < shared, shared_place, capacity + own_rank)
    place = jnp.where(one_lane == classes, empty, place)
    listed_here = jnp.where(one_lane < shared, is_used[0:1] * (1 - other), is_used[1:2])
    here = down == jnp.where(listed_here > 0, place, -1)
    found = lookup(jnp.where(list_row == 0, lane // 16, lane % 16), jnp.where(here, 1.0, 0.0))
    ordered = found[0:1] * 16 + found[1:2]
    count = jnp.sum(is_used.astype(F32), axis=1, keepdims=True).astype(I32)
    first_end = (count[0:1] - (me & 1) + 1) // 2
    ends = jnp.where(one_lane == 0, first_end, capacity + count[1:2])
    listed = jnp.where(list_row == 0, ordered, jnp.where(list_row == 1, place, ends))
    listed_ref[...] = listed
    to_smem = pltpu.make_async_copy(listed_ref, list_ref, sems.at[len(pairs)])
    to_smem.start()
    copies[2].wait()
    position = lax.broadcasted_iota(I32, (1, directions), 1)
    band_size = jnp.ones((1, directions), I32)
    bands = off_ref.shape[0] - 1
    for d in range(bands):
        start, end = off_ref[d], off_ref[d + 1]
        band_size = jnp.where((position >= start) & (position < end), end - start, band_size)
    weight = directions / (bands * band_size.astype(F32))
    copies[3].wait()
    weighted_ref[...] = (recv_ref[...].astype(F32) * weight).astype(BF16)
    copies[4].wait()
    rows_ref[...] = table_ref[...].astype(F32)
    to_smem.wait()
    copies[5].wait()
    fill_operators(0, list_ref[2, 0], list_ref, rows_ref, weighted_ref, rad_ref, t_ref)


def second_kernel(
    second_end,
    empty,
    near_shift,
    list_ref,
    rows_ref,
    weighted_ref,
    rad_ref,
    near_src_ref,
    near_src_other_ref,
    near_hbm,
    near_other_hbm,
    low_ref,
    t_ref,
    near_ref,
    near_map_ref,
    sems,
):
    boxes, near_slots = near_hbm.shape[1:3]
    copies = []
    for i, array in enumerate((near_hbm, near_other_hbm)):
        for j in range(boxes):
            row = i * boxes + j
            copies.append(
                pltpu.make_async_copy(array.at[0, j], near_ref.at[row, pl.ds(0, near_slots)], sems.at[row])
            )
            copies[-1].start()
    first_count = low_ref.shape[0]
    copies.append(pltpu.make_async_copy(low_ref, t_ref.at[pl.ds(0, first_count)], sems.at[2 * boxes]))
    copies[-1].start()
    t_ref[empty] = jnp.zeros(t_ref.shape[1:], BF16)
    for row in range(2 * boxes):
        near_ref[row, near_slots] = jnp.zeros(near_ref.shape[2:], BF16)
    width = near_map_ref.shape[1]
    near_at = lax.broadcasted_iota(I32, (width, near_slots), 0)
    row_at = lax.broadcasted_iota(I32, (ROWS, near_slots), 0)
    lane_at = lax.broadcasted_iota(I32, (ROWS, near_slots), 1)
    out_row = lax.broadcasted_iota(I32, near_map_ref.shape, 0)
    near_map = jnp.full(near_map_ref.shape, near_slots, I32)
    for j in range(2 * boxes):
        near = (near_src_ref if j < boxes else near_src_other_ref)[j % boxes]
        found = lookup(jnp.where(row_at == 0, lane_at, 1), jnp.where((near_at == near + near_shift) & (near >= 0), 1.0, 0.0))
        value = jnp.where(found[1:2] > 0, found[0:1], near_slots)
        near_map = jnp.where(out_row == j, value, near_map)
    near_map_ref[...] = near_map
    end = jnp.minimum(list_ref[2, 1], second_end)
    fill_operators(first_count, end, list_ref, rows_ref, weighted_ref, rad_ref, t_ref)
    for copy in copies:
        copy.wait()


def add_products(places, first_row, boxes, halo, cls_ref, near_map_ref, list_ref, t_ref, near_ref, source_refs, start, store):
    me = lax.axis_index("dir")
    region_boxes = boxes * lax.axis_size("dir")
    bases, groups, at = [], [], 0
    for rim, mask, parts in places:
        groups.append(source_refs[at : at + parts])
        at += parts
        owner = me ^ mask
        base = owner * boxes + halo
        if rim:
            base = base + jnp.where(owner * boxes >= halo, -region_boxes, region_boxes)
        bases.append(base)
    for j in range(boxes):
        row = first_row + j
        total = start(j)
        for base, refs in zip(bases, groups):
            blocks = []
            for b in range(boxes):
                n = list_ref[1, cls_ref[row, base + b]]
                blocks.append(t_ref[n] + near_ref[row, near_map_ref[row, base + b]])
            values = [ref[...].reshape(-1, ref.shape[-1]) for ref in refs]
            rhs = values[0] if len(values) == 1 else jnp.concatenate(values, 0)
            added = jnp.dot(jnp.concatenate(blocks, 1), rhs, preferred_element_type=F32)
            total = added if total is None else total + added
        store(j, total)


def third_kernel(
    second_end,
    empty,
    places,
    early,
    boxes,
    halo,
    list_ref,
    cls_ref,
    near_map_ref,
    rows_ref,
    weighted_ref,
    rad_ref,
    near_ref,
    low_ref,
    *rest,
):
    source_count = sum(parts for _, _, parts in places)
    source_refs, (_, t_ref, other_ref, own_ref, sem) = rest[:source_count], rest[source_count:]
    copy = pltpu.make_async_copy(low_ref, t_ref.at[pl.ds(empty + 1, low_ref.shape[0])], sem)
    copy.start()
    fill_operators(second_end, list_ref[2, 1], list_ref, rows_ref, weighted_ref, rad_ref, t_ref)
    copy.wait()

    def store_other(j, total):
        other_ref[j] = total.astype(other_ref.dtype)

    def store_own(j, total):
        own_ref[j] = total

    refs = (cls_ref, near_map_ref, list_ref, t_ref, near_ref)
    add_products(places, boxes, boxes, halo, *refs, source_refs, lambda j: None, store_other)
    add_products(places[:early], 0, boxes, halo, *refs, source_refs, lambda j: None, store_own)


def apply_kernel(
    places, first_row, boxes, halo, with_total, with_other, cls_ref, near_map_ref, list_ref, t_ref, near_ref, *rest
):
    source_count = sum(parts for _, _, parts in places)
    source_refs, rest = rest[:source_count], rest[source_count:]
    if with_total:
        sum_ref, *rest = rest
    if with_other:
        other_ref, *rest = rest
    (out_ref,) = rest

    def start(j):
        total = sum_ref[j] if with_total else None
        if with_other:
            other = other_ref[j].astype(F32)
            total = other if total is None else total + other
        return total

    def store(j, total):
        if len(out_ref.shape) == 4:
            out_ref[0, j] = total.astype(out_ref.dtype)
        else:
            out_ref[j] = total.astype(out_ref.dtype)

    refs = (cls_ref, near_map_ref, list_ref, t_ref, near_ref)
    add_products(places, first_row, boxes, halo, *refs, source_refs, start, store)


def shards(
    currents,
    radiate,
    receive,
    transfer_table,
    near_blocks,
    dir_offsets,
    trans_src,
    trans_tid,
    near_src,
):
    dir_count = lax.axis_size("dir")
    region_count = lax.axis_size("region")
    own = currents[0]
    boxes, unknowns, incidences = own.shape
    near_slots = near_src.shape[2]
    near_src = near_src.reshape(boxes, 1, near_slots)
    region_boxes = boxes * dir_count
    halo = region_boxes // 2
    near_halo = region_boxes // 4
    classes, directions = transfer_table.shape
    shared = classes // 2
    capacity = (shared + 1) // 2
    empty = capacity + classes - shared
    second_end = capacity + pad_to(classes // 8, UNROLL)
    top = dir_count // 2
    inner = range(2, top, 2)
    targets = 2 * boxes

    def partner(array, mask):
        return lax.ppermute(array, "dir", [(i, i ^ mask) for i in range(dir_count)])

    along = []
    for i in range(dir_count):
        for z in range(region_count):
            target = z + 1 if i >= top else z - 1
            if 0 <= target < region_count:
                along.append((i * region_count + z, i * region_count + target))

    def beyond(array):
        return lax.ppermute(array, ("dir", "region"), along)

    def pinned(array):
        return pltpu.with_memory_space_constraint(array, pltpu.VMEM)

    def in_hbm(array):
        return pltpu.with_memory_space_constraint(array, pltpu.HBM)

    width = pad_to(region_boxes + 2 * halo, LANES)
    map_shape = (pad_to(targets, ROWS), width)
    table_shape = (empty + 1 + capacity, unknowns, unknowns)
    low_shape = (capacity, unknowns, unknowns)
    list_shape = (ROWS, pad_to(classes + 1, LANES))
    vmem, smem, hbm = whole(pltpu.VMEM), whole(pltpu.SMEM), whole(pltpu.HBM)
    operator_cost = pl.CostEstimate(
        flops=classes * unknowns * unknowns * directions, bytes_accessed=MIB, transcendentals=0
    )

    field = {0: own}
    rim = {}
    for m in inner:
        field[m] = partner(own, m)
    field[top] = partner(own, top)
    rim[0] = beyond(own)
    near_other = partner(near_blocks, 1)
    near_src_other = partner(near_src, 1)
    low, weighted, rad_here, rows, cls, listed = pl.pallas_call(
        functools.partial(first_kernel, shared, boxes, halo, region_boxes),
        in_specs=[hbm] * 6,
        out_specs=[vmem] * 6,
        out_shape=(
            pltpu.VMEM(low_shape, BF16),
            pltpu.VMEM((unknowns, directions), BF16),
            pltpu.VMEM((directions, unknowns), BF16),
            pltpu.VMEM((classes, directions), F32),
            pltpu.VMEM(map_shape, I32),
            pltpu.VMEM(list_shape, I32),
        ),
        scratch_shapes=[
            pltpu.SMEM(dir_offsets.shape, I32),
            pltpu.VMEM(trans_src.shape, I32),
            pltpu.VMEM(trans_tid.shape, I32),
            pltpu.VMEM(transfer_table.shape, BF16),
            pltpu.VMEM(receive.shape, BF16),
            pltpu.SMEM(list_shape, I32),
            pltpu.SemaphoreType.DMA((7,)),
        ],
        compiler_params=pltpu.CompilerParams(vmem_limit_bytes=8 * MIB),
        cost_estimate=operator_cost,
    )(*[in_hbm(a) for a in (dir_offsets, trans_src, trans_tid, transfer_table, receive, radiate)])

    tied = lax.optimization_barrier((low, [field[m] for m in inner], field[top], rim[0]))
    low, inner_fields, field[top], rim[0] = tied
    for m, value in zip(inner, inner_fields):
        field[m] = value
    low, near_other, near_src_other = lax.optimization_barrier((low, near_other, near_src_other))
    low_other = partner(low, 1)
    for m in inner:
        field[top + m] = partner(field[top], m)
    rim[top] = partner(rim[0], top)
    for m in inner:
        rim[m] = beyond(field[m])

    table, near_here, near_map = pl.pallas_call(
        functools.partial(second_kernel, second_end, empty, halo - near_halo),
        in_specs=[smem] + [vmem] * 5 + [hbm] * 2 + [vmem],
        out_specs=[vmem] * 3,
        out_shape=(
            pltpu.VMEM(table_shape, BF16),
            pltpu.VMEM((targets, near_slots + 1, unknowns, unknowns), BF16),
            pltpu.VMEM(map_shape, I32),
        ),
        scratch_shapes=[pltpu.SemaphoreType.DMA((targets + 1,))],
        compiler_params=pltpu.CompilerParams(vmem_limit_bytes=8 * MIB),
        cost_estimate=operator_cost,
    )(
        listed,
        pinned(rows),
        pinned(weighted),
        pinned(rad_here),
        near_src,
        near_src_other,
        in_hbm(near_blocks),
        near_other,
        pinned(low),
    )

    def apply(places, first_row, total, other, dtype, shape):
        if len(places) > GROUP:
            total = apply(places[:GROUP], first_row, total, None, F32, full)
            return apply(places[GROUP:], first_row, total, other, dtype, shape)
        args = [cls, near_map, listed, pinned(table), pinned(near_here)] + [pinned(part) for _, _, parts in places for part in parts]
        args += [pinned(extra) for extra in (total, other) if extra is not None]
        specs = [smem] * 3 + [vmem] * (len(args) - 3)
        layout = [(outside, mask, len(parts)) for outside, mask, parts in places]
        kernel = functools.partial(
            apply_kernel, layout, first_row, boxes, halo, total is not None, other is not None
        )
        return pl.pallas_call(
            kernel,
            in_specs=specs,
            out_specs=vmem,
            out_shape=pltpu.VMEM(shape, dtype) if len(shape) == 3 else jax.ShapeDtypeStruct(shape, dtype),
            compiler_params=pltpu.CompilerParams(vmem_limit_bytes=12 * MIB),
            cost_estimate=pl.CostEstimate(flops=MIB, bytes_accessed=MIB, transcendentals=0),
        )(*args)

    table, inner_rims = lax.optimization_barrier((table, [rim[m] for m in inner]))
    for m, value in zip(inner, inner_rims):
        rim[m] = value
    last = {m: partner(rim[m], top) for m in inner}

    full = (boxes, unknowns, incidences)
    early = [(False, m, [field[m]]) for m in (0, *inner, top)] + [(True, 0, [rim[0]])]
    middle = [(False, top + m, [field[top + m]]) for m in inner]
    middle += [(True, m, [rim[m]]) for m in (*inner, top)]
    ready = (early + middle)[:GROUP]
    left = (early + middle)[GROUP:]
    count = min(len(early), GROUP)
    table, for_other, total = pl.pallas_call(
        functools.partial(
            third_kernel, second_end, empty, [(outside, mask, 1) for outside, mask, _ in ready], count, boxes, halo
        ),
        in_specs=[smem] * 3 + [vmem] * (6 + len(ready)),
        out_specs=[vmem] * 3,
        out_shape=(
            pltpu.VMEM(table_shape, BF16),
            pltpu.VMEM(full, F32 if left else BF16),
            pltpu.VMEM(full, F32),
        ),
        input_output_aliases={8 + len(ready): 0},
        scratch_shapes=[pltpu.SemaphoreType.DMA],
        compiler_params=pltpu.CompilerParams(vmem_limit_bytes=12 * MIB),
        cost_estimate=pl.CostEstimate(flops=MIB, bytes_accessed=MIB, transcendentals=0),
    )(
        listed,
        cls,
        near_map,
        *[pinned(a) for a in (rows, weighted, rad_here, near_here, low_other, *[parts[0] for _, _, parts in ready], table)],
    )
    if left:
        for_other = apply(left, boxes, for_other, None, BF16, full)
    from_other = partner(for_other, 1)

    total, last = lax.optimization_barrier((total, last))
    turned = {m: partner(last[m], 1) for m in inner}
    total = apply((early + middle)[count:], 0, total, None, F32, full)
    late = [(True, top + m, [last[m]]) for m in inner]
    late += [(True, top + m + 1, [turned[m]]) for m in inner]
    return apply(late, 0, total, from_other, BF16, currents.shape)


def solution(mesh):
    placed = (
        P("region", "dir", None, None),
        P(),
        P(),
        P(),
        P("region", "dir", None, None, None),
        P(),
        P("region", None, None),
        P("region", None, None),
        P("region", "dir", None),
    )
    return jax.shard_map(
        shards,
        mesh=mesh,
        in_specs=placed,
        out_specs=P("region", "dir", None, None),
        check_vma=False,
    )
```
